128 devices in a mesh: blk: 8 (over x, core), lon: 16 (over z, y).
Axes of the slice: x: 4, y: 4, z: 4, core: 2. Of those that a mesh axis runs over, the one named last changes fastest.
Arguments:
- temp_salt: float32 [2, 8, 256, 8192], P(None, None, 'blk', 'lon'), may hold values from -6 to 6
- east_vel: float32 [8, 256, 8192], P(None, 'blk', 'lon'), may hold values from -0.15 to 0.15
- north_vel: float32 [8, 256, 8192], P(None, 'blk', 'lon'), may hold values from -0.15 to 0.15
- land_mask: int32 [256, 8192], P('blk', 'lon'), may hold values 0 or 1
- fluxes: float32 [10, 128, 4096], P(None, ('blk', 'lon')), may hold values from -6 to 6
- remap_code: int32 [4, 256, 8192], P(None, 'blk', 'lon'), may hold values from 0 to 8
- remap_weight: float32 [4, 256, 8192], P(None, 'blk', 'lon'), may hold values from 0.1 to 1
- fold_source: int32 [8192], P('lon'), may hold values from 0 to 8191, as said below
Outputs:
- ocean_state: float32 [2, 8, 256, 8192], P(None, None, 'blk', 'lon')
- skin_heat_atmospheric_grid: float32 [128, 4096], P(('blk', 'lon'))
The draws below stay inside these ranges and needn't reach their ends.
Inputs may be any that keep to these rules, and one draw needn't show every extreme that they name: fold_source is a reflection of the columns about a pole column p drawn per case: entry x is (2 p - 1 - x) mod 8192.
All inputs are finite; a program needn't handle non-finite values. No bound on the sum of `land_mask` on one device may be relied on, other than what follows from the above.
Results may differ from the reference program's by a relative error of at most 0.00012.
Values sent between devices are 32-bit elements; how exact they have to be, the bound alone decides.
No kernel may reach another device: no remote copies, remote signals or barrier semaphores. Data moves between devices by JAX's collectives and lax.ppermute only.
A program may use at most 192 MiB of HBM per device.

```python
import jax
import jax.numpy as jnp
from jax import lax

KL = 8
STEPS = 6
FIELDS = 10
NY = 256
NX = 8192
AY = 128
AX = 4096


def draw_fold_source(key, part):
    key = jax.random.fold_in(key, 7)
    pole = jax.random.randint(key, (), 0, NX, dtype=jnp.int32)
    columns = jnp.arange(NX, dtype=jnp.int32)
    return jnp.mod(2 * pole - 1 - columns, NX).astype(jnp.int32)


def place_ends(values, stream_key, least, top_value):
    dims = values.shape
    index_at = [jax.random.randint(jax.random.fold_in(stream_key, axis), (), 0, dims[axis]) for axis in range(len(dims))]
    values = values.at[tuple(index_at)].set(least)
    longest = dims.index(max(dims))
    index_at[longest] = (index_at[longest] + 1) % dims[longest]
    return values.at[tuple(index_at)].set(top_value)


def shard_levels(stream_key, dims, cuts, smallest, high):
    def one(position, blocks):
        draws = jax.random.uniform(jax.random.fold_in(jax.random.fold_in(stream_key, 6), position), (blocks,), jnp.float32, smallest / len(cuts), high / len(cuts))
        return jnp.repeat(jnp.exp(draws), dims[position] // blocks).reshape((-1,) + (1,) * (len(dims) - position - 1))

    loudness = one(*cuts[0])
    for cut in cuts[1:]:
        loudness = loudness * one(*cut)
    return loudness


def normal_values(stream_key, extent, scale, limit, shards=(), held_as=jnp.bfloat16):
    entries = jax.random.normal(stream_key, extent, jnp.float32) * scale
    if len(shards) > 0:
        entries = shard_levels(stream_key, extent, shards, -0.22, 0.18) * entries
    return jnp.clip(entries, min=-limit, max=limit).astype(held_as)


def setup_inputs(seed: int = 0) -> dict:
    splits = jax.random.split(jax.random.key(seed), 9)
    return {
        "temp_salt": normal_values(splits[0], (2, KL, NY, NX), 1.0, 6.0, ((2, 8), (3, 16)), jnp.float32),
        "east_vel": jnp.clip(jax.random.uniform(splits[1], (KL, NY, NX), jnp.float32, -0.15, 0.15) * shard_levels(splits[1], (KL, NY, NX), ((1, 8), (2, 16)), -0.4, 0.0), -0.15, 0.15),
        "north_vel": jnp.clip(jax.random.uniform(splits[2], (KL, NY, NX), jnp.float32, -0.15, 0.15) * shard_levels(splits[2], (KL, NY, NX), ((1, 8), (2, 16)), -0.4, 0.0), -0.15, 0.15),
        "land_mask": place_ends((jax.random.randint(splits[3], (NY, NX), 0, 4) < 3).astype(jnp.int32), jax.random.fold_in(splits[3], 1), 0, 1),
        "fluxes": normal_values(splits[4], (FIELDS, AY, AX), 1.0, 6.0, ((1, 128),), jnp.float32),
        "remap_code": place_ends(jax.random.randint(splits[5], (4, NY, NX), 0, 9), jax.random.fold_in(splits[5], 1), 0, 8).astype(jnp.int32),
        "remap_weight": jnp.clip(0.1 + 0.9 * jax.random.uniform(splits[6], (4, NY, NX), jnp.float32) ** shard_levels(splits[6], (4, NY, NX), ((1, 8), (2, 16)), -0.2, 0.2), 0.1, 1.0),
        "fold_source": draw_fold_source(jax.random.fold_in(splits[8], 71), 0),
    }


def remap_padded(atm_pad, code, weight):
    fields = atm_pad.shape[0]
    rows = atm_pad.shape[1] - 2
    cols = atm_pad.shape[2] - 2
    wsum = lax.optimization_barrier(jnp.sum(weight, axis=0))
    total = jnp.zeros((fields, rows, 2, cols, 2), jnp.float32)
    for dy in (-1, 0, 1):
        for dx in (-1, 0, 1):
            label = (dy + 1) * 3 + (dx + 1)
            coef = lax.optimization_barrier(jnp.sum(jnp.where(code == label, weight, 0.0), axis=0)) / wsum
            coef = coef.reshape(rows, 2, cols, 2)
            shifted = atm_pad[:, 1 + dy:1 + dy + rows, 1 + dx:1 + dx + cols]
            total = total + shifted[:, :, None, :, None] * coef[None]
    return total.reshape(fields, 2 * rows, 2 * cols)

def combine(f):
    heat = f[1] + f[2] + f[3] - 0.33 * f[5]
    fresh = f[4] + f[5] + f[6] + f[7]
    return jnp.stack([f[0], heat, fresh, f[8], f[9]])

def build_surface_forcing(fields, mask, depth_indices):
    level = jnp.arange(depth_indices, dtype=jnp.int32)
    depth = jnp.exp2(-(level + 1).astype(jnp.float32))[:, None, None]
    surface = (level == 0).astype(jnp.float32)[:, None, None]
    heat_term = 0.05 * mask * (depth * fields[0] + surface * fields[1])
    salt_term = -0.05 * mask * surface * fields[2]
    kv_top = 0.05 + 0.04 * jnp.sqrt(fields[3] * fields[3] + fields[4] * fields[4] + 0.01)
    return (jnp.stack([heat_term, salt_term]), kv_top)

def advance(qp, east_pad, north_pad, mask_pad, forcing, kv_top):
    qc = qp[..., 1:-1, 1:-1]
    q_east = qp[..., 1:-1, 2:]
    q_west = qp[..., 1:-1, :-2]
    q_north = qp[..., 2:, 1:-1]
    q_south = qp[..., :-2, 1:-1]
    mc = mask_pad[1:-1, 1:-1]
    open_e = mc * mask_pad[1:-1, 2:]
    open_w = mask_pad[1:-1, :-2] * mc
    open_n = mc * mask_pad[2:, 1:-1]
    open_s = mask_pad[:-2, 1:-1] * mc
    vel_e = east_pad[:, 1:-1, 1:-1]
    vel_w = east_pad[:, 1:-1, :-2]
    vel_n = north_pad[:, 1:-1, 1:-1]
    vel_s = north_pad[:, :-2, 1:-1]
    flux_e = open_e * (jnp.maximum(vel_e, 0.0) * qc + jnp.minimum(vel_e, 0.0) * q_east)
    flux_w = open_w * (jnp.maximum(vel_w, 0.0) * q_west + jnp.minimum(vel_w, 0.0) * qc)
    flux_n = open_n * (jnp.maximum(vel_n, 0.0) * qc + jnp.minimum(vel_n, 0.0) * q_north)
    flux_s = open_s * (jnp.maximum(vel_s, 0.0) * q_south + jnp.minimum(vel_s, 0.0) * qc)
    spread = 0.08 * (open_e * (q_east - qc) - open_w * (qc - q_west) + open_n * (q_north - qc) - open_s * (qc - q_south))
    horizontal = -(flux_e - flux_w + flux_n - flux_s) + spread
    depth_indices = qc.shape[1]
    inner = jnp.full((depth_indices - 2,) + kv_top.shape, 0.05, jnp.float32)
    mixing = jnp.concatenate([kv_top[None], inner], axis=0)
    downward = mixing * (qc[:, 1:] - qc[:, :-1])
    surface_layer = jnp.zeros_like(downward[:, :1])
    vertical = jnp.concatenate([downward, surface_layer], axis=1) - jnp.concatenate([surface_layer, downward], axis=1)
    return qc + mc * (horizontal + vertical) + forcing

def pad_global(field, fold_source):
    north = jnp.take(field[..., -1, :], fold_source, axis=-1)
    rows = jnp.concatenate([jnp.zeros_like(field[..., :1, :]), field, north[..., None, :]], axis=-2)
    zero_col = jnp.zeros_like(rows[..., :1])
    inner = jnp.concatenate([rows[..., -1:], rows, rows[..., :1]], axis=-1)
    top = jnp.concatenate([zero_col[..., -1, :], north, zero_col[..., -1, :]], axis=-1)
    bottom = jnp.zeros_like(top)
    return jnp.concatenate([bottom[..., None, :], inner[..., 1:-1, :], top[..., None, :]], axis=-2)

def reference(temp_salt, east_vel, north_vel, land_mask, fluxes, remap_code, remap_weight, fold_source):
    mask = land_mask.astype(jnp.float32)
    atm_pad = jnp.pad(fluxes, ((0, 0), (1, 1), (0, 0)))
    atm_pad = jnp.concatenate([atm_pad[..., -1:], atm_pad, atm_pad[..., :1]], axis=-1)
    fields = combine(remap_padded(atm_pad, remap_code, remap_weight))
    forcing, kv_top = build_surface_forcing(fields, mask, KL)
    east_pad = pad_global(east_vel, fold_source)
    north_pad = pad_global(north_vel, fold_source)
    mask_pad = pad_global(mask, fold_source)
    ocean_prognostics = temp_salt
    for step in range(STEPS):
        ocean_prognostics = advance(pad_global(ocean_prognostics, fold_source), east_pad, north_pad, mask_pad, forcing, kv_top)
    weights = mask.reshape(AY, 2, AX, 2)
    cumulative_accumulator = lax.optimization_barrier(jnp.sum((ocean_prognostics[0, 0] * mask).reshape(AY, 2, AX, 2), axis=(1, 3)))
    contribution_number = lax.optimization_barrier(jnp.sum(weights, axis=(1, 3)))
    skin_heat_atmospheric_grid = cumulative_accumulator / jnp.maximum(contribution_number, 1.0)
    return (ocean_prognostics, skin_heat_atmospheric_grid)
```

```python
import jax
import jax.numpy as jnp
from jax import lax
from jax.experimental import pallas as pl
from jax.experimental.pallas import tpu as pltpu
from jax.sharding import PartitionSpec as P

STEPS = 6
F32 = jnp.float32
LEVELS = 8
BLK, LON = 8, 16
ROWS, COLS = 32, 512
EXT_ROWS, EXT_COLS = 48, 640
NX = 8192
SLABS = 41
PART = 232
MSG = 4 * PART + 32
VMEM = pltpu.VMEM
SMEM = pltpu.SMEM
LIMIT = pltpu.CompilerParams(vmem_limit_bytes=56 * 1024 * 1024)


def iota(shape, dim):
    return lax.broadcasted_iota(jnp.int32, shape, dim)


def full(shape):
    return pl.BlockSpec(shape, lambda i: (0,) * len(shape))


def at_block(shape, place):
    return pl.BlockSpec(shape, lambda i: place)


SCALARS = pl.BlockSpec(memory_space=SMEM)


def pack_columns(flux, st0, st3, vn0, vn3, ve0, ve3, cd0, cd3, wt0, wt3, mk0, mk3, to_west, to_east, band):
    band[0] = flux[0]
    band[1] = flux[1] + flux[2] + flux[3] - 0.33 * flux[5]
    band[2] = flux[4] + flux[5] + flux[6] + flux[7]
    band[3] = flux[8]
    band[4] = flux[9]
    lane = iota((ROWS, 128), 1)

    def pack(groups, shift, out):
        for g, tiles in enumerate(groups):
            acc = jnp.zeros((ROWS, 128), F32)
            for j, tile in enumerate(tiles):
                moved = pltpu.roll(tile().astype(F32), (8 * j + shift) % 128, axis=1)
                acc = jnp.where((lane >= 8 * j) & (lane < 8 * j + 8), moved, acc)
            out[g] = acc

    def groups(st, vn, ve, cd, wt, mk):
        first = [lambda t=t, k=k: st[t, k] for t in range(2) for k in range(LEVELS)]
        second = [lambda k=k: vn[k] for k in range(LEVELS)] + [lambda k=k: ve[k] for k in range(LEVELS)]
        third = [lambda k=k: cd[k] for k in range(4)] + [lambda k=k: wt[k] for k in range(4)] + [lambda: mk[...]]
        return [first, second, third]

    pack(groups(st0, vn0, ve0, cd0, wt0, mk0), 0, to_west)
    pack(groups(st3, vn3, ve3, cd3, wt3, mk3), 6, to_east)


def chunk_bands(sc, band, other, out, own, held, turned):
    is_fold = sc[0] == BLK - 1
    own[...] = band[...].reshape(160, 128)
    held[...] = other[...].reshape(160, 128)

    @pl.when(is_fold & (sc[1] < 4))
    def _():
        pole = sc[4]
        pq, pr = pole // 128, pole % 128
        lane8 = iota((8, 128), 1)
        index = (pr - lane8) & 127
        for n in range(20):
            turned[8 * n : 8 * n + 8, :] = jnp.take_along_axis(held[8 * n : 8 * n + 8, :], index, axis=1)
        lane1 = iota((1, 128), 1)

        def one(row, carry):
            near = (pq - row) & 31
            far = (pq - row - 1) & 31
            for f in range(5):
                a = turned[pl.ds(32 * f + near, 1), :]
                b = turned[pl.ds(32 * f + far, 1), :]
                held[pl.ds(32 * f + row, 1), :] = jnp.where(lane1 <= pr, a, b)
            return carry

        lax.fori_loop(0, 32, one, 0)

    lane = iota((16, 128), 1)
    for slot, src in enumerate((own, held)):
        for f in range(5):
            even = src[pl.ds(32 * f, 16, stride=2), :]
            odd = src[pl.ds(32 * f + 1, 16, stride=2), :]
            side = jnp.where(lane < 64, pltpu.roll(even, 15, axis=0), pltpu.roll(odd, 1, axis=0))
            for part, value in enumerate((even, odd, side)):
                out[pl.ds(16 * slot + 3 * f + part, 16, stride=32), :] = value
        out[pl.ds(16 * slot + 15, 16, stride=32), :] = jnp.zeros((16, 128), F32)


def pack_rows(
    sc, from_west, from_east, st_s, st_n, vn_s, vn_n, ve_s, ve_n, cd_s, cd_n, wt_s, wt_n, mk_s, mk_n,
    sides, msg_a, msg_b, south, north,
):
    lane = iota((ROWS, 128), 1)
    for s in range(SLABS):
        g, j = s // 16, s % 16
        east = pltpu.roll(from_east[g], (128 - 8 * j) % 128, axis=1)
        west = pltpu.roll(from_west[g], (122 - 8 * j) % 128, axis=1)
        tile = jnp.where(lane < 6, east, jnp.where(lane >= 122, west, 0.0))
        sides[ROWS * s : ROWS * s + ROWS, :] = tile
        if s < SLABS - 1:
            south[(4 * SLABS + s) * 8 : (4 * SLABS + s) * 8 + 8, :] = tile[0:8]
            north[(4 * SLABS + s) * 8 : (4 * SLABS + s) * 8 + 8, :] = tile[24:32]
        else:
            south[(4 * SLABS + s) * 8 : (4 * SLABS + s) * 8 + 8, :] = tile[0:8]
            for i in range(8):
                north[(4 * SLABS + s) * 8 + i : (4 * SLABS + s) * 8 + i + 1, :] = tile[31 - i : 32 - i]

    def stage(dst, st, vn, ve, cd, wt):
        for j in range(4):
            cols = slice(128 * j, 128 * j + 128)

            def put(s, value):
                dst[(j * SLABS + s) * 8 : (j * SLABS + s) * 8 + 8, :] = value

            for k in range(LEVELS):
                put(k, st[0, k, :, cols])
                put(8 + k, st[1, k, :, cols])
                put(16 + k, vn[k, :, cols])
                put(24 + k, ve[k, :, cols])
            for k in range(4):
                put(32 + k, cd[k, :, cols].astype(F32))
                put(36 + k, wt[k, :, cols])

    stage(south, st_s, vn_s, ve_s, cd_s, wt_s)
    stage(north, st_n, vn_n, ve_n, cd_n, wt_n)
    for j in range(4):
        base = (j * SLABS + 40) * 8
        cols = slice(128 * j, 128 * j + 128)
        south[base : base + 8, :] = mk_s[:, cols].astype(F32)
        flipped = mk_n[:, cols].astype(F32)
        for i in range(8):
            north[base + i : base + i + 1, :] = flipped[7 - i : 8 - i]

    lane8 = iota((8, 128), 1)

    def build(msg, edge, is_north, turn):
        corner = [jnp.zeros((8, 128), F32) for _ in range(4)]
        if turn:
            rq, rr = sc[3] // 128, sc[3] % 128
            index = (rr - lane8) & 127
            near = lane8 <= rr
            order = [rq, (rq - 1) & 3, (rq - 2) & 3, (rq - 3) & 3]
            below = jnp.where(rq == 0, 4, rq - 1)
            above = jnp.where(rq == 3, 4, rq + 1)
        for n in range(29):
            i, rt = (n // 5, n % 5) if n < 28 else (0, 5)
            if n < 28:
                row = 7 - i if is_north else i

                def load(j):
                    return edge[pl.ds((j * SLABS + rt * 8) * 8 + row, 8, stride=8), :]
            else:

                def load(j):
                    return edge[pl.ds(pl.multiple_of((j * SLABS + 40) * 8, 8), 8), :]

            if turn:
                def pick(j):
                    return jnp.take_along_axis(load(j), index, axis=1)

                g = [pick(j) for j in order]
                tiles = [jnp.where(near, g[j], g[(j + 1) % 4]) for j in range(4)]
                fifth = jnp.where(
                    lane8 < 64, jnp.where(near, g[0], pick(below)), jnp.where(near, pick(above), g[0])
                )
            else:
                tiles = [load(j) for j in range(4)]
                fifth = load(4)
            for j in range(4):
                msg[j * PART + 8 * n : j * PART + 8 * n + 8, :] = tiles[j]
            slot = n % 8
            moved = pltpu.roll(fifth, (6 + 16 * slot) % 128, axis=1)
            corner[n // 8] = jnp.where((lane8 >= 16 * slot) & (lane8 < 16 * slot + 12), moved, corner[n // 8])
        for v in range(4):
            msg[4 * PART + 8 * v : 4 * PART + 8 * v + 8, :] = corner[v]

    parity = sc[0] & 1

    @pl.when(parity == 0)
    def _():
        build(msg_a, north, True, False)
        build(msg_b, south, False, False)

    @pl.when(parity == 1)
    def _():
        build(msg_a, south, False, False)

    @pl.when((parity == 1) & (sc[0] < BLK - 1))
    def _():
        build(msg_b, north, True, False)

    @pl.when(sc[0] == BLK - 1)
    def _():
        build(msg_b, north, True, True)


def interval(
    sc, st, vn, ve, cd, wt, mk, sides, got_a, got_b, fold_1, fold_2, atm, out, sst,
    ghost_s, ghost_n, qa, qb, vx, ux, cx, wx, mx, atm_rows, doubled, coef,
    ce, cw, cn, cs, cc, force, pairs,
):
    lane8 = iota((8, 128), 1)
    edge_lanes = (lane8 < 6) | (lane8 >= 122)
    is_fold = sc[0] == BLK - 1
    parity = sc[0] & 1
    ghost_s[...] = jnp.zeros_like(ghost_s)
    ghost_n[...] = jnp.zeros_like(ghost_n)

    def unpack(load, corner, ghost, is_north):
        for n in range(29):
            i, rt = (n // 5, n % 5) if n < 28 else (0, 5)
            tiles = [load(j, n) for j in range(4)]
            slot = n % 8
            fifth = pltpu.roll(corner(n // 8, slot), (256 - 6 - 16 * slot) % 128, axis=1)
            tiles.append(jnp.where(edge_lanes, fifth, 0.0))
            for j in range(5):
                if n < 28:
                    row = i if is_north else 7 - i
                    ghost[pl.ds((j * SLABS + rt * 8) * 8 + row, 8, stride=8), :] = tiles[j]
                else:
                    base = (j * SLABS + 40) * 8
                    if is_north:
                        ghost[base : base + 8, :] = tiles[j]
                    else:
                        for r in range(8):
                            ghost[base + r : base + r + 1, :] = tiles[j][7 - r : 8 - r]

    def plain(msg, ghost, is_north):
        unpack(
            lambda j, n: msg[j * PART + 8 * n : j * PART + 8 * n + 8, :],
            lambda v, slot: msg[4 * PART + 8 * v : 4 * PART + 8 * v + 8, :],
            ghost,
            is_north,
        )

    @pl.when(parity == 0)
    def _():
        plain(got_a, ghost_n, True)
        plain(got_b, ghost_s, False)

    @pl.when(parity == 1)
    def _():
        plain(got_a, ghost_s, False)

    @pl.when((parity == 1) & (sc[0] < BLK - 1))
    def _():
        plain(got_b, ghost_n, True)

    @pl.when(is_fold)
    def _():
        seam = sc[3]

        def load(j, n):
            at = slice(j * PART + 8 * n, j * PART + 8 * n + 8)
            return jnp.where(lane8 + 128 * j <= seam, fold_1[at, :], fold_2[at, :])

        def corner(v, slot):
            at = slice(4 * PART + 8 * v, 4 * PART + 8 * v + 8)
            return jnp.where((lane8 & 15) < 6, fold_1[at, :], fold_2[at, :])

        unpack(load, corner, ghost_n, True)

    def extend(ext, at, s, own, north_fix=None):
        base = EXT_ROWS * at
        ext[base + 8 : base + 40, 0:COLS] = own
        ext[base + 8 : base + 40, COLS:EXT_COLS] = sides[ROWS * s : ROWS * s + ROWS, :]
        for j in range(5):
            cols = slice(128 * j, 128 * j + 128)
            g = (j * SLABS + s) * 8
            ext[base : base + 8, cols] = ghost_s[g : g + 8, :]
            top = ghost_n[g : g + 8, :]
            ext[base + 40 : base + 48, cols] = top if north_fix is None else north_fix(top)

    flip = jnp.where(is_fold, -1.0, 1.0).astype(F32)
    for t in range(2):
        for k in range(LEVELS):
            extend(qa, 8 * t + k, 8 * t + k, st[t, k])
    for k in range(LEVELS):
        extend(vx, k, 16 + k, vn[k], lambda g: g * flip)
        extend(ux, k, 24 + k, ve[k], lambda g: g * flip)
    for k in range(4):
        extend(cx, k, 32 + k, cd[k].astype(F32), lambda g: jnp.where(is_fold, 8.0 - g, g))
        extend(wx, k, 36 + k, wt[k])
    extend(mx, 0, 40, mk[...].astype(F32))

    row8 = iota((8, 128), 0)
    for f in range(5):
        for part in range(3):
            cols = slice(128 * part, 128 * part + 128)
            atm_rows[24 * f : 24 * f + 16, cols] = atm[pl.ds(3 * f + part, 16, stride=32), :]
            far = atm[pl.ds(16 + 3 * f + part, 16, stride=32), :]
            atm_rows[24 * f + 16 : 24 * f + 24, cols] = jnp.where(row8 < 4, far[0:8], far[8:16])
    src = iota((384, EXT_COLS), 0)
    dst = iota((384, EXT_COLS), 1)
    table = (src == jnp.where(dst < 576, dst // 2, dst // 2 + 64)).astype(F32)
    wide = jnp.dot(atm_rows[...], table, precision=lax.Precision.HIGHEST, preferred_element_type=F32)
    for f in range(5):
        for j in range(5):
            tile = wide[24 * f : 24 * f + 24, 128 * j : 128 * j + 128]
            base = (5 * f + j) * 48
            doubled[pl.ds(base, 24, stride=2), :] = tile
            doubled[pl.ds(base + 1, 24, stride=2), :] = tile

    shape = (EXT_ROWS, EXT_COLS)
    row = iota(shape, 0)
    wsum = wx[0:48, :] + wx[48:96, :] + wx[96:144, :] + wx[144:192, :]
    inv = 1.0 / jnp.where(wsum > 0.0, wsum, 1.0)
    up_ok = jnp.where(is_fold & (row >= 38) & (row < 40), 0.0, 1.0)
    down_ok = jnp.where(is_fold & (row >= 40) & (row < 42), 0.0, 1.0)
    for c in range(9):
        total = jnp.zeros(shape, F32)
        for t in range(4):
            total = total + jnp.where(cx[48 * t : 48 * t + 48, :] == float(c), wx[48 * t : 48 * t + 48, :], 0.0)
        total = total * inv
        if c < 3:
            total = total * down_ok
        if c >= 6:
            total = total * up_ok
        coef[48 * c : 48 * c + 48, :] = total
    fields = []
    for f in range(5):
        tiles = [doubled[(5 * f + j) * 48 : (5 * f + j) * 48 + 48, :] for j in range(5)]
        grid = jnp.concatenate(tiles, axis=1)
        grid = jnp.concatenate([grid[40:48], grid[0:40]], axis=0)
        total = jnp.zeros(shape, F32)
        for dy in (-1, 0, 1):
            by_row = grid if dy == 0 else pltpu.roll(grid, (EXT_ROWS - 2 * dy) % EXT_ROWS, axis=0)
            for dx in (-1, 0, 1):
                c = 3 * (dy + 1) + dx + 1
                moved = by_row if dx == 0 else pltpu.roll(by_row, (EXT_COLS - 2 * dx) % EXT_COLS, axis=1)
                total = total + moved * coef[48 * c : 48 * c + 48, :]
        fields.append(total)
    m = mx[...]
    force[0:48, :] = 0.05 * m * fields[0]
    force[48:96, :] = 0.05 * m * fields[1]
    force[96:144, :] = -0.05 * m * fields[2]
    kv = 0.05 + 0.04 * jnp.sqrt(fields[3] * fields[3] + fields[4] * fields[4] + 0.01)
    force[144:192, :] = m * kv
    force[192:240, :] = 0.05 * m

    def east_of(x):
        return pltpu.roll(x, EXT_COLS - 1, axis=1)

    def west_of(x):
        return pltpu.roll(x, 1, axis=1)

    def north_of(x):
        return pltpu.roll(x, EXT_ROWS - 1, axis=0)

    def south_of(x):
        return pltpu.roll(x, 1, axis=0)

    over = is_fold & (row >= 40)
    oe, ow, on, os = m * east_of(m), m * west_of(m), m * north_of(m), m * south_of(m)
    for k in range(LEVELS):
        at = slice(48 * k, 48 * k + 48)
        u, v = ux[at, :], vx[at, :]
        ue = jnp.where(over, east_of(u), u)
        uw = jnp.where(over, u, west_of(u))
        vt = jnp.where(over, north_of(v), v)
        vb = jnp.where(over, v, south_of(v))
        ce[at, :] = oe * (0.08 - jnp.minimum(ue, 0.0))
        cw[at, :] = ow * (0.08 + jnp.maximum(uw, 0.0))
        cn[at, :] = on * (0.08 - jnp.minimum(vt, 0.0))
        cs[at, :] = os * (0.08 + jnp.maximum(vb, 0.0))
        centre = 1.0 - oe * (0.08 + jnp.maximum(ue, 0.0)) - ow * (0.08 - jnp.minimum(uw, 0.0))
        centre = centre - on * (0.08 + jnp.maximum(vt, 0.0)) - os * (0.08 - jnp.minimum(vb, 0.0))
        top, mid = force[144:192, :], force[192:240, :]
        if k == 0:
            centre = centre - top
        elif k == 1:
            centre = centre - top - mid
        elif k == LEVELS - 1:
            centre = centre - mid
        else:
            centre = centre - 2.0 * mid
        cc[at, :] = centre

    def step(old, new):
        for t in range(2):
            for k in range(LEVELS):
                at = slice(48 * k, 48 * k + 48)
                base = 48 * (8 * t + k)
                q = old[base : base + 48, :]
                total = cc[at, :] * q + ce[at, :] * east_of(q) + cw[at, :] * west_of(q)
                total = total + cn[at, :] * north_of(q) + cs[at, :] * south_of(q)
                top, mid = force[144:192, :], force[192:240, :]
                if k == 0:
                    total = total + top * old[base + 48 : base + 96, :]
                elif k == 1:
                    total = total + top * old[base - 48 : base, :] + mid * old[base + 48 : base + 96, :]
                elif k == LEVELS - 1:
                    total = total + mid * old[base - 48 : base, :]
                else:
                    total = total + mid * (old[base - 48 : base, :] + old[base + 48 : base + 96, :])
                if t == 0:
                    total = total + (0.5 ** (k + 1)) * force[0:48, :]
                    if k == 0:
                        total = total + force[48:96, :]
                elif k == 0:
                    total = total + force[96:144, :]
                new[base : base + 48, :] = total

    def two(i, carry):
        step(qa, qb)
        step(qb, qa)
        return carry

    lax.fori_loop(0, STEPS // 2, two, 0)
    for t in range(2):
        for k in range(LEVELS):
            base = 48 * (8 * t + k)
            out[t, k] = qa[base + 8 : base + 40, 0:COLS]

    own_mask = mx[8:40, 0:COLS]
    heat = qa[8:40, 0:COLS] * own_mask
    sums = []
    table2 = (iota((COLS, COLS // 2), 0) // 2 == iota((COLS, COLS // 2), 1)).astype(F32)
    for value in (heat, own_mask):
        parts = []
        for j in range(4):
            pairs[...] = value[:, 128 * j : 128 * j + 128]
            parts.append(pairs[pl.ds(0, 16, stride=2), :] + pairs[pl.ds(1, 16, stride=2), :])
        narrow = jnp.concatenate(parts, axis=1)
        sums.append(jnp.dot(narrow, table2, precision=lax.Precision.HIGHEST, preferred_element_type=F32))
    result = sums[0] / jnp.maximum(sums[1], 1.0)
    sst[:, 0, :] = result[:, 0:128]
    sst[:, 1, :] = result[:, 128:256]


def place(b, l):
    return b * LON + l % LON


def body(temp_salt, east_vel, north_vel, land_mask, fluxes, remap_code, remap_weight, fold_source):
    axes = ("blk", "lon")
    b, l = lax.axis_index("blk"), lax.axis_index("lon")
    mirror = lax.rem(fold_source[0] + COLS * l, NX)
    sc = jnp.stack([b, l, mirror // COLS, mirror % COLS, (mirror - 1) // 2]).astype(jnp.int32)
    arrays = (temp_salt, north_vel, east_vel, remap_code, remap_weight, land_mask)

    specs, operands = [full((10, 32, 128))], [fluxes.reshape(10, 32, 128)]
    for x in arrays:
        lead = x.shape[:-2]
        for j in (0, 3):
            specs.append(at_block(lead + (ROWS, 128), (0,) * len(lead) + (0, j)))
            operands.append(x)
    to_west, to_east, band = pl.pallas_call(
        pack_columns,
        grid=(1,),
        in_specs=specs,
        out_specs=[full((3, ROWS, 128)), full((3, ROWS, 128)), full((5, 32, 128))],
        out_shape=[
            jax.ShapeDtypeStruct((3, ROWS, 128), F32),
            jax.ShapeDtypeStruct((3, ROWS, 128), F32),
            jax.ShapeDtypeStruct((5, 32, 128), F32),
        ],
        compiler_params=LIMIT,
        name="pack_columns",
    )(*operands)

    band_pairs = []
    for n in range(4):
        for blk in range(BLK):
            if blk > 0:
                band_pairs.append((place(blk, n), place(blk - 1, n)))
            if blk < BLK - 1:
                band_pairs.append((place(blk, 12 + n), place(blk + 1, 12 + n)))
        band_pairs.append((place(BLK - 1, 15 - n), place(BLK - 1, n)))
    other = lax.ppermute(band, axes, band_pairs)
    from_west = lax.ppermute(to_east, "lon", [(i, (i + 1) % LON) for i in range(LON)])
    from_east = lax.ppermute(to_west, "lon", [((i + 1) % LON, i) for i in range(LON)])

    chunks = pl.pallas_call(
        chunk_bands,
        grid=(1,),
        in_specs=[SCALARS, full((5, 32, 128)), full((5, 32, 128))],
        out_specs=full((512, 128)),
        out_shape=jax.ShapeDtypeStruct((512, 128), F32),
        scratch_shapes=[VMEM((160, 128), F32)] * 3,
        compiler_params=LIMIT,
        name="chunk_bands",
    )(sc, band, other)
    atm = lax.all_to_all(chunks, "lon", split_axis=0, concat_axis=0, tiled=True)

    specs, operands = [SCALARS, full((3, ROWS, 128)), full((3, ROWS, 128))], [sc, from_west, from_east]
    for x in arrays:
        lead = x.shape[:-2]
        for j in (0, 3):
            specs.append(at_block(lead + (8, COLS), (0,) * len(lead) + (j, 0)))
            operands.append(x)
    message = jax.ShapeDtypeStruct((MSG, 128), F32)
    sides, msg_a, msg_b = pl.pallas_call(
        pack_rows,
        grid=(1,),
        in_specs=specs,
        out_specs=[full((SLABS * ROWS, 128)), full((MSG, 128)), full((MSG, 128))],
        out_shape=[jax.ShapeDtypeStruct((SLABS * ROWS, 128), F32), message, message],
        scratch_shapes=[VMEM((5 * SLABS * 8, 128), F32)] * 2,
        compiler_params=LIMIT,
        name="pack_rows",
    )(*operands)

    on_chip = [(place(i, n), place(i ^ 1, n)) for i in range(BLK) for n in range(LON)]
    across = []
    for i in range(1, BLK - 1, 2):
        for n in range(LON):
            across += [(place(i, n), place(i + 1, n)), (place(i + 1, n), place(i, n))]
    got_a = lax.ppermute(msg_a, axes, on_chip)
    got_b = lax.ppermute(msg_b, axes, across)

    def branch(shift):
        def send(x):
            top = BLK - 1
            one = [(place(top, n), place(top, (shift - n) % LON)) for n in range(LON)]
            two = [(place(top, n), place(top, (shift - 1 - n) % LON)) for n in range(LON)]
            return lax.ppermute(x, axes, one), lax.ppermute(x, axes, two)

        return send

    fold_1, fold_2 = lax.switch(sc[2], [branch(k) for k in range(LON)], msg_b)

    ext = lambda n: VMEM((EXT_ROWS * n, EXT_COLS), F32)
    whole = lambda x: full(x.shape)
    state, skin = pl.pallas_call(
        interval,
        grid=(1,),
        in_specs=[SCALARS]
        + [whole(x) for x in arrays]
        + [full((SLABS * ROWS, 128))]
        + [full((MSG, 128))] * 4
        + [full((512, 128))],
        out_specs=[full((2, LEVELS, ROWS, COLS)), full((LON, 2, 128))],
        out_shape=[
            jax.ShapeDtypeStruct((2, LEVELS, ROWS, COLS), F32),
            jax.ShapeDtypeStruct((LON, 2, 128), F32),
        ],
        scratch_shapes=[VMEM((5 * SLABS * 8, 128), F32)] * 2
        + [ext(16), ext(16), ext(8), ext(8), ext(4), ext(4), ext(1)]
        + [VMEM((120, 384), F32), VMEM((25 * 48, 128), F32), ext(9)]
        + [ext(8)] * 5
        + [ext(5), VMEM((ROWS, 128), F32)],
        compiler_params=LIMIT,
        name="interval",
    )(sc, *arrays, sides, got_a, got_b, fold_1, fold_2, atm)
    bands = lax.all_to_all(skin, "lon", split_axis=0, concat_axis=0, tiled=True)
    return state, bands.reshape(1, LON * 256)


def solution(mesh):
    placed = (
        P(None, None, "blk", "lon"),
        P(None, "blk", "lon"),
        P(None, "blk", "lon"),
        P("blk", "lon"),
        P(None, ("blk", "lon"), None),
        P(None, "blk", "lon"),
        P(None, "blk", "lon"),
        P("lon"),
    )
    return jax.shard_map(
        body,
        mesh=mesh,
        in_specs=placed,
        out_specs=(P(None, None, "blk", "lon"), P(("blk", "lon"), None)),
        check_vma=False,
    )
```

```python
import jax
import jax.numpy as jnp
from jax import lax
from jax.experimental import pallas as pl
from jax.experimental.pallas import tpu as pltpu
from jax.sharding import PartitionSpec as P

STEPS = 6
F32 = jnp.float32
LEVELS = 8
BLK, LON = 8, 16
ROWS, COLS = 32, 512
EXT_ROWS, EXT_COLS = 48, 640
NX = 8192
SLABS = 41
PART = 232
HEAD = 32
WHOLE = HEAD + 4 * PART
HALF = HEAD + 2 * PART
VMEM = pltpu.VMEM
SMEM = pltpu.SMEM
LIMIT = pltpu.CompilerParams(vmem_limit_bytes=56 * 1024 * 1024)


def iota(shape, dim):
    return lax.broadcasted_iota(jnp.int32, shape, dim)


def full(shape):
    return pl.BlockSpec(shape, lambda i: (0,) * len(shape))


def at_block(shape, place):
    return pl.BlockSpec(shape, lambda i: place)


SCALARS = pl.BlockSpec(memory_space=SMEM)


def combine_bands(flux, band):
    band[0] = flux[0]
    band[1] = flux[1] + flux[2] + flux[3] - 0.33 * flux[5]
    band[2] = flux[4] + flux[5] + flux[6] + flux[7]
    band[3] = flux[8]
    band[4] = flux[9]


def pack_columns(st0, st3, vn0, vn3, ve0, ve3, cd0, cd3, wt0, wt3, mk0, mk3, to_west, to_east):
    lane = iota((ROWS, 128), 1)

    def pack(groups, shift, out):
        for g, tiles in enumerate(groups):
            acc = jnp.zeros((ROWS, 128), F32)
            for j, tile in enumerate(tiles):
                moved = pltpu.roll(tile().astype(F32), (8 * j + shift) % 128, axis=1)
                acc = jnp.where((lane >= 8 * j) & (lane < 8 * j + 8), moved, acc)
            out[g] = acc

    def groups(st, vn, ve, cd, wt, mk):
        first = [lambda t=t, k=k: st[t, k] for t in range(2) for k in range(LEVELS)]
        second = [lambda k=k: vn[k] for k in range(LEVELS)] + [lambda k=k: ve[k] for k in range(LEVELS)]
        third = [lambda k=k: cd[k] for k in range(4)] + [lambda k=k: wt[k] for k in range(4)] + [lambda: mk[...]]
        return [first, second, third]

    pack(groups(st0, vn0, ve0, cd0, wt0, mk0), 0, to_west)
    pack(groups(st3, vn3, ve3, cd3, wt3, mk3), 6, to_east)


def chunk_bands(sc, band, other, out, own, held, turned):
    is_fold = sc[0] == BLK - 1
    own[...] = band[...].reshape(160, 128)
    held[...] = other[...].reshape(160, 128)

    @pl.when(is_fold & (sc[1] < 4))
    def _():
        pole = sc[4]
        pq, pr = pole // 128, pole % 128
        lane8 = iota((8, 128), 1)
        index = (pr - lane8) & 127
        for n in range(20):
            turned[8 * n : 8 * n + 8, :] = jnp.take_along_axis(held[8 * n : 8 * n + 8, :], index, axis=1)
        lane1 = iota((1, 128), 1)

        def one(row, carry):
            near = (pq - row) & 31
            far = (pq - row - 1) & 31
            for f in range(5):
                a = turned[pl.ds(32 * f + near, 1), :]
                b = turned[pl.ds(32 * f + far, 1), :]
                held[pl.ds(32 * f + row, 1), :] = jnp.where(lane1 <= pr, a, b)
            return carry

        lax.fori_loop(0, 32, one, 0)

    lane = iota((16, 128), 1)
    for slot, src in enumerate((own, held)):
        for f in range(5):
            even = src[pl.ds(32 * f, 16, stride=2), :]
            odd = src[pl.ds(32 * f + 1, 16, stride=2), :]
            side = jnp.where(lane < 64, pltpu.roll(even, 15, axis=0), pltpu.roll(odd, 1, axis=0))
            for part, value in enumerate((even, odd, side)):
                out[pl.ds(16 * slot + 3 * f + part, 16, stride=32), :] = value
        out[pl.ds(16 * slot + 15, 16, stride=32), :] = jnp.zeros((16, 128), F32)


def slot_lanes(lane8, slot):
    return (lane8 >= 16 * slot) & (lane8 < 16 * slot + 12)


def fold_lanes(sc, lane8):
    rq, rr = sc[3] // 128, sc[3] % 128
    return rq, (rr - lane8) & 127, lane8 <= rr


def pack_rows(
    sc, st_s, st_n, vn_s, vn_n, ve_s, ve_n, cd_s, cd_n, wt_s, wt_n, mk_s, mk_n,
    msg_a, msg_b, low, high, window, south, north,
):
    lane8 = iota((8, 128), 1)

    def stage(dst, st, vn, ve, cd, wt):
        for j in range(4):
            cols = slice(128 * j, 128 * j + 128)

            def put(s, value):
                dst[(j * SLABS + s) * 8 : (j * SLABS + s) * 8 + 8, :] = value

            for k in range(LEVELS):
                put(k, st[0, k, :, cols])
                put(8 + k, st[1, k, :, cols])
                put(16 + k, vn[k, :, cols])
                put(24 + k, ve[k, :, cols])
            for k in range(4):
                put(32 + k, cd[k, :, cols].astype(F32))
                put(36 + k, wt[k, :, cols])

    stage(south, st_s, vn_s, ve_s, cd_s, wt_s)
    stage(north, st_n, vn_n, ve_n, cd_n, wt_n)
    for j in range(4):
        base = (j * SLABS + 40) * 8
        cols = slice(128 * j, 128 * j + 128)
        south[base : base + 8, :] = mk_s[:, cols].astype(F32)
        flipped = mk_n[:, cols].astype(F32)
        for i in range(8):
            north[base + i : base + i + 1, :] = flipped[7 - i : 8 - i]

    def loader(edge, is_north, n):
        if n == 28:
            return lambda j: edge[pl.ds((j * SLABS + 40) * 8, 8), :]
        i, rt = n // 5, n % 5
        row = 7 - i if is_north else i
        return lambda j: edge[pl.ds((j * SLABS + rt * 8) * 8 + row, 8, stride=8), :]

    def build(put, edge, is_north):
        for n in range(29):
            load = loader(edge, is_north, n)
            for j in range(4):
                put(j, n, load(j))

    def put_a(j, n, tile):
        at = HEAD + j * PART + 8 * n
        msg_a[at : at + 8, :] = tile

    def put_b(j, n, tile):
        at = HEAD + j * PART + 8 * n
        msg_b[at : at + 8, :] = tile

    parity = sc[0] & 1
    window[...] = jnp.zeros_like(window)

    @pl.when(parity == 0)
    def _():
        build(put_a, north, True)
        build(put_b, south, False)

    @pl.when(parity == 1)
    def _():
        build(put_a, south, False)

    @pl.when((parity == 1) & (sc[0] < BLK - 1))
    def _():
        build(put_b, north, True)

    @pl.when(sc[0] == BLK - 1)
    def _():
        rq, index, near = fold_lanes(sc, lane8)
        order = [rq, (rq - 1) & 3, (rq - 2) & 3, (rq - 3) & 3]
        corner = [jnp.zeros((8, 128), F32) for _ in range(4)]
        for n in range(29):
            load = loader(north, True, n)
            g = [jnp.take_along_axis(load(j), index, axis=1) for j in order]
            for j in range(4):
                tile = jnp.where(near, g[j], g[(j + 1) % 4])
                put_b(j, n, tile)
                at = HEAD + (j % 2) * PART + 8 * n
                (low, high)[j // 2][at : at + 8, :] = tile
            below = jnp.where(rq == 0, 0.0, g[1])
            above = jnp.where(rq == 3, 0.0, g[3])
            fifth = jnp.where(lane8 < 64, jnp.where(near, g[0], below), jnp.where(near, above, g[0]))
            moved = pltpu.roll(fifth, (6 + 16 * (n % 8)) % 128, axis=1)
            corner[n // 8] = jnp.where(slot_lanes(lane8, n % 8), moved, corner[n // 8])
        for v in range(4):
            window[8 * v : 8 * v + 8, :] = corner[v]


def pack_corners(
    sc, from_west, from_east, window, a_in, b_in, low_in, high_in, sides, corner_a, corner_b, corner_low, corner_high
):
    lane = iota((ROWS, 128), 1)
    for s in range(SLABS):
        g, j = s // 16, s % 16
        east = pltpu.roll(from_east[g], (128 - 8 * j) % 128, axis=1)
        west = pltpu.roll(from_west[g], (122 - 8 * j) % 128, axis=1)
        sides[ROWS * s : ROWS * s + ROWS, :] = jnp.where(lane < 6, east, jnp.where(lane >= 122, west, 0.0))
    lane8 = iota((8, 128), 1)

    def build(dst, is_north, turn):
        corner = [window[8 * v : 8 * v + 8, :] if turn else jnp.zeros((8, 128), F32) for v in range(4)]
        if turn:
            rq, index, near = fold_lanes(sc, lane8)
            low = (lane8 < 64) & (rq == 0) & ~near
            high = (lane8 >= 64) & (rq == 3) & near
        for n in range(29):
            if n < 28:
                i, rt = n // 5, n % 5
                row = 31 - i if is_north else i
                fifth = sides[pl.ds(rt * 8 * ROWS + row, 8, stride=ROWS), :]
            else:
                mask = sides[40 * ROWS + (24 if is_north else 0) : 40 * ROWS + (32 if is_north else 8), :]
                fifth = jnp.concatenate([mask[7 - i : 8 - i] for i in range(8)], axis=0) if is_north else mask
            if turn:
                fifth = jnp.where(low | high, jnp.take_along_axis(fifth, index, axis=1), 0.0)
            moved = pltpu.roll(fifth, (6 + 16 * (n % 8)) % 128, axis=1)
            if turn:
                corner[n // 8] = corner[n // 8] + jnp.where(slot_lanes(lane8, n % 8), moved, 0.0)
            else:
                corner[n // 8] = jnp.where(slot_lanes(lane8, n % 8), moved, corner[n // 8])
        for v in range(4):
            dst[8 * v : 8 * v + 8, :] = corner[v]

    parity = sc[0] & 1

    @pl.when(parity == 0)
    def _():
        build(corner_a, True, False)
        build(corner_b, False, False)

    @pl.when(parity == 1)
    def _():
        build(corner_a, False, False)

    @pl.when((parity == 1) & (sc[0] < BLK - 1))
    def _():
        build(corner_b, True, False)

    @pl.when(sc[0] == BLK - 1)
    def _():
        build(corner_b, True, True)
        corner_low[...] = corner_b[...]
        corner_high[...] = corner_b[...]


def interval(
    sc, st, vn, ve, cd, wt, mk, sides, got_a, got_b, major, minor, atm, out, sst,
    ghost_s, ghost_n, qa, qb, vx, ux, cx, wx, mx, atm_rows, doubled, coef,
    ce, cw, cn, cs, cc, force, pairs,
):
    lane8 = iota((8, 128), 1)
    edge_lanes = (lane8 < 6) | (lane8 >= 122)
    is_fold = sc[0] == BLK - 1
    parity = sc[0] & 1
    ghost_s[...] = jnp.zeros_like(ghost_s)
    ghost_n[...] = jnp.zeros_like(ghost_n)

    def unpack(load, corner, ghost, is_north):
        for n in range(29):
            i, rt = (n // 5, n % 5) if n < 28 else (0, 5)
            tiles = [load(j, n) for j in range(4)]
            slot = n % 8
            fifth = pltpu.roll(corner(n // 8, slot), (256 - 6 - 16 * slot) % 128, axis=1)
            tiles.append(jnp.where(edge_lanes, fifth, 0.0))
            for j in range(5):
                if n < 28:
                    row = i if is_north else 7 - i
                    ghost[pl.ds((j * SLABS + rt * 8) * 8 + row, 8, stride=8), :] = tiles[j]
                else:
                    base = (j * SLABS + 40) * 8
                    if is_north:
                        ghost[base : base + 8, :] = tiles[j]
                    else:
                        for r in range(8):
                            ghost[base + r : base + r + 1, :] = tiles[j][7 - r : 8 - r]

    def plain(msg, ghost, is_north):
        unpack(
            lambda j, n: msg[HEAD + j * PART + 8 * n : HEAD + j * PART + 8 * n + 8, :],
            lambda v, slot: msg[8 * v : 8 * v + 8, :],
            ghost,
            is_north,
        )

    @pl.when(parity == 0)
    def _():
        plain(got_a, ghost_n, True)
        plain(got_b, ghost_s, False)

    @pl.when(parity == 1)
    def _():
        plain(got_a, ghost_s, False)

    @pl.when((parity == 1) & (sc[0] < BLK - 1))
    def _():
        plain(got_b, ghost_n, True)

    def fold(first_is_major):
        seam = sc[3]

        def load(j, n):
            at = HEAD + j * PART + 8 * n
            value = major[at : at + 8, :]
            if first_is_major == (j >= 2):
                at = HEAD + (j % 2) * PART + 8 * n
                second = lane8 + 128 * j > seam
                value = jnp.where(second if first_is_major else ~second, minor[at : at + 8, :], value)
            return value

        def corner(v, slot):
            at = slice(8 * v, 8 * v + 8)
            first, second = (major, minor) if first_is_major else (minor, major)
            return jnp.where((lane8 & 15) < 6, first[at, :], second[at, :])

        unpack(load, corner, ghost_n, True)

    @pl.when(is_fold & (sc[3] >= 256))
    def _():
        fold(True)

    @pl.when(is_fold & (sc[3] < 256))
    def _():
        fold(False)

    def extend(ext, at, s, own, north_fix=None):
        base = EXT_ROWS * at
        ext[base + 8 : base + 40, 0:COLS] = own
        ext[base + 8 : base + 40, COLS:EXT_COLS] = sides[ROWS * s : ROWS * s + ROWS, :]
        for j in range(5):
            cols = slice(128 * j, 128 * j + 128)
            g = (j * SLABS + s) * 8
            ext[base : base + 8, cols] = ghost_s[g : g + 8, :]
            top = ghost_n[g : g + 8, :]
            ext[base + 40 : base + 48, cols] = top if north_fix is None else north_fix(top)

    flip = jnp.where(is_fold, -1.0, 1.0).astype(F32)
    for t in range(2):
        for k in range(LEVELS):
            extend(qa, 8 * t + k, 8 * t + k, st[t, k])
    for k in range(LEVELS):
        extend(vx, k, 16 + k, vn[k], lambda g: g * flip)
        extend(ux, k, 24 + k, ve[k], lambda g: g * flip)
    for k in range(4):
        extend(cx, k, 32 + k, cd[k].astype(F32), lambda g: jnp.where(is_fold, 8.0 - g, g))
        extend(wx, k, 36 + k, wt[k])
    extend(mx, 0, 40, mk[...].astype(F32))

    row8 = iota((8, 128), 0)
    for f in range(5):
        for part in range(3):
            cols = slice(128 * part, 128 * part + 128)
            atm_rows[24 * f : 24 * f + 16, cols] = atm[pl.ds(3 * f + part, 16, stride=32), :]
            far = atm[pl.ds(16 + 3 * f + part, 16, stride=32), :]
            atm_rows[24 * f + 16 : 24 * f + 24, cols] = jnp.where(row8 < 4, far[0:8], far[8:16])
    src = iota((384, EXT_COLS), 0)
    dst = iota((384, EXT_COLS), 1)
    table = (src == jnp.where(dst < 576, dst // 2, dst // 2 + 64)).astype(F32)
    wide = jnp.dot(atm_rows[...], table, precision=lax.Precision.HIGHEST, preferred_element_type=F32)
    for f in range(5):
        for j in range(5):
            tile = wide[24 * f : 24 * f + 24, 128 * j : 128 * j + 128]
            base = (5 * f + j) * 48
            doubled[pl.ds(base, 24, stride=2), :] = tile
            doubled[pl.ds(base + 1, 24, stride=2), :] = tile

    shape = (EXT_ROWS, EXT_COLS)
    row = iota(shape, 0)
    wsum = wx[0:48, :] + wx[48:96, :] + wx[96:144, :] + wx[144:192, :]
    inv = 1.0 / jnp.where(wsum > 0.0, wsum, 1.0)
    up_ok = jnp.where(is_fold & (row >= 38) & (row < 40), 0.0, 1.0)
    down_ok = jnp.where(is_fold & (row >= 40) & (row < 42), 0.0, 1.0)
    for c in range(9):
        total = jnp.zeros(shape, F32)
        for t in range(4):
            total = total + jnp.where(cx[48 * t : 48 * t + 48, :] == float(c), wx[48 * t : 48 * t + 48, :], 0.0)
        total = total * inv
        if c < 3:
            total = total * down_ok
        if c >= 6:
            total = total * up_ok
        coef[48 * c : 48 * c + 48, :] = total
    fields = []
    for f in range(5):
        tiles = [doubled[(5 * f + j) * 48 : (5 * f + j) * 48 + 48, :] for j in range(5)]
        grid = jnp.concatenate(tiles, axis=1)
        grid = jnp.concatenate([grid[40:48], grid[0:40]], axis=0)
        total = jnp.zeros(shape, F32)
        for dy in (-1, 0, 1):
            by_row = grid if dy == 0 else pltpu.roll(grid, (EXT_ROWS - 2 * dy) % EXT_ROWS, axis=0)
            for dx in (-1, 0, 1):
                c = 3 * (dy + 1) + dx + 1
                moved = by_row if dx == 0 else pltpu.roll(by_row, (EXT_COLS - 2 * dx) % EXT_COLS, axis=1)
                total = total + moved * coef[48 * c : 48 * c + 48, :]
        fields.append(total)
    m = mx[...]
    force[0:48, :] = 0.05 * m * fields[0]
    force[48:96, :] = 0.05 * m * fields[1]
    force[96:144, :] = -0.05 * m * fields[2]
    kv = 0.05 + 0.04 * jnp.sqrt(fields[3] * fields[3] + fields[4] * fields[4] + 0.01)
    force[144:192, :] = m * kv
    force[192:240, :] = 0.05 * m

    def east_of(x):
        return pltpu.roll(x, EXT_COLS - 1, axis=1)

    def west_of(x):
        return pltpu.roll(x, 1, axis=1)

    def north_of(x):
        return pltpu.roll(x, EXT_ROWS - 1, axis=0)

    def south_of(x):
        return pltpu.roll(x, 1, axis=0)

    over = is_fold & (row >= 40)
    oe, ow, on, os = m * east_of(m), m * west_of(m), m * north_of(m), m * south_of(m)
    for k in range(LEVELS):
        at = slice(48 * k, 48 * k + 48)
        u, v = ux[at, :], vx[at, :]
        ue = jnp.where(over, east_of(u), u)
        uw = jnp.where(over, u, west_of(u))
        vt = jnp.where(over, north_of(v), v)
        vb = jnp.where(over, v, south_of(v))
        ce[at, :] = oe * (0.08 - jnp.minimum(ue, 0.0))
        cw[at, :] = ow * (0.08 + jnp.maximum(uw, 0.0))
        cn[at, :] = on * (0.08 - jnp.minimum(vt, 0.0))
        cs[at, :] = os * (0.08 + jnp.maximum(vb, 0.0))
        centre = 1.0 - oe * (0.08 + jnp.maximum(ue, 0.0)) - ow * (0.08 - jnp.minimum(uw, 0.0))
        centre = centre - on * (0.08 + jnp.maximum(vt, 0.0)) - os * (0.08 - jnp.minimum(vb, 0.0))
        top, mid = force[144:192, :], force[192:240, :]
        if k == 0:
            centre = centre - top
        elif k == 1:
            centre = centre - top - mid
        elif k == LEVELS - 1:
            centre = centre - mid
        else:
            centre = centre - 2.0 * mid
        cc[at, :] = centre

    def step(old, new):
        for t in range(2):
            for k in range(LEVELS):
                at = slice(48 * k, 48 * k + 48)
                base = 48 * (8 * t + k)
                q = old[base : base + 48, :]
                total = cc[at, :] * q + ce[at, :] * east_of(q) + cw[at, :] * west_of(q)
                total = total + cn[at, :] * north_of(q) + cs[at, :] * south_of(q)
                top, mid = force[144:192, :], force[192:240, :]
                if k == 0:
                    total = total + top * old[base + 48 : base + 96, :]
                elif k == 1:
                    total = total + top * old[base - 48 : base, :] + mid * old[base + 48 : base + 96, :]
                elif k == LEVELS - 1:
                    total = total + mid * old[base - 48 : base, :]
                else:
                    total = total + mid * (old[base - 48 : base, :] + old[base + 48 : base + 96, :])
                if t == 0:
                    total = total + (0.5 ** (k + 1)) * force[0:48, :]
                    if k == 0:
                        total = total + force[48:96, :]
                elif k == 0:
                    total = total + force[96:144, :]
                new[base : base + 48, :] = total

    def two(i, carry):
        step(qa, qb)
        step(qb, qa)
        return carry

    lax.fori_loop(0, STEPS // 2, two, 0)
    for t in range(2):
        for k in range(LEVELS):
            base = 48 * (8 * t + k)
            out[t, k] = qa[base + 8 : base + 40, 0:COLS]

    own_mask = mx[8:40, 0:COLS]
    heat = qa[8:40, 0:COLS] * own_mask
    sums = []
    table2 = (iota((COLS, COLS // 2), 0) // 2 == iota((COLS, COLS // 2), 1)).astype(F32)
    for value in (heat, own_mask):
        parts = []
        for j in range(4):
            pairs[...] = value[:, 128 * j : 128 * j + 128]
            parts.append(pairs[pl.ds(0, 16, stride=2), :] + pairs[pl.ds(1, 16, stride=2), :])
        narrow = jnp.concatenate(parts, axis=1)
        sums.append(jnp.dot(narrow, table2, precision=lax.Precision.HIGHEST, preferred_element_type=F32))
    result = sums[0] / jnp.maximum(sums[1], 1.0)
    sst[:, 0, :] = result[:, 0:128]
    sst[:, 1, :] = result[:, 128:256]


def place(b, l):
    return b * LON + l % LON


def body(temp_salt, east_vel, north_vel, land_mask, fluxes, remap_code, remap_weight, fold_source):
    axes = ("blk", "lon")
    b, l = lax.axis_index("blk"), lax.axis_index("lon")
    mirror = lax.rem(fold_source[0] + COLS * l, NX)
    sc = jnp.stack([b, l, mirror // COLS, mirror % COLS, (mirror - 1) // 2]).astype(jnp.int32)
    arrays = (temp_salt, north_vel, east_vel, remap_code, remap_weight, land_mask)

    sds = lambda *shape: jax.ShapeDtypeStruct(shape, F32)
    band = pl.pallas_call(
        combine_bands,
        grid=(1,),
        in_specs=[full((10, 32, 128))],
        out_specs=full((5, 32, 128)),
        out_shape=sds(5, 32, 128),
        compiler_params=LIMIT,
        name="combine_bands",
    )(fluxes.reshape(10, 32, 128))
    band_pairs = []
    for n in range(4):
        for blk in range(BLK):
            if blk > 0:
                band_pairs.append((place(blk, n), place(blk - 1, n)))
            if blk < BLK - 1:
                band_pairs.append((place(blk, 12 + n), place(blk + 1, 12 + n)))
        band_pairs.append((place(BLK - 1, 15 - n), place(BLK - 1, n)))
    other = lax.ppermute(band, axes, band_pairs)

    first, _ = lax.optimization_barrier((land_mask, band))
    specs, operands = [], []
    for x in (*arrays[:-1], first):
        lead = x.shape[:-2]
        for j in (0, 3):
            specs.append(at_block(lead + (ROWS, 128), (0,) * len(lead) + (0, j)))
            operands.append(x)
    to_west, to_east = pl.pallas_call(
        pack_columns,
        grid=(1,),
        in_specs=specs,
        out_specs=[full((3, ROWS, 128))] * 2,
        out_shape=[sds(3, ROWS, 128)] * 2,
        compiler_params=LIMIT,
        name="pack_columns",
    )(*operands)
    from_west = lax.ppermute(to_east, "lon", [(i, (i + 1) % LON) for i in range(LON)])
    from_east = lax.ppermute(to_west, "lon", [((i + 1) % LON, i) for i in range(LON)])

    chunks = pl.pallas_call(
        chunk_bands,
        grid=(1,),
        in_specs=[SCALARS, full((5, 32, 128)), full((5, 32, 128))],
        out_specs=full((512, 128)),
        out_shape=sds(512, 128),
        scratch_shapes=[VMEM((160, 128), F32)] * 3,
        compiler_params=LIMIT,
        name="chunk_bands",
    )(sc, band, other)
    atm = lax.all_to_all(chunks, "lon", split_axis=0, concat_axis=0, tiled=True)

    later, _ = lax.optimization_barrier((sc, chunks))
    specs, operands = [SCALARS], [later]
    for x in arrays:
        lead = x.shape[:-2]
        for j in (0, 3):
            specs.append(at_block(lead + (8, COLS), (0,) * len(lead) + (j, 0)))
            operands.append(x)
    sizes = (WHOLE, WHOLE, HALF, HALF)
    *messages, window = pl.pallas_call(
        pack_rows,
        grid=(1,),
        in_specs=specs,
        out_specs=[full((n, 128)) for n in sizes] + [full((HEAD, 128))],
        out_shape=[sds(n, 128) for n in sizes] + [sds(HEAD, 128)],
        scratch_shapes=[VMEM((4 * SLABS * 8, 128), F32)] * 2,
        compiler_params=LIMIT,
        name="pack_rows",
    )(*operands)
    later, _ = lax.optimization_barrier((sc, atm))
    sides, msg_a, msg_b, low, high = pl.pallas_call(
        pack_corners,
        grid=(1,),
        in_specs=[SCALARS, full((3, ROWS, 128)), full((3, ROWS, 128)), full((HEAD, 128))]
        + [pl.BlockSpec(memory_space=pl.ANY)] * 4,
        out_specs=[full((SLABS * ROWS, 128))] + [full((HEAD, 128))] * 4,
        out_shape=[sds(SLABS * ROWS, 128)] + [sds(n, 128) for n in sizes],
        input_output_aliases={4: 1, 5: 2, 6: 3, 7: 4},
        compiler_params=LIMIT,
        name="pack_corners",
    )(later, from_west, from_east, window, *messages)

    on_chip = [(place(i, n), place(i ^ 1, n)) for i in range(BLK) for n in range(LON)]
    across = []
    for i in range(1, BLK - 1, 2):
        for n in range(LON):
            across += [(place(i, n), place(i + 1, n)), (place(i + 1, n), place(i, n))]
    got_a = lax.ppermute(msg_a, axes, on_chip)
    got_b = lax.ppermute(msg_b, axes, across)

    def branch(shift, second_half):
        top = BLK - 1
        one = [(place(top, n), place(top, (shift - n) % LON)) for n in range(LON)]
        two = [(place(top, n), place(top, (shift - 1 - n) % LON)) for n in range(LON)]

        def send(whole, low, high):
            if second_half:
                return lax.ppermute(whole, axes, one), lax.ppermute(high, axes, two)
            return lax.ppermute(whole, axes, two), lax.ppermute(low, axes, one)

        return send

    got_f = lax.switch(
        sc[2] * 2 + sc[3] // 256,
        [branch(shift, half) for shift in range(LON) for half in range(2)],
        msg_b,
        low,
        high,
    )

    ext = lambda n: VMEM((EXT_ROWS * n, EXT_COLS), F32)
    whole = lambda x: full(x.shape)
    state, skin = pl.pallas_call(
        interval,
        grid=(1,),
        in_specs=[SCALARS]
        + [whole(x) for x in arrays]
        + [full(x.shape) for x in (sides, got_a, got_b, *got_f, atm)],
        out_specs=[full((2, LEVELS, ROWS, COLS)), full((LON, 2, 128))],
        out_shape=[
            jax.ShapeDtypeStruct((2, LEVELS, ROWS, COLS), F32),
            jax.ShapeDtypeStruct((LON, 2, 128), F32),
        ],
        scratch_shapes=[VMEM((5 * SLABS * 8, 128), F32)] * 2
        + [ext(16), ext(16), ext(8), ext(8), ext(4), ext(4), ext(1)]
        + [VMEM((120, 384), F32), VMEM((25 * 48, 128), F32), ext(9)]
        + [ext(8)] * 5
        + [ext(5), VMEM((ROWS, 128), F32)],
        compiler_params=LIMIT,
        name="interval",
    )(sc, *arrays, sides, got_a, got_b, *got_f, atm)
    bands = lax.all_to_all(skin, "lon", split_axis=0, concat_axis=0, tiled=True)
    return state, bands.reshape(1, LON * 256)


def solution(mesh):
    placed = (
        P(None, None, "blk", "lon"),
        P(None, "blk", "lon"),
        P(None, "blk", "lon"),
        P("blk", "lon"),
        P(None, ("blk", "lon"), None),
        P(None, "blk", "lon"),
        P(None, "blk", "lon"),
        P("lon"),
    )
    return jax.shard_map(
        body,
        mesh=mesh,
        in_specs=placed,
        out_specs=(P(None, None, "blk", "lon"), P(("blk", "lon"), None)),
        check_vma=False,
    )
```

```python
import jax
import jax.numpy as jnp
from jax import lax
from jax.experimental import pallas as pl
from jax.experimental.pallas import tpu as pltpu
from jax.sharding import PartitionSpec as P

STEPS = 6
F32 = jnp.float32
LEVELS = 8
BLK, LON = 8, 16
ROWS, COLS = 32, 512
EXT_ROWS, EXT_COLS = 48, 640
NX = 8192
SLABS = 41
PART = 232
HEAD = 32
WHOLE = HEAD + 4 * PART
HALF = HEAD + 2 * PART
VMEM = pltpu.VMEM
SMEM = pltpu.SMEM
LIMIT = pltpu.CompilerParams(vmem_limit_bytes=56 * 1024 * 1024)


def iota(shape, dim):
    return lax.broadcasted_iota(jnp.int32, shape, dim)


def full(shape):
    return pl.BlockSpec(shape, lambda i: (0,) * len(shape))


def at_block(shape, place):
    return pl.BlockSpec(shape, lambda i: place)


SCALARS = pl.BlockSpec(memory_space=SMEM)


def combine_bands(flux, band):
    band[0] = flux[0]
    band[1] = flux[1] + flux[2] + flux[3] - 0.33 * flux[5]
    band[2] = flux[4] + flux[5] + flux[6] + flux[7]
    band[3] = flux[8]
    band[4] = flux[9]


def pack_columns(st0, st3, vn0, vn3, ve0, ve3, cd0, cd3, wt0, wt3, mk0, mk3, to_west, to_east):
    lane = iota((ROWS, 128), 1)

    def pack(groups, shift, out):
        for g, tiles in enumerate(groups):
            acc = jnp.zeros((ROWS, 128), F32)
            for j, tile in enumerate(tiles):
                moved = pltpu.roll(tile().astype(F32), (8 * j + shift) % 128, axis=1)
                acc = jnp.where((lane >= 8 * j) & (lane < 8 * j + 8), moved, acc)
            out[g] = acc

    def groups(st, vn, ve, cd, wt, mk):
        first = [lambda t=t, k=k: st[t, k] for t in range(2) for k in range(LEVELS)]
        second = [lambda k=k: vn[k] for k in range(LEVELS)] + [lambda k=k: ve[k] for k in range(LEVELS)]
        third = [lambda k=k: cd[k] for k in range(4)] + [lambda k=k: wt[k] for k in range(4)] + [lambda: mk[...]]
        return [first, second, third]

    pack(groups(st0, vn0, ve0, cd0, wt0, mk0), 0, to_west)
    pack(groups(st3, vn3, ve3, cd3, wt3, mk3), 6, to_east)


def chunk_bands(sc, band, other, out, own, held, turned):
    is_fold = sc[0] == BLK - 1
    own[...] = band[...].reshape(160, 128)
    held[...] = other[...].reshape(160, 128)

    @pl.when(is_fold & (sc[1] < 4))
    def _():
        pole = sc[4]
        pq, pr = pole // 128, pole % 128
        lane8 = iota((8, 128), 1)
        index = (pr - lane8) & 127
        for n in range(20):
            turned[8 * n : 8 * n + 8, :] = jnp.take_along_axis(held[8 * n : 8 * n + 8, :], index, axis=1)
        lane1 = iota((1, 128), 1)

        def one(row, carry):
            near = (pq - row) & 31
            far = (pq - row - 1) & 31
            for f in range(5):
                a = turned[pl.ds(32 * f + near, 1), :]
                b = turned[pl.ds(32 * f + far, 1), :]
                held[pl.ds(32 * f + row, 1), :] = jnp.where(lane1 <= pr, a, b)
            return carry

        lax.fori_loop(0, 32, one, 0)

    lane = iota((16, 128), 1)
    for slot, src in enumerate((own, held)):
        for f in range(5):
            even = src[pl.ds(32 * f, 16, stride=2), :]
            odd = src[pl.ds(32 * f + 1, 16, stride=2), :]
            side = jnp.where(lane < 64, pltpu.roll(even, 15, axis=0), pltpu.roll(odd, 1, axis=0))
            for part, value in enumerate((even, odd, side)):
                out[pl.ds(16 * slot + 3 * f + part, 16, stride=32), :] = value
        out[pl.ds(16 * slot + 15, 16, stride=32), :] = jnp.zeros((16, 128), F32)


def slot_lanes(lane8, slot):
    return (lane8 >= 16 * slot) & (lane8 < 16 * slot + 12)


def fold_lanes(sc, lane8):
    rq, rr = sc[3] // 128, sc[3] % 128
    return rq, (rr - lane8) & 127, lane8 <= rr


def pack_rows(
    sc, st_s, st_n, vn_s, vn_n, ve_s, ve_n, cd_s, cd_n, wt_s, wt_n, mk_s, mk_n,
    msg_a, msg_b, low, high, window, south, north,
):
    lane8 = iota((8, 128), 1)

    def stage(dst, st, vn, ve, cd, wt):
        for j in range(4):
            cols = slice(128 * j, 128 * j + 128)

            def put(s, value):
                dst[(j * SLABS + s) * 8 : (j * SLABS + s) * 8 + 8, :] = value

            for k in range(LEVELS):
                put(k, st[0, k, :, cols])
                put(8 + k, st[1, k, :, cols])
                put(16 + k, vn[k, :, cols])
                put(24 + k, ve[k, :, cols])
            for k in range(4):
                put(32 + k, cd[k, :, cols].astype(F32))
                put(36 + k, wt[k, :, cols])

    stage(south, st_s, vn_s, ve_s, cd_s, wt_s)
    stage(north, st_n, vn_n, ve_n, cd_n, wt_n)
    for j in range(4):
        base = (j * SLABS + 40) * 8
        cols = slice(128 * j, 128 * j + 128)
        south[base : base + 8, :] = mk_s[:, cols].astype(F32)
        flipped = mk_n[:, cols].astype(F32)
        for i in range(8):
            north[base + i : base + i + 1, :] = flipped[7 - i : 8 - i]

    def loader(edge, is_north, n):
        if n == 28:
            return lambda j: edge[pl.ds((j * SLABS + 40) * 8, 8), :]
        i, rt = n // 5, n % 5
        row = 7 - i if is_north else i
        return lambda j: edge[pl.ds((j * SLABS + rt * 8) * 8 + row, 8, stride=8), :]

    def build(put, edge, is_north):
        for n in range(29):
            load = loader(edge, is_north, n)
            for j in range(4):
                put(j, n, load(j))

    def put_a(j, n, tile):
        at = HEAD + j * PART + 8 * n
        msg_a[at : at + 8, :] = tile

    def put_b(j, n, tile):
        at = HEAD + j * PART + 8 * n
        msg_b[at : at + 8, :] = tile

    parity = sc[0] & 1
    window[...] = jnp.zeros_like(window)

    @pl.when(parity == 0)
    def _():
        build(put_a, north, True)
        build(put_b, south, False)

    @pl.when(parity == 1)
    def _():
        build(put_a, south, False)

    @pl.when((parity == 1) & (sc[0] < BLK - 1))
    def _():
        build(put_b, north, True)

    @pl.when(sc[0] == BLK - 1)
    def _():
        rq, index, near = fold_lanes(sc, lane8)
        order = [rq, (rq - 1) & 3, (rq - 2) & 3, (rq - 3) & 3]
        corner = [jnp.zeros((8, 128), F32) for _ in range(4)]
        for n in range(29):
            load = loader(north, True, n)
            g = [jnp.take_along_axis(load(j), index, axis=1) for j in order]
            for j in range(4):
                tile = jnp.where(near, g[j], g[(j + 1) % 4])
                put_b(j, n, tile)
                at = HEAD + (j % 2) * PART + 8 * n
                (low, high)[j // 2][at : at + 8, :] = tile
            below = jnp.where(rq == 0, 0.0, g[1])
            above = jnp.where(rq == 3, 0.0, g[3])
            fifth = jnp.where(lane8 < 64, jnp.where(near, g[0], below), jnp.where(near, above, g[0]))
            moved = pltpu.roll(fifth, (6 + 16 * (n % 8)) % 128, axis=1)
            corner[n // 8] = jnp.where(slot_lanes(lane8, n % 8), moved, corner[n // 8])
        for v in range(4):
            window[8 * v : 8 * v + 8, :] = corner[v]


def pack_corners(
    sc, from_west, from_east, window, a_in, b_in, low_in, high_in, sides, corner_a, corner_b, corner_low, corner_high
):
    lane = iota((ROWS, 128), 1)
    for s in range(SLABS):
        g, j = s // 16, s % 16
        east = pltpu.roll(from_east[g], (128 - 8 * j) % 128, axis=1)
        west = pltpu.roll(from_west[g], (122 - 8 * j) % 128, axis=1)
        sides[ROWS * s : ROWS * s + ROWS, :] = jnp.where(lane < 6, east, jnp.where(lane >= 122, west, 0.0))
    lane8 = iota((8, 128), 1)

    def build(dst, is_north, turn):
        corner = [window[8 * v : 8 * v + 8, :] if turn else jnp.zeros((8, 128), F32) for v in range(4)]
        if turn:
            rq, index, near = fold_lanes(sc, lane8)
            low = (lane8 < 64) & (rq == 0) & ~near
            high = (lane8 >= 64) & (rq == 3) & near
        for n in range(29):
            if n < 28:
                i, rt = n // 5, n % 5
                row = 31 - i if is_north else i
                fifth = sides[pl.ds(rt * 8 * ROWS + row, 8, stride=ROWS), :]
            else:
                mask = sides[40 * ROWS + (24 if is_north else 0) : 40 * ROWS + (32 if is_north else 8), :]
                fifth = jnp.concatenate([mask[7 - i : 8 - i] for i in range(8)], axis=0) if is_north else mask
            if turn:
                fifth = jnp.where(low | high, jnp.take_along_axis(fifth, index, axis=1), 0.0)
            moved = pltpu.roll(fifth, (6 + 16 * (n % 8)) % 128, axis=1)
            if turn:
                corner[n // 8] = corner[n // 8] + jnp.where(slot_lanes(lane8, n % 8), moved, 0.0)
            else:
                corner[n // 8] = jnp.where(slot_lanes(lane8, n % 8), moved, corner[n // 8])
        for v in range(4):
            dst[8 * v : 8 * v + 8, :] = corner[v]

    parity = sc[0] & 1

    @pl.when(parity == 0)
    def _():
        build(corner_a, True, False)
        build(corner_b, False, False)

    @pl.when(parity == 1)
    def _():
        build(corner_a, False, False)

    @pl.when((parity == 1) & (sc[0] < BLK - 1))
    def _():
        build(corner_b, True, False)

    @pl.when(sc[0] == BLK - 1)
    def _():
        build(corner_b, True, True)
        corner_low[...] = corner_b[...]
        corner_high[...] = corner_b[...]


GUARD = 8


def shifted_lanes(tiles, by, lane8):
    count = len(tiles)
    rolled = [pltpu.roll(t, (-by) % 128, axis=1) for t in tiles]
    if by > 0:
        return [jnp.where(lane8 >= 128 - by, rolled[(j + 1) % count], rolled[j]) for j in range(count)]
    return [jnp.where(lane8 < -by, rolled[(j - 1) % count], rolled[j]) for j in range(count)]


def place_ghost(load, corner, row_of, rows, old, q, v, u, taps, m, turned):
    lane8 = iota((8, 128), 1)
    edge_lanes = (lane8 < 6) | (lane8 >= 122)
    row8 = iota((8, 128), 0)
    for n in range(29):
        tiles = [load(j, n) for j in range(4)]
        fifth = pltpu.roll(corner(n // 8), (256 - 6 - 16 * (n % 8)) % 128, axis=1)
        tiles.append(jnp.where(edge_lanes, fifth, 0.0))
        if n == 28:
            for j in range(5):
                for i in range(6):
                    m[pl.ds(GUARD + j * rows + row_of(i), 1), :] = tiles[j][i : i + 1]
            continue
        i, rt = n // 5, n % 5
        for j in range(5):
            tile = tiles[j]
            if turned and rt in (2, 3):
                tile = -tile
            if turned and rt == 4:
                tile = jnp.where(row8 < 4, 8.0 - tile, tile)
            if rt < 2:
                ref, block = q, j * 16 + 8 * rt
                at = old + GUARD + block * rows + row_of(i)
            else:
                ref = (v, u, taps)[rt - 2]
                at = GUARD + j * 8 * rows + row_of(i)
            ref[pl.ds(at, 8, stride=rows), :] = tile


def own_rows(st, vn, ve, cd, wt, mk, sides, count, rows, at, side_row, q, v, u, taps, m):
    def put(ref, block, value):
        ref[pl.ds(GUARD + block * rows + at, count), :] = value

    def side(s):
        return sides[pl.ds(ROWS * s + side_row, count), :]

    for j in range(5):
        cols = slice(128 * j, 128 * j + 128)
        for t in range(2):
            for k in range(LEVELS):
                s = 8 * t + k
                put(q, j * 16 + s, st[t, k, :, cols] if j < 4 else side(s))
        for k in range(LEVELS):
            put(v, j * 8 + k, vn[k, :, cols] if j < 4 else side(16 + k))
            put(u, j * 8 + k, ve[k, :, cols] if j < 4 else side(24 + k))
        for k in range(4):
            put(taps, j * 8 + k, cd[k, :, cols].astype(F32) if j < 4 else side(32 + k))
            put(taps, j * 8 + 4 + k, wt[k, :, cols] if j < 4 else side(36 + k))
        put(m, j, mk[:, cols].astype(F32) if j < 4 else side(40))


def clear_rows(ref, blocks, rows, at, base=0):
    for b in range(blocks):
        ref[pl.ds(base + GUARD + b * rows + at, 8), :] = jnp.zeros((8, 128), F32)


def weights(is_fold, rows, first, low, count, doubled, v, u, taps, m, coef, force, ce, cw, cn, cs, cc):
    lane8 = iota((8, 128), 1)
    row8 = iota((8, 128), 0)

    def one(n):
        r = 8 * (low + n)
        ext_row = row8 + (first + r)

        def read(ref, block, shift=0):
            return ref[pl.ds(GUARD + block * rows + r + shift, 8), :]

        up_ok = jnp.where(is_fold & (ext_row >= 38) & (ext_row < 40), 0.0, 1.0)
        down_ok = jnp.where(is_fold & (ext_row >= 40) & (ext_row < 42), 0.0, 1.0)
        for j in range(5):
            w = [read(taps, 8 * j + 4 + t) for t in range(4)]
            c = [read(taps, 8 * j + t) for t in range(4)]
            wsum = w[0] + w[1] + w[2] + w[3]
            inv = 1.0 / jnp.where(wsum > 0.0, wsum, 1.0)
            w = [x * inv for x in w]
            for code in range(9):
                hit = [jnp.where(c[t] == float(code), w[t], 0.0) for t in range(4)]
                total = (hit[0] + hit[1]) + (hit[2] + hit[3])
                if code < 3:
                    total = total * down_ok
                if code >= 6:
                    total = total * up_ok
                coef[8 * (5 * code + j) : 8 * (5 * code + j) + 8, :] = total
        fields = []
        for f in range(5):
            total = None
            for dy in (-1, 0, 1):
                at = [GUARD + (5 * f + j) * 48 + first + r + 2 * dy for j in range(5)]
                grid = [doubled[pl.ds(a, 8), :] for a in at]
                for dx in (-1, 0, 1):
                    code = 3 * (dy + 1) + dx + 1
                    moved = grid if dx == 0 else shifted_lanes(grid, 2 * dx, lane8)
                    part = [
                        moved[j] * coef[8 * (5 * code + j) : 8 * (5 * code + j) + 8, :] for j in range(5)
                    ]
                    total = part if total is None else [a + b for a, b in zip(total, part)]
            fields.append(total)
        mc = [read(m, j) for j in range(5)]
        me, mw = shifted_lanes(mc, 1, lane8), shifted_lanes(mc, -1, lane8)
        oe = [mc[j] * me[j] for j in range(5)]
        ow = [mc[j] * mw[j] for j in range(5)]
        on = [mc[j] * read(m, j, 1) for j in range(5)]
        os = [mc[j] * read(m, j, -1) for j in range(5)]

        def put(ref, block, value):
            ref[pl.ds(GUARD + block * rows + r, 8), :] = value

        top, mid = [], []
        for j in range(5):
            sw, heat, fresh, tx, ty = (fields[f][j] for f in range(5))
            kv = 0.05 + 0.04 * jnp.sqrt(tx * tx + ty * ty + 0.01)
            top.append(mc[j] * kv)
            mid.append(0.05 * mc[j])
            put(force, j, 0.05 * mc[j] * sw)
            put(force, 5 + j, 0.05 * mc[j] * heat)
            put(force, 10 + j, -0.05 * mc[j] * fresh)
            put(force, 15 + j, top[j])
            put(force, 20 + j, mid[j])
        over = is_fold & (ext_row >= 40)
        for k in range(LEVELS):
            uc = [read(u, 8 * j + k) for j in range(5)]
            east, west = shifted_lanes(uc, 1, lane8), shifted_lanes(uc, -1, lane8)
            for j in range(5):
                vc = read(v, 8 * j + k)
                vt = jnp.where(over, read(v, 8 * j + k, 1), vc)
                vb = jnp.where(over, vc, read(v, 8 * j + k, -1))
                et = jnp.where(over, east[j], uc[j])
                wt = jnp.where(over, uc[j], west[j])
                put(ce, 8 * j + k, oe[j] * (0.08 - jnp.minimum(et, 0.0)))
                put(cw, 8 * j + k, ow[j] * (0.08 + jnp.maximum(wt, 0.0)))
                put(cn, 8 * j + k, on[j] * (0.08 - jnp.minimum(vt, 0.0)))
                put(cs, 8 * j + k, os[j] * (0.08 + jnp.maximum(vb, 0.0)))
                centre = 1.0 - oe[j] * (0.08 + jnp.maximum(et, 0.0)) - ow[j] * (0.08 - jnp.minimum(wt, 0.0))
                centre = centre - on[j] * (0.08 + jnp.maximum(vt, 0.0)) - os[j] * (0.08 - jnp.minimum(vb, 0.0))
                if k == 0:
                    centre = centre - top[j]
                elif k == 1:
                    centre = centre - top[j] - mid[j]
                elif k == LEVELS - 1:
                    centre = centre - mid[j]
                else:
                    centre = centre - 2.0 * mid[j]
                put(cc, 8 * j + k, centre)

    for n in range(count):
        one(n)


def steps(rows, qa, qb, force, ce, cw, cn, cs, cc):
    lane8 = iota((8, 128), 1)

    def one(q, p, r, width):
        def read(ref, block, shift=0):
            at = GUARD + block * rows + r + shift
            return ref[at : at + 8, :]

        def state(t, k, j, shift=0):
            return read(q, 16 * j + 8 * t + k, shift)

        mid = [read(force, 20 + j) for j in range(width)]
        here = [[state(t, 0, j) for j in range(5)] for t in range(2)]
        below = [None, None]
        for k in range(LEVELS):
            weight = [[read(ref, 8 * j + k) for j in range(width)] for ref in (cc, ce, cw, cn, cs)]
            for t in range(2):
                above = here[t]
                after = [state(t, k + 1, j) for j in range(5)] if k < LEVELS - 1 else None
                east, west = shifted_lanes(above, 1, lane8), shifted_lanes(above, -1, lane8)
                for j in range(width):
                    total = weight[0][j] * above[j] + weight[1][j] * east[j]
                    total = total + weight[2][j] * west[j]
                    total = total + weight[3][j] * state(t, k, j, 1)
                    total = total + weight[4][j] * state(t, k, j, -1)
                    if k == 0:
                        total = total + read(force, 15 + j) * after[j]
                    elif k == 1:
                        total = total + read(force, 15 + j) * below[t][j] + mid[j] * after[j]
                    elif k == LEVELS - 1:
                        total = total + mid[j] * below[t][j]
                    else:
                        total = total + mid[j] * (below[t][j] + after[j])
                    if t == 0:
                        total = total + (0.5 ** (k + 1)) * read(force, j)
                        if k == 0:
                            total = total + read(force, 5 + j)
                    elif k == 0:
                        total = total + read(force, 10 + j)
                    at = GUARD + (16 * j + 8 * t + k) * rows + r
                    p[at : at + 8, :] = total
                below[t], here[t] = above, after

    def step(q, p, last=False):
        for n in range(1, 5) if last else range(6):
            one(q, p, 8 * n, 4 if last else 5)

    def two(i, carry):
        step(qa, qb)
        step(qb, qa)
        return carry

    lax.fori_loop(0, STEPS // 2 - 1, two, 0)
    step(qa, qb)
    step(qb, qa, True)


def skin_rows(q, m, rows, at, count, pairs):
    sums = []
    table = (iota((COLS, COLS // 2), 0) // 2 == iota((COLS, COLS // 2), 1)).astype(F32)
    for with_heat in (True, False):
        parts = []
        for j in range(4):
            value = m[GUARD + j * rows + at : GUARD + j * rows + at + count, :]
            if with_heat:
                value = value * q[GUARD + 16 * j * rows + at : GUARD + 16 * j * rows + at + count, :]
            pairs[0:count, :] = value
            parts.append(
                pairs[pl.ds(0, count // 2, stride=2), :] + pairs[pl.ds(1, count // 2, stride=2), :]
            )
        narrow = jnp.concatenate(parts, axis=1)
        sums.append(jnp.dot(narrow, table, precision=lax.Precision.HIGHEST, preferred_element_type=F32))
    return sums[0] / jnp.maximum(sums[1], 1.0)


def clear_guards(refs):
    for ref in refs:
        ref[0:GUARD, :] = jnp.zeros((GUARD, 128), F32)
        ref[ref.shape[0] - GUARD :, :] = jnp.zeros((GUARD, 128), F32)


def interval(
    sc, st, vn, ve, cd, wt, mk, sides, got_a, got_b, major, minor, atm, out, sst,
    qa, qb, v, u, taps, m, atm_rows, grids, coef, force, ce, cw, cn, cs, cc, pairs,
):
    rows = EXT_ROWS
    lane8 = iota((8, 128), 1)
    is_fold = sc[0] == BLK - 1
    odd = sc[0] & 1
    clear_guards((qa, qb, v, u, taps, m, grids))
    for at in (0, 40):
        clear_rows(qa, 80, rows, at)
        clear_rows(v, 40, rows, at)
        clear_rows(u, 40, rows, at)
        clear_rows(taps, 40, rows, at)
        clear_rows(m, 5, rows, at)
    own_rows(st, vn, ve, cd, wt, mk, sides, ROWS, rows, 8, 0, qa, v, u, taps, m)

    def to_north(i):
        return 40 + i

    def to_south(i):
        return 7 - i

    def plain(msg, row_of):
        place_ghost(
            lambda j, n: msg[HEAD + j * PART + 8 * n : HEAD + j * PART + 8 * n + 8, :],
            lambda g: msg[8 * g : 8 * g + 8, :],
            row_of, rows, 0, qa, v, u, taps, m, False,
        )

    @pl.when(odd == 0)
    def _():
        plain(got_a, to_north)
        plain(got_b, to_south)

    @pl.when(odd == 1)
    def _():
        plain(got_a, to_south)

    @pl.when((odd == 1) & jnp.logical_not(is_fold))
    def _():
        plain(got_b, to_north)

    def fold(first_is_major):
        seam = sc[3]

        def load(j, n):
            at = HEAD + j * PART + 8 * n
            value = major[at : at + 8, :]
            if first_is_major == (j >= 2):
                at = HEAD + (j % 2) * PART + 8 * n
                second = lane8 + 128 * j > seam
                value = jnp.where(second if first_is_major else ~second, minor[at : at + 8, :], value)
            return value

        def corner(g):
            at = slice(8 * g, 8 * g + 8)
            one, two = (major, minor) if first_is_major else (minor, major)
            return jnp.where((lane8 & 15) < 6, one[at, :], two[at, :])

        place_ghost(load, corner, to_north, rows, 0, qa, v, u, taps, m, True)

    @pl.when(is_fold & (sc[3] >= 256))
    def _():
        fold(True)

    @pl.when(is_fold & (sc[3] < 256))
    def _():
        fold(False)

    for f in range(5):
        for part in range(3):
            cols = slice(128 * part, 128 * part + 128)
            far = atm[pl.ds(16 + 3 * f + part, 16, stride=32), :]
            atm_rows[24 * f : 24 * f + 4, cols] = far[12:16]
            atm_rows[24 * f + 4 : 24 * f + 20, cols] = atm[pl.ds(3 * f + part, 16, stride=32), :]
            atm_rows[24 * f + 20 : 24 * f + 24, cols] = far[0:4]
    src = iota((384, EXT_COLS), 0)
    dst = iota((384, EXT_COLS), 1)
    table = (src == jnp.where(dst < 576, dst // 2, dst // 2 + 64)).astype(F32)
    wide = jnp.dot(atm_rows[...], table, precision=lax.Precision.HIGHEST, preferred_element_type=F32)
    for f in range(5):
        for j in range(5):
            tile = wide[24 * f : 24 * f + 24, 128 * j : 128 * j + 128]
            base = GUARD + (5 * f + j) * 48
            grids[pl.ds(base, 24, stride=2), :] = tile
            grids[pl.ds(base + 1, 24, stride=2), :] = tile
    weights(is_fold, rows, 0, 0, 6, grids, v, u, taps, m, coef, force, ce, cw, cn, cs, cc)
    steps(rows, qa, qb, force, ce, cw, cn, cs, cc)
    for t in range(2):
        for k in range(LEVELS):
            for j in range(4):
                base = GUARD + (16 * j + 8 * t + k) * rows + 8
                out[t, k, :, 128 * j : 128 * j + 128] = qa[base : base + ROWS, :]
    result = skin_rows(qa, m, rows, 8, ROWS, pairs)
    sst[:, 0, :] = result[:, 0:128]
    sst[:, 1, :] = result[:, 128:256]


def place(b, l):
    return b * LON + l % LON


def body(temp_salt, east_vel, north_vel, land_mask, fluxes, remap_code, remap_weight, fold_source):
    axes = ("blk", "lon")
    b, l = lax.axis_index("blk"), lax.axis_index("lon")
    mirror = lax.rem(fold_source[0] + COLS * l, NX)
    sc = jnp.stack([b, l, mirror // COLS, mirror % COLS, (mirror - 1) // 2]).astype(jnp.int32)
    arrays = (temp_salt, north_vel, east_vel, remap_code, remap_weight, land_mask)

    sds = lambda *shape: jax.ShapeDtypeStruct(shape, F32)
    band = pl.pallas_call(
        combine_bands,
        grid=(1,),
        in_specs=[full((10, 32, 128))],
        out_specs=full((5, 32, 128)),
        out_shape=sds(5, 32, 128),
        compiler_params=LIMIT,
        name="combine_bands",
    )(fluxes.reshape(10, 32, 128))
    band_pairs = []
    for n in range(4):
        for blk in range(BLK):
            if blk > 0:
                band_pairs.append((place(blk, n), place(blk - 1, n)))
            if blk < BLK - 1:
                band_pairs.append((place(blk, 12 + n), place(blk + 1, 12 + n)))
        band_pairs.append((place(BLK - 1, 15 - n), place(BLK - 1, n)))
    other = lax.ppermute(band, axes, band_pairs)

    first, _ = lax.optimization_barrier((land_mask, band))
    specs, operands = [], []
    for x in (*arrays[:-1], first):
        lead = x.shape[:-2]
        for j in (0, 3):
            specs.append(at_block(lead + (ROWS, 128), (0,) * len(lead) + (0, j)))
            operands.append(x)
    to_west, to_east = pl.pallas_call(
        pack_columns,
        grid=(1,),
        in_specs=specs,
        out_specs=[full((3, ROWS, 128))] * 2,
        out_shape=[sds(3, ROWS, 128)] * 2,
        compiler_params=LIMIT,
        name="pack_columns",
    )(*operands)
    from_west = lax.ppermute(to_east, "lon", [(i, (i + 1) % LON) for i in range(LON)])
    from_east = lax.ppermute(to_west, "lon", [((i + 1) % LON, i) for i in range(LON)])

    later, _ = lax.optimization_barrier((band, to_west))
    chunks = pl.pallas_call(
        chunk_bands,
        grid=(1,),
        in_specs=[SCALARS, full((5, 32, 128)), full((5, 32, 128))],
        out_specs=full((512, 128)),
        out_shape=sds(512, 128),
        scratch_shapes=[VMEM((160, 128), F32)] * 3,
        compiler_params=LIMIT,
        name="chunk_bands",
    )(sc, later, other)
    atm = lax.all_to_all(chunks, "lon", split_axis=0, concat_axis=0, tiled=True)

    later, _ = lax.optimization_barrier((sc, chunks))
    specs, operands = [SCALARS], [later]
    for x in arrays:
        lead = x.shape[:-2]
        for j in (0, 3):
            specs.append(at_block(lead + (8, COLS), (0,) * len(lead) + (j, 0)))
            operands.append(x)
    sizes = (WHOLE, WHOLE, HALF, HALF)
    *messages, window = pl.pallas_call(
        pack_rows,
        grid=(1,),
        in_specs=specs,
        out_specs=[full((n, 128)) for n in sizes] + [full((HEAD, 128))],
        out_shape=[sds(n, 128) for n in sizes] + [sds(HEAD, 128)],
        scratch_shapes=[VMEM((4 * SLABS * 8, 128), F32)] * 2,
        compiler_params=LIMIT,
        name="pack_rows",
    )(*operands)
    later, _ = lax.optimization_barrier((sc, atm))
    sides, msg_a, msg_b, low, high = pl.pallas_call(
        pack_corners,
        grid=(1,),
        in_specs=[SCALARS, full((3, ROWS, 128)), full((3, ROWS, 128)), full((HEAD, 128))]
        + [pl.BlockSpec(memory_space=pl.ANY)] * 4,
        out_specs=[full((SLABS * ROWS, 128))] + [full((HEAD, 128))] * 4,
        out_shape=[sds(SLABS * ROWS, 128)] + [sds(n, 128) for n in sizes],
        input_output_aliases={4: 1, 5: 2, 6: 3, 7: 4},
        compiler_params=LIMIT,
        name="pack_corners",
    )(later, from_west, from_east, window, *messages)

    on_chip = [(place(i, n), place(i ^ 1, n)) for i in range(BLK) for n in range(LON)]
    across = []
    for i in range(1, BLK - 1, 2):
        for n in range(LON):
            across += [(place(i, n), place(i + 1, n)), (place(i + 1, n), place(i, n))]
    got_a = lax.ppermute(msg_a, axes, on_chip)
    got_b = lax.ppermute(msg_b, axes, across)

    def branch(shift, second_half):
        top = BLK - 1
        one = [(place(top, n), place(top, (shift - n) % LON)) for n in range(LON)]
        two = [(place(top, n), place(top, (shift - 1 - n) % LON)) for n in range(LON)]

        def send(whole, low, high):
            if second_half:
                return lax.ppermute(whole, axes, one), lax.ppermute(high, axes, two)
            return lax.ppermute(whole, axes, two), lax.ppermute(low, axes, one)

        return send

    got_f = lax.switch(
        sc[2] * 2 + sc[3] // 256,
        [branch(shift, half) for shift in range(LON) for half in range(2)],
        msg_b,
        low,
        high,
    )

    ext = lambda n: VMEM((GUARD * 2 + n * EXT_ROWS, 128), F32)
    state, skin = pl.pallas_call(
        interval,
        grid=(1,),
        in_specs=[SCALARS] + [full(x.shape) for x in (*arrays, sides, got_a, got_b, *got_f, atm)],
        out_specs=[full((2, LEVELS, ROWS, COLS)), full((LON, 2, 128))],
        out_shape=[sds(2, LEVELS, ROWS, COLS), sds(LON, 2, 128)],
        scratch_shapes=[ext(80), ext(80), ext(40), ext(40), ext(40), ext(5), VMEM((120, 384), F32), ext(25)]
        + [VMEM((360, 128), F32), ext(25)]
        + [ext(40)] * 5
        + [VMEM((ROWS, 128), F32)],
        compiler_params=LIMIT,
        name="interval",
    )(sc, *arrays, sides, got_a, got_b, *got_f, atm)
    bands = lax.all_to_all(skin, "lon", split_axis=0, concat_axis=0, tiled=True)
    return state, bands.reshape(1, LON * 256)


def solution(mesh):
    placed = (
        P(None, None, "blk", "lon"),
        P(None, "blk", "lon"),
        P(None, "blk", "lon"),
        P("blk", "lon"),
        P(None, ("blk", "lon"), None),
        P(None, "blk", "lon"),
        P(None, "blk", "lon"),
        P("lon"),
    )
    return jax.shard_map(
        body,
        mesh=mesh,
        in_specs=placed,
        out_specs=(P(None, None, "blk", "lon"), P(("blk", "lon"), None)),
        check_vma=False,
    )
```

```python
import jax
import jax.numpy as jnp
from jax import lax
from jax.experimental import pallas as pl
from jax.experimental.pallas import tpu as pltpu
from jax.sharding import PartitionSpec as P

STEPS = 6
F32 = jnp.float32
LEVELS = 8
BLK, LON = 8, 16
ROWS, COLS = 32, 512
EXT_ROWS, EXT_COLS = 48, 640
NX = 8192
SLABS = 41
PART = 232
HEAD = 32
WHOLE = HEAD + 4 * PART
HALF = HEAD + 2 * PART
VMEM = pltpu.VMEM
SMEM = pltpu.SMEM


def limit(mib):
    return pltpu.CompilerParams(vmem_limit_bytes=mib * 1024 * 1024)


RELAY = BLK - 2
SLOT = 48


def iota(shape, dim):
    return lax.broadcasted_iota(jnp.int32, shape, dim)


def full(shape):
    return pl.BlockSpec(shape, lambda i: (0,) * len(shape))


def at_block(shape, place):
    return pl.BlockSpec(shape, lambda i: place)


SCALARS = pl.BlockSpec(memory_space=SMEM)


def combine_bands(fold, flux, sc, band):
    l = lax.axis_index("lon")
    mirror = lax.rem(fold[0] + COLS * l, NX)
    sc[0] = lax.axis_index("blk")
    sc[1] = l
    sc[2] = mirror // COLS
    sc[3] = lax.rem(mirror, COLS)
    sc[4] = (mirror - 1) // 2
    sc[5] = mirror // 256
    sc[6] = 0
    sc[7] = 0
    band[0] = flux[0]
    band[1] = flux[1] + flux[2] + flux[3] - 0.33 * flux[5]
    band[2] = flux[4] + flux[5] + flux[6] + flux[7]
    band[3] = flux[8]
    band[4] = flux[9]


def pack_columns(st0, st3, vn0, vn3, ve0, ve3, cd0, cd3, wt0, wt3, mk0, mk3, to_west, to_east):
    lane = iota((ROWS, 128), 1)

    def pack(groups, shift, out):
        for g, tiles in enumerate(groups):
            acc = jnp.zeros((ROWS, 128), F32)
            for j, tile in enumerate(tiles):
                moved = pltpu.roll(tile().astype(F32), (8 * j + shift) % 128, axis=1)
                acc = jnp.where((lane >= 8 * j) & (lane < 8 * j + 8), moved, acc)
            out[g] = acc

    def groups(st, vn, ve, cd, wt, mk):
        first = [lambda t=t, k=k: st[t, k] for t in range(2) for k in range(LEVELS)]
        second = [lambda k=k: vn[k] for k in range(LEVELS)] + [lambda k=k: ve[k] for k in range(LEVELS)]
        third = [lambda k=k: cd[k] for k in range(4)] + [lambda k=k: wt[k] for k in range(4)] + [lambda: mk[...]]
        return [first, second, third]

    pack(groups(st0, vn0, ve0, cd0, wt0, mk0), 0, to_west)
    pack(groups(st3, vn3, ve3, cd3, wt3, mk3), 6, to_east)


def chunk_bands(sc, band, other, top, out, own, held, relayed, turned):
    own[...] = band[...].reshape(160, 128)
    held[...] = other[...].reshape(160, 128)
    relayed[...] = top[...].reshape(160, 128)
    is_relay = sc[0] == RELAY

    @pl.when(is_relay & (sc[1] < 4))
    def _():
        pole = sc[4]
        pq, pr = pole // 128, pole % 128
        lane8 = iota((8, 128), 1)
        index = (pr - lane8) & 127
        for n in range(20):
            turned[8 * n : 8 * n + 8, :] = jnp.take_along_axis(relayed[8 * n : 8 * n + 8, :], index, axis=1)
        lane1 = iota((1, 128), 1)

        def one(row, carry):
            near = (pq - row) & 31
            far = (pq - row - 1) & 31
            for f in range(5):
                a = turned[pl.ds(32 * f + near, 1), :]
                b = turned[pl.ds(32 * f + far, 1), :]
                held[pl.ds(32 * f + row, 1), :] = jnp.where(lane1 <= pr, a, b)
            return carry

        lax.fori_loop(0, 32, one, 0)

    lane = iota((16, 128), 1)
    for slot, src in enumerate((own, held, relayed)):
        for f in range(5):
            even = src[pl.ds(32 * f, 16, stride=2), :]
            odd = src[pl.ds(32 * f + 1, 16, stride=2), :]
            side = jnp.where(lane < 64, pltpu.roll(even, 15, axis=0), pltpu.roll(odd, 1, axis=0))
            for part, value in enumerate((even, odd, side)):
                out[pl.ds(16 * slot + 3 * f + part, 16, stride=SLOT), :] = value
        out[pl.ds(16 * slot + 15, 16, stride=SLOT), :] = jnp.zeros((16, 128), F32)


def slot_lanes(lane8, slot):
    return (lane8 >= 16 * slot) & (lane8 < 16 * slot + 12)


def fold_lanes(sc, lane8):
    rq, rr = sc[3] // 128, sc[3] % 128
    return rq, (rr - lane8) & 127, lane8 <= rr


def pack_rows(
    sc, st_s, st_n, vn_s, vn_n, ve_s, ve_n, cd_s, cd_n, wt_s, wt_n, mk_s, mk_n,
    msg_a, msg_b, low, high, window, south, north,
):
    lane8 = iota((8, 128), 1)

    def stage(dst, st, vn, ve, cd, wt):
        for j in range(4):
            cols = slice(128 * j, 128 * j + 128)

            def put(s, value):
                dst[(j * SLABS + s) * 8 : (j * SLABS + s) * 8 + 8, :] = value

            for k in range(LEVELS):
                put(k, st[0, k, :, cols])
                put(8 + k, st[1, k, :, cols])
                put(16 + k, vn[k, :, cols])
                put(24 + k, ve[k, :, cols])
            for k in range(4):
                put(32 + k, cd[k, :, cols].astype(F32))
                put(36 + k, wt[k, :, cols])

    stage(south, st_s, vn_s, ve_s, cd_s, wt_s)
    stage(north, st_n, vn_n, ve_n, cd_n, wt_n)
    for j in range(4):
        base = (j * SLABS + 40) * 8
        cols = slice(128 * j, 128 * j + 128)
        south[base : base + 8, :] = mk_s[:, cols].astype(F32)
        flipped = mk_n[:, cols].astype(F32)
        for i in range(8):
            north[base + i : base + i + 1, :] = flipped[7 - i : 8 - i]

    def loader(edge, is_north, n):
        if n == 28:
            return lambda j: edge[pl.ds((j * SLABS + 40) * 8, 8), :]
        i, rt = n // 5, n % 5
        row = 7 - i if is_north else i
        return lambda j: edge[pl.ds((j * SLABS + rt * 8) * 8 + row, 8, stride=8), :]

    def build(put, edge, is_north):
        for n in range(29):
            load = loader(edge, is_north, n)
            for j in range(4):
                put(j, n, load(j))

    def put_a(j, n, tile):
        at = HEAD + j * PART + 8 * n
        msg_a[at : at + 8, :] = tile

    def put_b(j, n, tile):
        at = HEAD + j * PART + 8 * n
        msg_b[at : at + 8, :] = tile

    parity = sc[0] & 1
    window[...] = jnp.zeros_like(window)

    @pl.when(parity == 0)
    def _():
        build(put_a, north, True)
        build(put_b, south, False)

    @pl.when(parity == 1)
    def _():
        build(put_a, south, False)

    @pl.when((parity == 1) & (sc[0] < BLK - 1))
    def _():
        build(put_b, north, True)

    @pl.when(sc[0] == BLK - 1)
    def _():
        rq, index, near = fold_lanes(sc, lane8)
        order = [rq, (rq - 1) & 3, (rq - 2) & 3, (rq - 3) & 3]
        corner = [jnp.zeros((8, 128), F32) for _ in range(4)]
        for n in range(29):
            load = loader(north, True, n)
            g = [jnp.take_along_axis(load(j), index, axis=1) for j in order]
            for j in range(4):
                tile = jnp.where(near, g[j], g[(j + 1) % 4])
                put_b(j, n, tile)
                at = HEAD + (j % 2) * PART + 8 * n
                (low, high)[j // 2][at : at + 8, :] = tile
            below = jnp.where(rq == 0, 0.0, g[1])
            above = jnp.where(rq == 3, 0.0, g[3])
            fifth = jnp.where(lane8 < 64, jnp.where(near, g[0], below), jnp.where(near, above, g[0]))
            moved = pltpu.roll(fifth, (6 + 16 * (n % 8)) % 128, axis=1)
            corner[n // 8] = jnp.where(slot_lanes(lane8, n % 8), moved, corner[n // 8])
        for v in range(4):
            window[8 * v : 8 * v + 8, :] = corner[v]


def pack_corners(
    sc, from_west, from_east, window, a_in, b_in, low_in, high_in, sides, corner_a, corner_b, corner_low, corner_high
):
    lane = iota((ROWS, 128), 1)
    for s in range(SLABS):
        g, j = s // 16, s % 16
        east = pltpu.roll(from_east[g], (128 - 8 * j) % 128, axis=1)
        west = pltpu.roll(from_west[g], (122 - 8 * j) % 128, axis=1)
        sides[ROWS * s : ROWS * s + ROWS, :] = jnp.where(lane < 6, east, jnp.where(lane >= 122, west, 0.0))
    lane8 = iota((8, 128), 1)

    def build(dst, is_north, turn):
        corner = [window[8 * v : 8 * v + 8, :] if turn else jnp.zeros((8, 128), F32) for v in range(4)]
        if turn:
            rq, index, near = fold_lanes(sc, lane8)
            low = (lane8 < 64) & (rq == 0) & ~near
            high = (lane8 >= 64) & (rq == 3) & near
        for n in range(29):
            if n < 28:
                i, rt = n // 5, n % 5
                row = 31 - i if is_north else i
                fifth = sides[pl.ds(rt * 8 * ROWS + row, 8, stride=ROWS), :]
            else:
                mask = sides[40 * ROWS + (24 if is_north else 0) : 40 * ROWS + (32 if is_north else 8), :]
                fifth = jnp.concatenate([mask[7 - i : 8 - i] for i in range(8)], axis=0) if is_north else mask
            if turn:
                fifth = jnp.where(low | high, jnp.take_along_axis(fifth, index, axis=1), 0.0)
            moved = pltpu.roll(fifth, (6 + 16 * (n % 8)) % 128, axis=1)
            if turn:
                corner[n // 8] = corner[n // 8] + jnp.where(slot_lanes(lane8, n % 8), moved, 0.0)
            else:
                corner[n // 8] = jnp.where(slot_lanes(lane8, n % 8), moved, corner[n // 8])
        for v in range(4):
            dst[8 * v : 8 * v + 8, :] = corner[v]

    parity = sc[0] & 1

    @pl.when(parity == 0)
    def _():
        build(corner_a, True, False)
        build(corner_b, False, False)

    @pl.when(parity == 1)
    def _():
        build(corner_a, False, False)

    @pl.when((parity == 1) & (sc[0] < BLK - 1))
    def _():
        build(corner_b, True, False)

    @pl.when(sc[0] == BLK - 1)
    def _():
        build(corner_b, True, True)
        corner_low[...] = corner_b[...]
        corner_high[...] = corner_b[...]


GUARD = 8


def shifted_lanes(tiles, by, lane8):
    count = len(tiles)
    rolled = [pltpu.roll(t, (-by) % 128, axis=1) for t in tiles]
    if by > 0:
        return [jnp.where(lane8 >= 128 - by, rolled[(j + 1) % count], rolled[j]) for j in range(count)]
    return [jnp.where(lane8 < -by, rolled[(j - 1) % count], rolled[j]) for j in range(count)]


def place_ghost(load, corner, row_of, rows, old, q, v, u, taps, m, turned):
    lane8 = iota((8, 128), 1)
    edge_lanes = (lane8 < 6) | (lane8 >= 122)
    row8 = iota((8, 128), 0)
    for n in range(29):
        tiles = [load(j, n) for j in range(4)]
        fifth = pltpu.roll(corner(n // 8), (256 - 6 - 16 * (n % 8)) % 128, axis=1)
        tiles.append(jnp.where(edge_lanes, fifth, 0.0))
        if n == 28:
            for j in range(5):
                for i in range(6):
                    m[pl.ds(GUARD + j * rows + row_of(i), 1), :] = tiles[j][i : i + 1]
            continue
        i, rt = n // 5, n % 5
        for j in range(5):
            tile = tiles[j]
            if turned and rt in (2, 3):
                tile = -tile
            if turned and rt == 4:
                tile = jnp.where(row8 < 4, 8.0 - tile, tile)
            if rt < 2:
                ref, block = q, j * 16 + 8 * rt
                at = old + GUARD + block * rows + row_of(i)
            else:
                ref = (v, u, taps)[rt - 2]
                at = GUARD + j * 8 * rows + row_of(i)
            ref[pl.ds(at, 8, stride=rows), :] = tile


def own_rows(st, vn, ve, cd, wt, mk, sides, count, rows, at, side_row, q, v, u, taps, m):
    def put(ref, block, value):
        ref[pl.ds(GUARD + block * rows + at, count), :] = value

    def side(s):
        return sides[pl.ds(ROWS * s + side_row, count), :]

    for j in range(5):
        cols = slice(128 * j, 128 * j + 128)
        for t in range(2):
            for k in range(LEVELS):
                s = 8 * t + k
                put(q, j * 16 + s, st[t, k, :, cols] if j < 4 else side(s))
        for k in range(LEVELS):
            put(v, j * 8 + k, vn[k, :, cols] if j < 4 else side(16 + k))
            put(u, j * 8 + k, ve[k, :, cols] if j < 4 else side(24 + k))
        for k in range(4):
            put(taps, j * 8 + k, cd[k, :, cols].astype(F32) if j < 4 else side(32 + k))
            put(taps, j * 8 + 4 + k, wt[k, :, cols] if j < 4 else side(36 + k))
        put(m, j, mk[:, cols].astype(F32) if j < 4 else side(40))


def clear_rows(ref, blocks, rows, at, base=0):
    for b in range(blocks):
        ref[pl.ds(base + GUARD + b * rows + at, 8), :] = jnp.zeros((8, 128), F32)


def weights(is_fold, rows, first, low, count, doubled, v, u, taps, m, coef, force, ce, cw, cn, cs, cc):
    lane8 = iota((8, 128), 1)
    row8 = iota((8, 128), 0)

    def one(n):
        r = 8 * (low + n)
        ext_row = row8 + (first + r)

        def read(ref, block, shift=0):
            return ref[pl.ds(GUARD + block * rows + r + shift, 8), :]

        up_ok = jnp.where(is_fold & (ext_row >= 38) & (ext_row < 40), 0.0, 1.0)
        down_ok = jnp.where(is_fold & (ext_row >= 40) & (ext_row < 42), 0.0, 1.0)
        for j in range(5):
            w = [read(taps, 8 * j + 4 + t) for t in range(4)]
            c = [read(taps, 8 * j + t) for t in range(4)]
            wsum = w[0] + w[1] + w[2] + w[3]
            inv = 1.0 / jnp.where(wsum > 0.0, wsum, 1.0)
            w = [x * inv for x in w]
            for code in range(9):
                hit = [jnp.where(c[t] == float(code), w[t], 0.0) for t in range(4)]
                total = (hit[0] + hit[1]) + (hit[2] + hit[3])
                if code < 3:
                    total = total * down_ok
                if code >= 6:
                    total = total * up_ok
                coef[8 * (5 * code + j) : 8 * (5 * code + j) + 8, :] = total
        fields = []
        for f in range(5):
            total = None
            for dy in (-1, 0, 1):
                at = [GUARD + (5 * f + j) * 48 + first + r + 2 * dy for j in range(5)]
                grid = [doubled[pl.ds(a, 8), :] for a in at]
                for dx in (-1, 0, 1):
                    code = 3 * (dy + 1) + dx + 1
                    moved = grid if dx == 0 else shifted_lanes(grid, 2 * dx, lane8)
                    part = [
                        moved[j] * coef[8 * (5 * code + j) : 8 * (5 * code + j) + 8, :] for j in range(5)
                    ]
                    total = part if total is None else [a + b for a, b in zip(total, part)]
            fields.append(total)
        mc = [read(m, j) for j in range(5)]
        me, mw = shifted_lanes(mc, 1, lane8), shifted_lanes(mc, -1, lane8)
        oe = [mc[j] * me[j] for j in range(5)]
        ow = [mc[j] * mw[j] for j in range(5)]
        on = [mc[j] * read(m, j, 1) for j in range(5)]
        os = [mc[j] * read(m, j, -1) for j in range(5)]

        def put(ref, block, value):
            ref[pl.ds(GUARD + block * rows + r, 8), :] = value

        top, mid = [], []
        for j in range(5):
            sw, heat, fresh, tx, ty = (fields[f][j] for f in range(5))
            kv = 0.05 + 0.04 * jnp.sqrt(tx * tx + ty * ty + 0.01)
            top.append(mc[j] * kv)
            mid.append(0.05 * mc[j])
            put(force, j, 0.05 * mc[j] * sw)
            put(force, 5 + j, 0.05 * mc[j] * heat)
            put(force, 10 + j, -0.05 * mc[j] * fresh)
            put(force, 15 + j, top[j])
            put(force, 20 + j, mid[j])
        over = is_fold & (ext_row >= 40)
        for k in range(LEVELS):
            uc = [read(u, 8 * j + k) for j in range(5)]
            east, west = shifted_lanes(uc, 1, lane8), shifted_lanes(uc, -1, lane8)
            for j in range(5):
                vc = read(v, 8 * j + k)
                vt = jnp.where(over, read(v, 8 * j + k, 1), vc)
                vb = jnp.where(over, vc, read(v, 8 * j + k, -1))
                et = jnp.where(over, east[j], uc[j])
                wt = jnp.where(over, uc[j], west[j])
                put(ce, 8 * j + k, oe[j] * (0.08 - jnp.minimum(et, 0.0)))
                put(cw, 8 * j + k, ow[j] * (0.08 + jnp.maximum(wt, 0.0)))
                put(cn, 8 * j + k, on[j] * (0.08 - jnp.minimum(vt, 0.0)))
                put(cs, 8 * j + k, os[j] * (0.08 + jnp.maximum(vb, 0.0)))
                centre = 1.0 - oe[j] * (0.08 + jnp.maximum(et, 0.0)) - ow[j] * (0.08 - jnp.minimum(wt, 0.0))
                centre = centre - on[j] * (0.08 + jnp.maximum(vt, 0.0)) - os[j] * (0.08 - jnp.minimum(vb, 0.0))
                if k == 0:
                    centre = centre - top[j]
                elif k == 1:
                    centre = centre - top[j] - mid[j]
                elif k == LEVELS - 1:
                    centre = centre - mid[j]
                else:
                    centre = centre - 2.0 * mid[j]
                put(cc, 8 * j + k, centre)

    for n in range(count):
        one(n)


def steps(rows, qa, qb, force, ce, cw, cn, cs, cc):
    lane8 = iota((8, 128), 1)

    def one(q, p, r, width):
        def read(ref, block, shift=0):
            at = GUARD + block * rows + r + shift
            return ref[at : at + 8, :]

        def state(t, k, j, shift=0):
            return read(q, 16 * j + 8 * t + k, shift)

        mid = [read(force, 20 + j) for j in range(width)]
        here = [[state(t, 0, j) for j in range(5)] for t in range(2)]
        below = [None, None]
        for k in range(LEVELS):
            weight = [[read(ref, 8 * j + k) for j in range(width)] for ref in (cc, ce, cw, cn, cs)]
            for t in range(2):
                above = here[t]
                after = [state(t, k + 1, j) for j in range(5)] if k < LEVELS - 1 else None
                east, west = shifted_lanes(above, 1, lane8), shifted_lanes(above, -1, lane8)
                for j in range(width):
                    total = weight[0][j] * above[j] + weight[1][j] * east[j]
                    total = total + weight[2][j] * west[j]
                    total = total + weight[3][j] * state(t, k, j, 1)
                    total = total + weight[4][j] * state(t, k, j, -1)
                    if k == 0:
                        total = total + read(force, 15 + j) * after[j]
                    elif k == 1:
                        total = total + read(force, 15 + j) * below[t][j] + mid[j] * after[j]
                    elif k == LEVELS - 1:
                        total = total + mid[j] * below[t][j]
                    else:
                        total = total + mid[j] * (below[t][j] + after[j])
                    if t == 0:
                        total = total + (0.5 ** (k + 1)) * read(force, j)
                        if k == 0:
                            total = total + read(force, 5 + j)
                    elif k == 0:
                        total = total + read(force, 10 + j)
                    at = GUARD + (16 * j + 8 * t + k) * rows + r
                    p[at : at + 8, :] = total
                below[t], here[t] = above, after

    def step(q, p, last=False):
        for n in range(1, 5) if last else range(6):
            one(q, p, 8 * n, 4 if last else 5)

    def two(i, carry):
        step(qa, qb)
        step(qb, qa)
        return carry

    lax.fori_loop(0, STEPS // 2 - 1, two, 0)
    step(qa, qb)
    step(qb, qa, True)


def skin_rows(q, m, rows, at, count, pairs):
    sums = []
    table = (iota((COLS, COLS // 2), 0) // 2 == iota((COLS, COLS // 2), 1)).astype(F32)
    for with_heat in (True, False):
        parts = []
        for j in range(4):
            value = m[GUARD + j * rows + at : GUARD + j * rows + at + count, :]
            if with_heat:
                value = value * q[GUARD + 16 * j * rows + at : GUARD + 16 * j * rows + at + count, :]
            pairs[0:count, :] = value
            parts.append(
                pairs[pl.ds(0, count // 2, stride=2), :] + pairs[pl.ds(1, count // 2, stride=2), :]
            )
        narrow = jnp.concatenate(parts, axis=1)
        sums.append(jnp.dot(narrow, table, precision=lax.Precision.HIGHEST, preferred_element_type=F32))
    return sums[0] / jnp.maximum(sums[1], 1.0)


def clear_guards(refs):
    for ref in refs:
        ref[0:GUARD, :] = jnp.zeros((GUARD, 128), F32)
        ref[ref.shape[0] - GUARD :, :] = jnp.zeros((GUARD, 128), F32)


def interval(
    sc, st, vn, ve, cd, wt, mk, sides, got_a, got_b, major, minor, atm, atm_top, out, sst,
    qa, qb, v, u, taps, m, atm_rows, grids, coef, force, ce, cw, cn, cs, cc, pairs,
):
    rows = EXT_ROWS
    lane8 = iota((8, 128), 1)
    is_fold = sc[0] == BLK - 1
    odd = sc[0] & 1
    clear_guards((qa, qb, v, u, taps, m, grids))
    for at in (0, 40):
        clear_rows(qa, 80, rows, at)
        clear_rows(v, 40, rows, at)
        clear_rows(u, 40, rows, at)
        clear_rows(taps, 40, rows, at)
        clear_rows(m, 5, rows, at)
    own_rows(st, vn, ve, cd, wt, mk, sides, ROWS, rows, 8, 0, qa, v, u, taps, m)

    def to_north(i):
        return 40 + i

    def to_south(i):
        return 7 - i

    def plain(msg, row_of):
        place_ghost(
            lambda j, n: msg[HEAD + j * PART + 8 * n : HEAD + j * PART + 8 * n + 8, :],
            lambda g: msg[8 * g : 8 * g + 8, :],
            row_of, rows, 0, qa, v, u, taps, m, False,
        )

    @pl.when(odd == 0)
    def _():
        plain(got_a, to_north)
        plain(got_b, to_south)

    @pl.when(odd == 1)
    def _():
        plain(got_a, to_south)

    @pl.when((odd == 1) & jnp.logical_not(is_fold))
    def _():
        plain(got_b, to_north)

    def fold(first_is_major):
        seam = sc[3]

        def load(j, n):
            at = HEAD + j * PART + 8 * n
            value = major[at : at + 8, :]
            if first_is_major == (j >= 2):
                at = HEAD + (j % 2) * PART + 8 * n
                second = lane8 + 128 * j > seam
                value = jnp.where(second if first_is_major else ~second, minor[at : at + 8, :], value)
            return value

        def corner(g):
            at = slice(8 * g, 8 * g + 8)
            one, two = (major, minor) if first_is_major else (minor, major)
            return jnp.where((lane8 & 15) < 6, one[at, :], two[at, :])

        place_ghost(load, corner, to_north, rows, 0, qa, v, u, taps, m, True)

    @pl.when(is_fold & (sc[3] >= 256))
    def _():
        fold(True)

    @pl.when(is_fold & (sc[3] < 256))
    def _():
        fold(False)

    def each(put):
        for f in range(5):
            for part in range(3):
                put(24 * f, slice(128 * part, 128 * part + 128), 3 * f + part)

    @pl.when(jnp.logical_not(is_fold))
    def _():
        def put(at, cols, row):
            far = atm[pl.ds(16 + row, 16, stride=SLOT), :]
            atm_rows[at : at + 4, cols] = far[12:16]
            atm_rows[at + 4 : at + 20, cols] = atm[pl.ds(row, 16, stride=SLOT), :]
            atm_rows[at + 20 : at + 24, cols] = far[0:4]

        each(put)

    @pl.when(sc[0] == RELAY)
    def _():
        def put(at, cols, row):
            for i in range(4):
                source = (15 - i) * SLOT + 32 + row
                atm_rows[at + 20 + i : at + 21 + i, cols] = atm[source : source + 1, :]

        each(put)

    @pl.when(is_fold)
    def _():
        def put(at, cols, row):
            atm_rows[at : at + 4, cols] = atm_top[pl.ds(row, 16, stride=SLOT), :][12:16]
            for i in range(16):
                source = (15 - i) * SLOT + 32 + row
                atm_rows[at + 4 + i : at + 5 + i, cols] = atm_top[source : source + 1, :]
            atm_rows[at + 20 : at + 24, cols] = atm_top[pl.ds(16 + row, 16, stride=SLOT), :][0:4]

        each(put)

    src = iota((384, EXT_COLS), 0)
    dst = iota((384, EXT_COLS), 1)
    table = (src == jnp.where(dst < 576, dst // 2, dst // 2 + 64)).astype(F32)
    wide = jnp.dot(atm_rows[...], table, precision=lax.Precision.HIGHEST, preferred_element_type=F32)
    for f in range(5):
        for j in range(5):
            tile = wide[24 * f : 24 * f + 24, 128 * j : 128 * j + 128]
            base = GUARD + (5 * f + j) * 48
            grids[pl.ds(base, 24, stride=2), :] = tile
            grids[pl.ds(base + 1, 24, stride=2), :] = tile
    weights(is_fold, rows, 0, 0, 6, grids, v, u, taps, m, coef, force, ce, cw, cn, cs, cc)
    steps(rows, qa, qb, force, ce, cw, cn, cs, cc)
    for t in range(2):
        for k in range(LEVELS):
            for j in range(4):
                base = GUARD + (16 * j + 8 * t + k) * rows + 8
                out[t, k, :, 128 * j : 128 * j + 128] = qa[base : base + ROWS, :]
    result = skin_rows(qa, m, rows, 8, ROWS, pairs)
    sst[:, 0, :] = result[:, 0:128]
    sst[:, 1, :] = result[:, 128:256]


def place(b, l):
    return b * LON + l % LON


def body(temp_salt, east_vel, north_vel, land_mask, fluxes, remap_code, remap_weight, fold_source):
    axes = ("blk", "lon")
    arrays = (temp_salt, north_vel, east_vel, remap_code, remap_weight, land_mask)

    sds = lambda *shape: jax.ShapeDtypeStruct(shape, F32)
    sc, band = pl.pallas_call(
        combine_bands,
        grid=(1,),
        in_specs=[SCALARS, full((10, 32, 128))],
        out_specs=[SCALARS, full((5, 32, 128))],
        out_shape=[jax.ShapeDtypeStruct((8,), jnp.int32), sds(5, 32, 128)],
        compiler_params=limit(56),
        name="combine_bands",
    )(fold_source, fluxes.reshape(10, 32, 128))
    band_pairs = []
    for n in range(4):
        for blk in range(RELAY):
            band_pairs.append((place(blk + 1, n), place(blk, n)))
            band_pairs.append((place(blk, 12 + n), place(blk + 1, 12 + n)))
    other = lax.ppermute(band, axes, band_pairs)
    top = lax.ppermute(band, axes, [(place(BLK - 1, n), place(RELAY, 15 - n)) for n in range(LON)])

    first, _ = lax.optimization_barrier((land_mask, band))
    specs, operands = [], []
    for x in (*arrays[:-1], first):
        lead = x.shape[:-2]
        for j in (0, 3):
            specs.append(at_block(lead + (ROWS, 128), (0,) * len(lead) + (0, j)))
            operands.append(x)
    to_west, to_east = pl.pallas_call(
        pack_columns,
        grid=(1,),
        in_specs=specs,
        out_specs=[full((3, ROWS, 128))] * 2,
        out_shape=[sds(3, ROWS, 128)] * 2,
        compiler_params=limit(56),
        name="pack_columns",
    )(*operands)
    from_west = lax.ppermute(to_east, "lon", [(i, (i + 1) % LON) for i in range(LON)])
    from_east = lax.ppermute(to_west, "lon", [((i + 1) % LON, i) for i in range(LON)])

    first, _, other, top = lax.optimization_barrier((land_mask, to_west, other, top))
    specs, operands = [SCALARS], [sc]
    for x in (*arrays[:-1], first):
        lead = x.shape[:-2]
        for j in (0, 3):
            specs.append(at_block(lead + (8, COLS), (0,) * len(lead) + (j, 0)))
            operands.append(x)
    sizes = (WHOLE, WHOLE, HALF, HALF)
    *messages, window = pl.pallas_call(
        pack_rows,
        grid=(1,),
        in_specs=specs,
        out_specs=[full((n, 128)) for n in sizes] + [full((HEAD, 128))],
        out_shape=[sds(n, 128) for n in sizes] + [sds(HEAD, 128)],
        scratch_shapes=[VMEM((4 * SLABS * 8, 128), F32)] * 2,
        compiler_params=limit(56),
        name="pack_rows",
    )(*operands)
    sides, msg_a, msg_b, low, high = pl.pallas_call(
        pack_corners,
        grid=(1,),
        in_specs=[SCALARS, full((3, ROWS, 128)), full((3, ROWS, 128)), full((HEAD, 128))]
        + [pl.BlockSpec(memory_space=pl.ANY)] * 4,
        out_specs=[full((SLABS * ROWS, 128))] + [full((HEAD, 128))] * 4,
        out_shape=[sds(SLABS * ROWS, 128)] + [sds(n, 128) for n in sizes],
        input_output_aliases={4: 1, 5: 2, 6: 3, 7: 4},
        compiler_params=limit(56),
        name="pack_corners",
    )(sc, from_west, from_east, window, *messages)

    on_chip = [(place(i, n), place(i ^ 1, n)) for i in range(BLK) for n in range(LON)]
    across = []
    for i in range(1, BLK - 1, 2):
        for n in range(LON):
            across += [(place(i, n), place(i + 1, n)), (place(i + 1, n), place(i, n))]
    got_a = lax.ppermute(msg_a, axes, on_chip)
    got_b = lax.ppermute(msg_b, axes, across)

    def spread(band, other, top):
        chunks = pl.pallas_call(
            chunk_bands,
            grid=(1,),
            in_specs=[SCALARS] + [full((5, 32, 128))] * 3,
            out_specs=full((LON * SLOT, 128)),
            out_shape=sds(LON * SLOT, 128),
            scratch_shapes=[VMEM((160, 128), F32)] * 4,
            compiler_params=limit(8),
            name="chunk_bands",
        )(sc, band, other, top)
        return lax.all_to_all(chunks, "lon", split_axis=0, concat_axis=0, tiled=True)

    later, _ = lax.optimization_barrier((band, msg_a))
    atm = lax.cond(
        lax.axis_index("blk") == BLK - 1, lambda *x: jnp.zeros((LON * SLOT, 128), F32), spread, later, other, top
    )
    atm_top = lax.ppermute(atm, axes, [(place(RELAY, n), place(BLK - 1, n)) for n in range(LON)])

    def branch(shift, second_half):
        top = BLK - 1
        one = [(place(top, n), place(top, (shift - n) % LON)) for n in range(LON)]
        two = [(place(top, n), place(top, (shift - 1 - n) % LON)) for n in range(LON)]

        def send(whole, low, high):
            if second_half:
                return lax.ppermute(whole, axes, one), lax.ppermute(high, axes, two)
            return lax.ppermute(whole, axes, two), lax.ppermute(low, axes, one)

        return send

    whole_b, _ = lax.optimization_barrier((msg_b, atm))
    got_f = lax.switch(
        sc[5],
        [branch(shift, half) for shift in range(LON) for half in range(2)],
        whole_b,
        low,
        high,
    )

    ext = lambda n: VMEM((GUARD * 2 + n * EXT_ROWS, 128), F32)
    state, skin = pl.pallas_call(
        interval,
        grid=(1,),
        in_specs=[SCALARS] + [full(x.shape) for x in (*arrays, sides, got_a, got_b, *got_f, atm, atm_top)],
        out_specs=[full((2, LEVELS, ROWS, COLS)), full((LON, 2, 128))],
        out_shape=[sds(2, LEVELS, ROWS, COLS), sds(LON, 2, 128)],
        scratch_shapes=[ext(80), ext(80), ext(40), ext(40), ext(40), ext(5), VMEM((120, 384), F32), ext(25)]
        + [VMEM((360, 128), F32), ext(25)]
        + [ext(40)] * 5
        + [VMEM((ROWS, 128), F32)],
        compiler_params=limit(36),
        name="interval",
    )(sc, *arrays, sides, got_a, got_b, *got_f, atm, atm_top)
    bands = lax.all_to_all(skin, "lon", split_axis=0, concat_axis=0, tiled=True)
    return state, bands.reshape(1, LON * 256)


def solution(mesh):
    placed = (
        P(None, None, "blk", "lon"),
        P(None, "blk", "lon"),
        P(None, "blk", "lon"),
        P("blk", "lon"),
        P(None, ("blk", "lon"), None),
        P(None, "blk", "lon"),
        P(None, "blk", "lon"),
        P("lon"),
    )
    return jax.shard_map(
        body,
        mesh=mesh,
        in_specs=placed,
        out_specs=(P(None, None, "blk", "lon"), P(("blk", "lon"), None)),
        check_vma=False,
    )
```

```python
import jax
import jax.numpy as jnp
from jax import lax
from jax.experimental import pallas as pl
from jax.experimental.pallas import tpu as pltpu
from jax.sharding import PartitionSpec as P

STEPS = 6
F32 = jnp.float32
LEVELS = 8
BLK, LON = 8, 16
ROWS, COLS = 32, 512
EXT_ROWS, EXT_COLS = 48, 640
NX = 8192
SLABS = 41
PART = 232
HEAD = 32
WHOLE = HEAD + 4 * PART
HALF = HEAD + 2 * PART
VMEM = pltpu.VMEM
SMEM = pltpu.SMEM


def limit(mib):
    return pltpu.CompilerParams(vmem_limit_bytes=mib * 1024 * 1024)


RELAY = BLK - 2
SLOT = 48


def iota(shape, dim):
    return lax.broadcasted_iota(jnp.int32, shape, dim)


def full(shape):
    return pl.BlockSpec(shape, lambda i: (0,) * len(shape))


def at_block(shape, place):
    return pl.BlockSpec(shape, lambda i: place)


SCALARS = pl.BlockSpec(memory_space=SMEM)


def combine_bands(fold, flux, sc, band):
    l = lax.axis_index("lon")
    mirror = lax.rem(fold[0] + COLS * l, NX)
    sc[0] = lax.axis_index("blk")
    sc[1] = l
    sc[2] = mirror // COLS
    sc[3] = lax.rem(mirror, COLS)
    sc[4] = (mirror - 1) // 2
    sc[5] = mirror // 256
    sc[6] = 0
    sc[7] = 0
    band[0] = flux[0]
    band[1] = flux[1] + flux[2] + flux[3] - 0.33 * flux[5]
    band[2] = flux[4] + flux[5] + flux[6] + flux[7]
    band[3] = flux[8]
    band[4] = flux[9]


def pack_columns(st0, st3, vn0, vn3, ve0, ve3, cd0, cd3, wt0, wt3, mk0, mk3, to_west, to_east):
    lane = iota((ROWS, 128), 1)

    def pack(groups, shift, out):
        for g, tiles in enumerate(groups):
            acc = jnp.zeros((ROWS, 128), F32)
            for j, tile in enumerate(tiles):
                moved = pltpu.roll(tile().astype(F32), (8 * j + shift) % 128, axis=1)
                acc = jnp.where((lane >= 8 * j) & (lane < 8 * j + 8), moved, acc)
            out[g] = acc

    def groups(st, vn, ve, cd, wt, mk):
        first = [lambda t=t, k=k: st[t, k] for t in range(2) for k in range(LEVELS)]
        second = [lambda k=k: vn[k] for k in range(LEVELS)] + [lambda k=k: ve[k] for k in range(LEVELS)]
        third = [lambda k=k: cd[k] for k in range(4)] + [lambda k=k: wt[k] for k in range(4)] + [lambda: mk[...]]
        return [first, second, third]

    pack(groups(st0, vn0, ve0, cd0, wt0, mk0), 0, to_west)
    pack(groups(st3, vn3, ve3, cd3, wt3, mk3), 6, to_east)


def chunk_bands(sc, band, other, top, out, own, held, relayed, turned):
    own[...] = band[...].reshape(160, 128)
    held[...] = other[...].reshape(160, 128)
    relayed[...] = top[...].reshape(160, 128)
    is_relay = sc[0] == RELAY

    @pl.when(is_relay & (sc[1] < 4))
    def _():
        pole = sc[4]
        pq, pr = pole // 128, pole % 128
        lane8 = iota((8, 128), 1)
        index = (pr - lane8) & 127
        for n in range(20):
            turned[8 * n : 8 * n + 8, :] = jnp.take_along_axis(held[8 * n : 8 * n + 8, :], index, axis=1)
        lane1 = iota((1, 128), 1)

        def one(row, carry):
            near = (pq - row) & 31
            far = (pq - row - 1) & 31
            for f in range(5):
                a = turned[pl.ds(32 * f + near, 1), :]
                b = turned[pl.ds(32 * f + far, 1), :]
                held[pl.ds(32 * f + row, 1), :] = jnp.where(lane1 <= pr, a, b)
            return carry

        lax.fori_loop(0, 32, one, 0)

    lane = iota((16, 128), 1)
    for slot, src in enumerate((own, held, relayed)):
        for f in range(5):
            even = src[pl.ds(32 * f, 16, stride=2), :]
            odd = src[pl.ds(32 * f + 1, 16, stride=2), :]
            side = jnp.where(lane < 64, pltpu.roll(even, 15, axis=0), pltpu.roll(odd, 1, axis=0))
            for part, value in enumerate((even, odd, side)):
                out[pl.ds(16 * slot + 3 * f + part, 16, stride=SLOT), :] = value
        out[pl.ds(16 * slot + 15, 16, stride=SLOT), :] = jnp.zeros((16, 128), F32)


def slot_lanes(lane8, slot):
    return (lane8 >= 16 * slot) & (lane8 < 16 * slot + 12)


def fold_lanes(sc, lane8):
    rq, rr = sc[3] // 128, sc[3] % 128
    return rq, (rr - lane8) & 127, lane8 <= rr


def pack_rows(
    sc, st_s, st_n, vn_s, vn_n, ve_s, ve_n, cd_s, cd_n, wt_s, wt_n, mk_s, mk_n,
    msg_a, msg_b, low, high, window, south, north,
):
    lane8 = iota((8, 128), 1)

    def stage(dst, st, vn, ve, cd, wt):
        for j in range(4):
            cols = slice(128 * j, 128 * j + 128)

            def put(s, value):
                dst[(j * SLABS + s) * 8 : (j * SLABS + s) * 8 + 8, :] = value

            for k in range(LEVELS):
                put(k, st[0, k, :, cols])
                put(8 + k, st[1, k, :, cols])
                put(16 + k, vn[k, :, cols])
                put(24 + k, ve[k, :, cols])
            for k in range(4):
                put(32 + k, cd[k, :, cols].astype(F32))
                put(36 + k, wt[k, :, cols])

    stage(south, st_s, vn_s, ve_s, cd_s, wt_s)
    stage(north, st_n, vn_n, ve_n, cd_n, wt_n)
    for j in range(4):
        base = (j * SLABS + 40) * 8
        cols = slice(128 * j, 128 * j + 128)
        south[base : base + 8, :] = mk_s[:, cols].astype(F32)
        flipped = mk_n[:, cols].astype(F32)
        for i in range(8):
            north[base + i : base + i + 1, :] = flipped[7 - i : 8 - i]

    def loader(edge, is_north, n):
        if n == 28:
            return lambda j: edge[pl.ds((j * SLABS + 40) * 8, 8), :]
        i, rt = n // 5, n % 5
        row = 7 - i if is_north else i
        return lambda j: edge[pl.ds((j * SLABS + rt * 8) * 8 + row, 8, stride=8), :]

    def build(put, edge, is_north):
        for n in range(29):
            load = loader(edge, is_north, n)
            for j in range(4):
                put(j, n, load(j))

    def put_a(j, n, tile):
        at = HEAD + j * PART + 8 * n
        msg_a[at : at + 8, :] = tile

    def put_b(j, n, tile):
        at = HEAD + j * PART + 8 * n
        msg_b[at : at + 8, :] = tile

    parity = sc[0] & 1
    window[...] = jnp.zeros_like(window)

    @pl.when(parity == 0)
    def _():
        build(put_a, north, True)
        build(put_b, south, False)

    @pl.when(parity == 1)
    def _():
        build(put_a, south, False)

    @pl.when((parity == 1) & (sc[0] < BLK - 1))
    def _():
        build(put_b, north, True)

    @pl.when(sc[0] == BLK - 1)
    def _():
        rq, index, near = fold_lanes(sc, lane8)
        order = [rq, (rq - 1) & 3, (rq - 2) & 3, (rq - 3) & 3]
        corner = [jnp.zeros((8, 128), F32) for _ in range(4)]
        for n in range(29):
            load = loader(north, True, n)
            g = [jnp.take_along_axis(load(j), index, axis=1) for j in order]
            for j in range(4):
                tile = jnp.where(near, g[j], g[(j + 1) % 4])
                put_b(j, n, tile)
                at = HEAD + (j % 2) * PART + 8 * n
                (low, high)[j // 2][at : at + 8, :] = tile
            below = jnp.where(rq == 0, 0.0, g[1])
            above = jnp.where(rq == 3, 0.0, g[3])
            fifth = jnp.where(lane8 < 64, jnp.where(near, g[0], below), jnp.where(near, above, g[0]))
            moved = pltpu.roll(fifth, (6 + 16 * (n % 8)) % 128, axis=1)
            corner[n // 8] = jnp.where(slot_lanes(lane8, n % 8), moved, corner[n // 8])
        for v in range(4):
            window[8 * v : 8 * v + 8, :] = corner[v]


def pack_corners(
    sc, from_west, from_east, window, a_in, b_in, low_in, high_in, sides, corner_a, corner_b, corner_low, corner_high
):
    lane = iota((ROWS, 128), 1)
    for s in range(SLABS):
        g, j = s // 16, s % 16
        east = pltpu.roll(from_east[g], (128 - 8 * j) % 128, axis=1)
        west = pltpu.roll(from_west[g], (122 - 8 * j) % 128, axis=1)
        sides[ROWS * s : ROWS * s + ROWS, :] = jnp.where(lane < 6, east, jnp.where(lane >= 122, west, 0.0))
    lane8 = iota((8, 128), 1)

    def build(dst, is_north, turn):
        corner = [window[8 * v : 8 * v + 8, :] if turn else jnp.zeros((8, 128), F32) for v in range(4)]
        if turn:
            rq, index, near = fold_lanes(sc, lane8)
            low = (lane8 < 64) & (rq == 0) & ~near
            high = (lane8 >= 64) & (rq == 3) & near
        for n in range(29):
            if n < 28:
                i, rt = n // 5, n % 5
                row = 31 - i if is_north else i
                fifth = sides[pl.ds(rt * 8 * ROWS + row, 8, stride=ROWS), :]
            else:
                mask = sides[40 * ROWS + (24 if is_north else 0) : 40 * ROWS + (32 if is_north else 8), :]
                fifth = jnp.concatenate([mask[7 - i : 8 - i] for i in range(8)], axis=0) if is_north else mask
            if turn:
                fifth = jnp.where(low | high, jnp.take_along_axis(fifth, index, axis=1), 0.0)
            moved = pltpu.roll(fifth, (6 + 16 * (n % 8)) % 128, axis=1)
            if turn:
                corner[n // 8] = corner[n // 8] + jnp.where(slot_lanes(lane8, n % 8), moved, 0.0)
            else:
                corner[n // 8] = jnp.where(slot_lanes(lane8, n % 8), moved, corner[n // 8])
        for v in range(4):
            dst[8 * v : 8 * v + 8, :] = corner[v]

    parity = sc[0] & 1

    @pl.when(parity == 0)
    def _():
        build(corner_a, True, False)
        build(corner_b, False, False)

    @pl.when(parity == 1)
    def _():
        build(corner_a, False, False)

    @pl.when((parity == 1) & (sc[0] < BLK - 1))
    def _():
        build(corner_b, True, False)

    @pl.when(sc[0] == BLK - 1)
    def _():
        build(corner_b, True, True)
        corner_low[...] = corner_b[...]
        corner_high[...] = corner_b[...]


GUARD = 8


def shifted_lanes(tiles, by, lane8):
    count = len(tiles)
    rolled = [pltpu.roll(t, (-by) % 128, axis=1) for t in tiles]
    if by > 0:
        return [jnp.where(lane8 >= 128 - by, rolled[(j + 1) % count], rolled[j]) for j in range(count)]
    return [jnp.where(lane8 < -by, rolled[(j - 1) % count], rolled[j]) for j in range(count)]


def place_ghost(load, corner, row_of, rows, old, q, v, u, taps, m, turned):
    lane8 = iota((8, 128), 1)
    edge_lanes = (lane8 < 6) | (lane8 >= 122)
    row8 = iota((8, 128), 0)
    for n in range(29):
        tiles = [load(j, n) for j in range(4)]
        fifth = pltpu.roll(corner(n // 8), (256 - 6 - 16 * (n % 8)) % 128, axis=1)
        tiles.append(jnp.where(edge_lanes, fifth, 0.0))
        if n == 28:
            for j in range(5):
                for i in range(6):
                    m[pl.ds(GUARD + j * rows + row_of(i), 1), :] = tiles[j][i : i + 1]
            continue
        i, rt = n // 5, n % 5
        for j in range(5):
            tile = tiles[j]
            if turned and rt in (2, 3):
                tile = -tile
            if turned and rt == 4:
                tile = jnp.where(row8 < 4, 8.0 - tile, tile)
            if rt < 2:
                ref, block = q, j * 16 + 8 * rt
                at = old + GUARD + block * rows + row_of(i)
            else:
                ref = (v, u, taps)[rt - 2]
                at = GUARD + j * 8 * rows + row_of(i)
            ref[pl.ds(at, 8, stride=rows), :] = tile


def own_rows(st, vn, ve, cd, wt, mk, sides, count, rows, at, side_row, q, v, u, taps, m):
    def put(ref, block, value):
        ref[pl.ds(GUARD + block * rows + at, count), :] = value

    def side(s):
        return sides[pl.ds(ROWS * s + side_row, count), :]

    for j in range(5):
        cols = slice(128 * j, 128 * j + 128)
        for t in range(2):
            for k in range(LEVELS):
                s = 8 * t + k
                put(q, j * 16 + s, st[t, k, :, cols] if j < 4 else side(s))
        for k in range(LEVELS):
            put(v, j * 8 + k, vn[k, :, cols] if j < 4 else side(16 + k))
            put(u, j * 8 + k, ve[k, :, cols] if j < 4 else side(24 + k))
        for k in range(4):
            put(taps, j * 8 + k, cd[k, :, cols].astype(F32) if j < 4 else side(32 + k))
            put(taps, j * 8 + 4 + k, wt[k, :, cols] if j < 4 else side(36 + k))
        put(m, j, mk[:, cols].astype(F32) if j < 4 else side(40))


def clear_rows(ref, blocks, rows, at, base=0):
    for b in range(blocks):
        ref[pl.ds(base + GUARD + b * rows + at, 8), :] = jnp.zeros((8, 128), F32)


def weights(is_fold, rows, first, low, count, doubled, v, u, taps, m, coef, force, ce, cw, cn, cs, cc):
    lane8 = iota((8, 128), 1)
    row8 = iota((8, 128), 0)

    def one(n):
        r = 8 * (low + n)
        ext_row = row8 + (first + r)

        def read(ref, block, shift=0):
            return ref[pl.ds(GUARD + block * rows + r + shift, 8), :]

        up_ok = jnp.where(is_fold & (ext_row >= 38) & (ext_row < 40), 0.0, 1.0)
        down_ok = jnp.where(is_fold & (ext_row >= 40) & (ext_row < 42), 0.0, 1.0)
        for j in range(5):
            w = [read(taps, 8 * j + 4 + t) for t in range(4)]
            c = [read(taps, 8 * j + t) for t in range(4)]
            wsum = w[0] + w[1] + w[2] + w[3]
            inv = 1.0 / jnp.where(wsum > 0.0, wsum, 1.0)
            w = [x * inv for x in w]
            for code in range(9):
                hit = [jnp.where(c[t] == float(code), w[t], 0.0) for t in range(4)]
                total = (hit[0] + hit[1]) + (hit[2] + hit[3])
                if code < 3:
                    total = total * down_ok
                if code >= 6:
                    total = total * up_ok
                coef[8 * (5 * code + j) : 8 * (5 * code + j) + 8, :] = total
        fields = []
        for f in range(5):
            total = None
            for dy in (-1, 0, 1):
                at = [GUARD + (5 * f + j) * 48 + first + r + 2 * dy for j in range(5)]
                grid = [doubled[pl.ds(a, 8), :] for a in at]
                for dx in (-1, 0, 1):
                    code = 3 * (dy + 1) + dx + 1
                    moved = grid if dx == 0 else shifted_lanes(grid, 2 * dx, lane8)
                    part = [
                        moved[j] * coef[8 * (5 * code + j) : 8 * (5 * code + j) + 8, :] for j in range(5)
                    ]
                    total = part if total is None else [a + b for a, b in zip(total, part)]
            fields.append(total)
        mc = [read(m, j) for j in range(5)]
        me, mw = shifted_lanes(mc, 1, lane8), shifted_lanes(mc, -1, lane8)
        oe = [mc[j] * me[j] for j in range(5)]
        ow = [mc[j] * mw[j] for j in range(5)]
        on = [mc[j] * read(m, j, 1) for j in range(5)]
        os = [mc[j] * read(m, j, -1) for j in range(5)]

        def put(ref, block, value):
            ref[pl.ds(GUARD + block * rows + r, 8), :] = value

        top, mid = [], []
        for j in range(5):
            sw, heat, fresh, tx, ty = (fields[f][j] for f in range(5))
            kv = 0.05 + 0.04 * jnp.sqrt(tx * tx + ty * ty + 0.01)
            top.append(mc[j] * kv)
            mid.append(0.05 * mc[j])
            put(force, j, 0.05 * mc[j] * sw)
            put(force, 5 + j, 0.05 * mc[j] * heat)
            put(force, 10 + j, -0.05 * mc[j] * fresh)
            put(force, 15 + j, top[j])
            put(force, 20 + j, mid[j])
        over = is_fold & (ext_row >= 40)
        for k in range(LEVELS):
            uc = [read(u, 8 * j + k) for j in range(5)]
            east, west = shifted_lanes(uc, 1, lane8), shifted_lanes(uc, -1, lane8)
            for j in range(5):
                vc = read(v, 8 * j + k)
                vt = jnp.where(over, read(v, 8 * j + k, 1), vc)
                vb = jnp.where(over, vc, read(v, 8 * j + k, -1))
                et = jnp.where(over, east[j], uc[j])
                wt = jnp.where(over, uc[j], west[j])
                put(ce, 8 * j + k, oe[j] * (0.08 - jnp.minimum(et, 0.0)))
                put(cw, 8 * j + k, ow[j] * (0.08 + jnp.maximum(wt, 0.0)))
                put(cn, 8 * j + k, on[j] * (0.08 - jnp.minimum(vt, 0.0)))
                put(cs, 8 * j + k, os[j] * (0.08 + jnp.maximum(vb, 0.0)))
                centre = 1.0 - oe[j] * (0.08 + jnp.maximum(et, 0.0)) - ow[j] * (0.08 - jnp.minimum(wt, 0.0))
                centre = centre - on[j] * (0.08 + jnp.maximum(vt, 0.0)) - os[j] * (0.08 - jnp.minimum(vb, 0.0))
                if k == 0:
                    centre = centre - top[j]
                elif k == 1:
                    centre = centre - top[j] - mid[j]
                elif k == LEVELS - 1:
                    centre = centre - mid[j]
                else:
                    centre = centre - 2.0 * mid[j]
                put(cc, 8 * j + k, centre)

    for n in range(count):
        one(n)


def steps(rows, qa, qb, force, ce, cw, cn, cs, cc):
    lane8 = iota((8, 128), 1)

    def one(q, p, r, width):
        def read(ref, block, shift=0):
            at = GUARD + block * rows + r + shift
            return ref[at : at + 8, :]

        def state(t, k, j, shift=0):
            return read(q, 16 * j + 8 * t + k, shift)

        mid = [read(force, 20 + j) for j in range(width)]
        here = [[state(t, 0, j) for j in range(5)] for t in range(2)]
        below = [None, None]
        for k in range(LEVELS):
            weight = [[read(ref, 8 * j + k) for j in range(width)] for ref in (cc, ce, cw, cn, cs)]
            for t in range(2):
                above = here[t]
                after = [state(t, k + 1, j) for j in range(5)] if k < LEVELS - 1 else None
                east, west = shifted_lanes(above, 1, lane8), shifted_lanes(above, -1, lane8)
                for j in range(width):
                    total = weight[0][j] * above[j] + weight[1][j] * east[j]
                    total = total + weight[2][j] * west[j]
                    total = total + weight[3][j] * state(t, k, j, 1)
                    total = total + weight[4][j] * state(t, k, j, -1)
                    if k == 0:
                        total = total + read(force, 15 + j) * after[j]
                    elif k == 1:
                        total = total + read(force, 15 + j) * below[t][j] + mid[j] * after[j]
                    elif k == LEVELS - 1:
                        total = total + mid[j] * below[t][j]
                    else:
                        total = total + mid[j] * (below[t][j] + after[j])
                    if t == 0:
                        total = total + (0.5 ** (k + 1)) * read(force, j)
                        if k == 0:
                            total = total + read(force, 5 + j)
                    elif k == 0:
                        total = total + read(force, 10 + j)
                    at = GUARD + (16 * j + 8 * t + k) * rows + r
                    p[at : at + 8, :] = total
                below[t], here[t] = above, after

    def step(q, p, last=False):
        for n in range(1, 5) if last else range(6):
            one(q, p, 8 * n, 4 if last else 5)

    def two(i, carry):
        step(qa, qb)
        step(qb, qa)
        return carry

    lax.fori_loop(0, STEPS // 2 - 1, two, 0)
    step(qa, qb)
    step(qb, qa, True)


def skin_rows(q, m, rows, at, count, pairs):
    sums = []
    table = (iota((COLS, COLS // 2), 0) // 2 == iota((COLS, COLS // 2), 1)).astype(F32)
    for with_heat in (True, False):
        parts = []
        for j in range(4):
            value = m[GUARD + j * rows + at : GUARD + j * rows + at + count, :]
            if with_heat:
                value = value * q[GUARD + 16 * j * rows + at : GUARD + 16 * j * rows + at + count, :]
            pairs[0:count, :] = value
            parts.append(
                pairs[pl.ds(0, count // 2, stride=2), :] + pairs[pl.ds(1, count // 2, stride=2), :]
            )
        narrow = jnp.concatenate(parts, axis=1)
        sums.append(jnp.dot(narrow, table, precision=lax.Precision.HIGHEST, preferred_element_type=F32))
    return sums[0] / jnp.maximum(sums[1], 1.0)


def clear_guards(refs):
    for ref in refs:
        ref[0:GUARD, :] = jnp.zeros((GUARD, 128), F32)
        ref[ref.shape[0] - GUARD :, :] = jnp.zeros((GUARD, 128), F32)


def interval(
    sc, st, vn, ve, cd, wt, mk, sides, got_a, got_b, major, minor, atm, atm_top, out, sst,
    qa, qb, v, u, taps, m, atm_rows, grids, coef, force, ce, cw, cn, cs, cc, pairs,
):
    rows = EXT_ROWS
    lane8 = iota((8, 128), 1)
    is_fold = sc[0] == BLK - 1
    odd = sc[0] & 1
    clear_guards((qa, qb, v, u, taps, m, grids))
    for at in (0, 40):
        clear_rows(qa, 80, rows, at)
        clear_rows(v, 40, rows, at)
        clear_rows(u, 40, rows, at)
        clear_rows(taps, 40, rows, at)
        clear_rows(m, 5, rows, at)
    own_rows(st, vn, ve, cd, wt, mk, sides, ROWS, rows, 8, 0, qa, v, u, taps, m)

    def to_north(i):
        return 40 + i

    def to_south(i):
        return 7 - i

    def plain(msg, row_of):
        place_ghost(
            lambda j, n: msg[HEAD + j * PART + 8 * n : HEAD + j * PART + 8 * n + 8, :],
            lambda g: msg[8 * g : 8 * g + 8, :],
            row_of, rows, 0, qa, v, u, taps, m, False,
        )

    @pl.when(odd == 0)
    def _():
        plain(got_a, to_north)
        plain(got_b, to_south)

    @pl.when(odd == 1)
    def _():
        plain(got_a, to_south)

    @pl.when((odd == 1) & jnp.logical_not(is_fold))
    def _():
        plain(got_b, to_north)

    def fold(first_is_major):
        seam = sc[3]

        def load(j, n):
            at = HEAD + j * PART + 8 * n
            value = major[at : at + 8, :]
            if first_is_major == (j >= 2):
                at = HEAD + (j % 2) * PART + 8 * n
                second = lane8 + 128 * j > seam
                value = jnp.where(second if first_is_major else ~second, minor[at : at + 8, :], value)
            return value

        def corner(g):
            at = slice(8 * g, 8 * g + 8)
            one, two = (major, minor) if first_is_major else (minor, major)
            return jnp.where((lane8 & 15) < 6, one[at, :], two[at, :])

        place_ghost(load, corner, to_north, rows, 0, qa, v, u, taps, m, True)

    @pl.when(is_fold & (sc[3] >= 256))
    def _():
        fold(True)

    @pl.when(is_fold & (sc[3] < 256))
    def _():
        fold(False)

    def each(put):
        for f in range(5):
            for part in range(3):
                put(24 * f, slice(128 * part, 128 * part + 128), 3 * f + part)

    @pl.when(jnp.logical_not(is_fold))
    def _():
        def put(at, cols, row):
            far = atm[pl.ds(16 + row, 16, stride=SLOT), :]
            atm_rows[at : at + 4, cols] = far[12:16]
            atm_rows[at + 4 : at + 20, cols] = atm[pl.ds(row, 16, stride=SLOT), :]
            atm_rows[at + 20 : at + 24, cols] = far[0:4]

        each(put)

    @pl.when(sc[0] == RELAY)
    def _():
        def put(at, cols, row):
            atm_rows[at + 20 : at + 24, cols] = atm[pl.ds(32 + row, 16, stride=SLOT), :][0:4]

        each(put)

    @pl.when(is_fold)
    def _():
        def put(at, cols, row):
            atm_rows[at : at + 4, cols] = atm_top[pl.ds(row, 16, stride=SLOT), :][12:16]
            atm_rows[at + 4 : at + 20, cols] = atm_top[pl.ds(32 + row, 16, stride=SLOT), :]
            atm_rows[at + 20 : at + 24, cols] = atm_top[pl.ds(16 + row, 16, stride=SLOT), :][0:4]

        each(put)

    src = iota((384, EXT_COLS), 0)
    dst = iota((384, EXT_COLS), 1)
    table = (src == jnp.where(dst < 576, dst // 2, dst // 2 + 64)).astype(F32)
    wide = jnp.dot(atm_rows[...], table, precision=lax.Precision.HIGHEST, preferred_element_type=F32)
    for f in range(5):
        for j in range(5):
            tile = wide[24 * f : 24 * f + 24, 128 * j : 128 * j + 128]
            base = GUARD + (5 * f + j) * 48
            grids[pl.ds(base, 24, stride=2), :] = tile
            grids[pl.ds(base + 1, 24, stride=2), :] = tile
    weights(is_fold, rows, 0, 0, 6, grids, v, u, taps, m, coef, force, ce, cw, cn, cs, cc)
    steps(rows, qa, qb, force, ce, cw, cn, cs, cc)
    for t in range(2):
        for k in range(LEVELS):
            for j in range(4):
                base = GUARD + (16 * j + 8 * t + k) * rows + 8
                out[t, k, :, 128 * j : 128 * j + 128] = qa[base : base + ROWS, :]
    result = skin_rows(qa, m, rows, 8, ROWS, pairs)
    sst[:, 0, :] = result[:, 0:128]
    sst[:, 1, :] = result[:, 128:256]


def place(b, l):
    return b * LON + l % LON


def body(temp_salt, east_vel, north_vel, land_mask, fluxes, remap_code, remap_weight, fold_source):
    axes = ("blk", "lon")
    arrays = (temp_salt, north_vel, east_vel, remap_code, remap_weight, land_mask)

    sds = lambda *shape: jax.ShapeDtypeStruct(shape, F32)
    sc, band = pl.pallas_call(
        combine_bands,
        grid=(1,),
        in_specs=[SCALARS, full((10, 32, 128))],
        out_specs=[SCALARS, full((5, 32, 128))],
        out_shape=[jax.ShapeDtypeStruct((8,), jnp.int32), sds(5, 32, 128)],
        compiler_params=limit(56),
        name="combine_bands",
    )(fold_source, fluxes.reshape(10, 32, 128))
    band_pairs = []
    for n in range(4):
        for blk in range(RELAY):
            band_pairs.append((place(blk + 1, n), place(blk, n)))
            band_pairs.append((place(blk, 12 + n), place(blk + 1, 12 + n)))
        band_pairs.append((place(BLK - 1, 15 - n), place(RELAY, n)))
    other = lax.ppermute(band, axes, band_pairs)
    top = lax.ppermute(band, axes, [(place(BLK - 1, n), place(RELAY, n)) for n in range(LON)])

    first, _ = lax.optimization_barrier((land_mask, band))
    specs, operands = [], []
    for x in (*arrays[:-1], first):
        lead = x.shape[:-2]
        for j in (0, 3):
            specs.append(at_block(lead + (ROWS, 128), (0,) * len(lead) + (0, j)))
            operands.append(x)
    to_west, to_east = pl.pallas_call(
        pack_columns,
        grid=(1,),
        in_specs=specs,
        out_specs=[full((3, ROWS, 128))] * 2,
        out_shape=[sds(3, ROWS, 128)] * 2,
        compiler_params=limit(56),
        name="pack_columns",
    )(*operands)
    from_west = lax.ppermute(to_east, "lon", [(i, (i + 1) % LON) for i in range(LON)])
    from_east = lax.ppermute(to_west, "lon", [((i + 1) % LON, i) for i in range(LON)])

    first, _, other, top = lax.optimization_barrier((land_mask, to_west, other, top))
    specs, operands = [SCALARS], [sc]
    for x in (*arrays[:-1], first):
        lead = x.shape[:-2]
        for j in (0, 3):
            specs.append(at_block(lead + (8, COLS), (0,) * len(lead) + (j, 0)))
            operands.append(x)
    sizes = (WHOLE, WHOLE, HALF, HALF)
    *messages, window = pl.pallas_call(
        pack_rows,
        grid=(1,),
        in_specs=specs,
        out_specs=[full((n, 128)) for n in sizes] + [full((HEAD, 128))],
        out_shape=[sds(n, 128) for n in sizes] + [sds(HEAD, 128)],
        scratch_shapes=[VMEM((4 * SLABS * 8, 128), F32)] * 2,
        compiler_params=limit(56),
        name="pack_rows",
    )(*operands)
    sides, msg_a, msg_b, low, high = pl.pallas_call(
        pack_corners,
        grid=(1,),
        in_specs=[SCALARS, full((3, ROWS, 128)), full((3, ROWS, 128)), full((HEAD, 128))]
        + [pl.BlockSpec(memory_space=pl.ANY)] * 4,
        out_specs=[full((SLABS * ROWS, 128))] + [full((HEAD, 128))] * 4,
        out_shape=[sds(SLABS * ROWS, 128)] + [sds(n, 128) for n in sizes],
        input_output_aliases={4: 1, 5: 2, 6: 3, 7: 4},
        compiler_params=limit(56),
        name="pack_corners",
    )(sc, from_west, from_east, window, *messages)

    on_chip = [(place(i, n), place(i ^ 1, n)) for i in range(BLK) for n in range(LON)]
    across = []
    for i in range(1, BLK - 1, 2):
        for n in range(LON):
            across += [(place(i, n), place(i + 1, n)), (place(i + 1, n), place(i, n))]
    got_a = lax.ppermute(msg_a, axes, on_chip)
    got_b = lax.ppermute(msg_b, axes, across)

    def branch(shift, second_half):
        top = BLK - 1
        one = [(place(top, n), place(top, (shift - n) % LON)) for n in range(LON)]
        two = [(place(top, n), place(top, (shift - 1 - n) % LON)) for n in range(LON)]

        def send(whole, low, high):
            if second_half:
                return lax.ppermute(whole, axes, one), lax.ppermute(high, axes, two)
            return lax.ppermute(whole, axes, two), lax.ppermute(low, axes, one)

        return send

    got_f = lax.switch(
        sc[5],
        [branch(shift, half) for shift in range(LON) for half in range(2)],
        msg_b,
        low,
        high,
    )

    def spread(band, other, top):
        chunks = pl.pallas_call(
            chunk_bands,
            grid=(1,),
            in_specs=[SCALARS] + [full((5, 32, 128))] * 3,
            out_specs=full((LON * SLOT, 128)),
            out_shape=sds(LON * SLOT, 128),
            scratch_shapes=[VMEM((160, 128), F32)] * 4,
            compiler_params=limit(8),
            name="chunk_bands",
        )(sc, band, other, top)
        return lax.all_to_all(chunks, "lon", split_axis=0, concat_axis=0, tiled=True)

    later, _ = lax.optimization_barrier((band, got_f[1]))
    atm = lax.cond(
        lax.axis_index("blk") == BLK - 1, lambda *x: jnp.zeros((LON * SLOT, 128), F32), spread, later, other, top
    )
    atm_top = lax.ppermute(atm, axes, [(place(RELAY, n), place(BLK - 1, n)) for n in range(LON)])

    ext = lambda n: VMEM((GUARD * 2 + n * EXT_ROWS, 128), F32)
    state, skin = pl.pallas_call(
        interval,
        grid=(1,),
        in_specs=[SCALARS] + [full(x.shape) for x in (*arrays, sides, got_a, got_b, *got_f, atm, atm_top)],
        out_specs=[full((2, LEVELS, ROWS, COLS)), full((LON, 2, 128))],
        out_shape=[sds(2, LEVELS, ROWS, COLS), sds(LON, 2, 128)],
        scratch_shapes=[ext(80), ext(80), ext(40), ext(40), ext(40), ext(5), VMEM((120, 384), F32), ext(25)]
        + [VMEM((360, 128), F32), ext(25)]
        + [ext(40)] * 5
        + [VMEM((ROWS, 128), F32)],
        compiler_params=limit(36),
        name="interval",
    )(sc, *arrays, sides, got_a, got_b, *got_f, atm, atm_top)
    bands = lax.all_to_all(skin, "lon", split_axis=0, concat_axis=0, tiled=True)
    return state, bands.reshape(1, LON * 256)


def solution(mesh):
    placed = (
        P(None, None, "blk", "lon"),
        P(None, "blk", "lon"),
        P(None, "blk", "lon"),
        P("blk", "lon"),
        P(None, ("blk", "lon"), None),
        P(None, "blk", "lon"),
        P(None, "blk", "lon"),
        P("lon"),
    )
    return jax.shard_map(
        body,
        mesh=mesh,
        in_specs=placed,
        out_specs=(P(None, None, "blk", "lon"), P(("blk", "lon"), None)),
        check_vma=False,
    )
```

```python
import jax
import jax.numpy as jnp
from jax import lax
from jax.experimental import pallas as pl
from jax.experimental.pallas import tpu as pltpu
from jax.sharding import PartitionSpec as P

STEPS = 6
F32 = jnp.float32
LEVELS = 8
BLK, LON = 8, 16
ROWS, COLS = 32, 512
EXT_ROWS, EXT_COLS = 48, 640
NX = 8192
SLABS = 41
PART = 232
HEAD = 32
WHOLE = HEAD + 4 * PART
HALF = HEAD + 2 * PART
VMEM = pltpu.VMEM
SMEM = pltpu.SMEM


def limit(mib):
    return pltpu.CompilerParams(vmem_limit_bytes=mib * 1024 * 1024)


RELAY = BLK - 2
CHUNK = 32


def iota(shape, dim):
    return lax.broadcasted_iota(jnp.int32, shape, dim)


def full(shape):
    return pl.BlockSpec(shape, lambda i: (0,) * len(shape))


def at_block(shape, place):
    return pl.BlockSpec(shape, lambda i: place)


SCALARS = pl.BlockSpec(memory_space=SMEM)


def combine_bands(fold, flux, sc, band):
    l = lax.axis_index("lon")
    mirror = lax.rem(fold[0] + COLS * l, NX)
    sc[0] = lax.axis_index("blk")
    sc[1] = l
    sc[2] = mirror // COLS
    sc[3] = lax.rem(mirror, COLS)
    sc[4] = (mirror - 1) // 2
    sc[5] = mirror // 256
    sc[6] = 0
    sc[7] = 0
    band[0] = flux[0]
    band[1] = flux[1] + flux[2] + flux[3] - 0.33 * flux[5]
    band[2] = flux[4] + flux[5] + flux[6] + flux[7]
    band[3] = flux[8]
    band[4] = flux[9]


def pack_columns(st0, st3, vn0, vn3, ve0, ve3, cd0, cd3, wt0, wt3, mk0, mk3, to_west, to_east):
    lane = iota((ROWS, 128), 1)

    def pack(groups, shift, out):
        for g, tiles in enumerate(groups):
            acc = jnp.zeros((ROWS, 128), F32)
            for j, tile in enumerate(tiles):
                moved = pltpu.roll(tile().astype(F32), (8 * j + shift) % 128, axis=1)
                acc = jnp.where((lane >= 8 * j) & (lane < 8 * j + 8), moved, acc)
            out[g] = acc

    def groups(st, vn, ve, cd, wt, mk):
        first = [lambda t=t, k=k: st[t, k] for t in range(2) for k in range(LEVELS)]
        second = [lambda k=k: vn[k] for k in range(LEVELS)] + [lambda k=k: ve[k] for k in range(LEVELS)]
        third = [lambda k=k: cd[k] for k in range(4)] + [lambda k=k: wt[k] for k in range(4)] + [lambda: mk[...]]
        return [first, second, third]

    pack(groups(st0, vn0, ve0, cd0, wt0, mk0), 0, to_west)
    pack(groups(st3, vn3, ve3, cd3, wt3, mk3), 6, to_east)


def chunk_bands(sc, band, other, top, out, own, held, relayed, turned):
    own[...] = band[...].reshape(160, 128)
    held[...] = other[...].reshape(160, 128)
    relayed[...] = top[...].reshape(160, 128)
    is_relay = sc[0] == RELAY

    @pl.when(is_relay & (sc[1] < 4))
    def _():
        pole = sc[4]
        pq, pr = pole // 128, pole % 128
        lane8 = iota((8, 128), 1)
        index = (pr - lane8) & 127
        for n in range(20):
            turned[8 * n : 8 * n + 8, :] = jnp.take_along_axis(held[8 * n : 8 * n + 8, :], index, axis=1)
        lane1 = iota((1, 128), 1)

        def one(row, carry):
            near = (pq - row) & 31
            far = (pq - row - 1) & 31
            for f in range(5):
                a = turned[pl.ds(32 * f + near, 1), :]
                b = turned[pl.ds(32 * f + far, 1), :]
                held[pl.ds(32 * f + row, 1), :] = jnp.where(lane1 <= pr, a, b)
            return carry

        lax.fori_loop(0, 32, one, 0)

    lane = iota((16, 128), 1)
    sides = jnp.zeros((16, 128), F32)
    for slot, src in enumerate((own, held, relayed)):
        for f in range(5):
            even = src[pl.ds(32 * f, 16, stride=2), :]
            odd = src[pl.ds(32 * f + 1, 16, stride=2), :]
            out[pl.ds(10 * slot + 2 * f, 16, stride=CHUNK), :] = even
            out[pl.ds(10 * slot + 2 * f + 1, 16, stride=CHUNK), :] = odd
            side = jnp.where(lane < 64, pltpu.roll(even, 15, axis=0), pltpu.roll(odd, 1, axis=0))
            at = 8 * (5 * slot + f)
            sides = jnp.where((lane >= at) & (lane < at + 8), pltpu.roll(side, at + 4, axis=1), sides)
    out[pl.ds(30, 16, stride=CHUNK), :] = sides
    out[pl.ds(31, 16, stride=CHUNK), :] = jnp.zeros((16, 128), F32)


def slot_lanes(lane8, slot):
    return (lane8 >= 16 * slot) & (lane8 < 16 * slot + 12)


def fold_lanes(sc, lane8):
    rq, rr = sc[3] // 128, sc[3] % 128
    return rq, (rr - lane8) & 127, lane8 <= rr


def pack_rows(
    sc, st_s, st_n, vn_s, vn_n, ve_s, ve_n, cd_s, cd_n, wt_s, wt_n, mk_s, mk_n,
    msg_a, msg_b, low, high, window, south, north,
):
    lane8 = iota((8, 128), 1)

    def stage(dst, st, vn, ve, cd, wt):
        for j in range(4):
            cols = slice(128 * j, 128 * j + 128)

            def put(s, value):
                dst[(j * SLABS + s) * 8 : (j * SLABS + s) * 8 + 8, :] = value

            for k in range(LEVELS):
                put(k, st[0, k, :, cols])
                put(8 + k, st[1, k, :, cols])
                put(16 + k, vn[k, :, cols])
                put(24 + k, ve[k, :, cols])
            for k in range(4):
                put(32 + k, cd[k, :, cols].astype(F32))
                put(36 + k, wt[k, :, cols])

    stage(south, st_s, vn_s, ve_s, cd_s, wt_s)
    stage(north, st_n, vn_n, ve_n, cd_n, wt_n)
    for j in range(4):
        base = (j * SLABS + 40) * 8
        cols = slice(128 * j, 128 * j + 128)
        south[base : base + 8, :] = mk_s[:, cols].astype(F32)
        flipped = mk_n[:, cols].astype(F32)
        for i in range(8):
            north[base + i : base + i + 1, :] = flipped[7 - i : 8 - i]

    def loader(edge, is_north, n):
        if n == 28:
            return lambda j: edge[pl.ds((j * SLABS + 40) * 8, 8), :]
        i, rt = n // 5, n % 5
        row = 7 - i if is_north else i
        return lambda j: edge[pl.ds((j * SLABS + rt * 8) * 8 + row, 8, stride=8), :]

    def build(put, edge, is_north):
        for n in range(29):
            load = loader(edge, is_north, n)
            for j in range(4):
                put(j, n, load(j))

    def put_a(j, n, tile):
        at = HEAD + j * PART + 8 * n
        msg_a[at : at + 8, :] = tile

    def put_b(j, n, tile):
        at = HEAD + j * PART + 8 * n
        msg_b[at : at + 8, :] = tile

    parity = sc[0] & 1
    window[...] = jnp.zeros_like(window)

    @pl.when(parity == 0)
    def _():
        build(put_a, north, True)
        build(put_b, south, False)

    @pl.when(parity == 1)
    def _():
        build(put_a, south, False)

    @pl.when((parity == 1) & (sc[0] < BLK - 1))
    def _():
        build(put_b, north, True)

    @pl.when(sc[0] == BLK - 1)
    def _():
        rq, index, near = fold_lanes(sc, lane8)
        order = [rq, (rq - 1) & 3, (rq - 2) & 3, (rq - 3) & 3]
        corner = [jnp.zeros((8, 128), F32) for _ in range(4)]
        for n in range(29):
            load = loader(north, True, n)
            g = [jnp.take_along_axis(load(j), index, axis=1) for j in order]
            for j in range(4):
                tile = jnp.where(near, g[j], g[(j + 1) % 4])
                put_b(j, n, tile)
                at = HEAD + (j % 2) * PART + 8 * n
                (low, high)[j // 2][at : at + 8, :] = tile
            below = jnp.where(rq == 0, 0.0, g[1])
            above = jnp.where(rq == 3, 0.0, g[3])
            fifth = jnp.where(lane8 < 64, jnp.where(near, g[0], below), jnp.where(near, above, g[0]))
            moved = pltpu.roll(fifth, (6 + 16 * (n % 8)) % 128, axis=1)
            corner[n // 8] = jnp.where(slot_lanes(lane8, n % 8), moved, corner[n // 8])
        for v in range(4):
            window[8 * v : 8 * v + 8, :] = corner[v]


def pack_corners(
    sc, from_west, from_east, window, a_in, b_in, low_in, high_in, sides, corner_a, corner_b, corner_low, corner_high
):
    lane = iota((ROWS, 128), 1)
    for s in range(SLABS):
        g, j = s // 16, s % 16
        east = pltpu.roll(from_east[g], (128 - 8 * j) % 128, axis=1)
        west = pltpu.roll(from_west[g], (122 - 8 * j) % 128, axis=1)
        sides[ROWS * s : ROWS * s + ROWS, :] = jnp.where(lane < 6, east, jnp.where(lane >= 122, west, 0.0))
    lane8 = iota((8, 128), 1)

    def build(dst, is_north, turn):
        corner = [window[8 * v : 8 * v + 8, :] if turn else jnp.zeros((8, 128), F32) for v in range(4)]
        if turn:
            rq, index, near = fold_lanes(sc, lane8)
            low = (lane8 < 64) & (rq == 0) & ~near
            high = (lane8 >= 64) & (rq == 3) & near
        for n in range(29):
            if n < 28:
                i, rt = n // 5, n % 5
                row = 31 - i if is_north else i
                fifth = sides[pl.ds(rt * 8 * ROWS + row, 8, stride=ROWS), :]
            else:
                mask = sides[40 * ROWS + (24 if is_north else 0) : 40 * ROWS + (32 if is_north else 8), :]
                fifth = jnp.concatenate([mask[7 - i : 8 - i] for i in range(8)], axis=0) if is_north else mask
            if turn:
                fifth = jnp.where(low | high, jnp.take_along_axis(fifth, index, axis=1), 0.0)
            moved = pltpu.roll(fifth, (6 + 16 * (n % 8)) % 128, axis=1)
            if turn:
                corner[n // 8] = corner[n // 8] + jnp.where(slot_lanes(lane8, n % 8), moved, 0.0)
            else:
                corner[n // 8] = jnp.where(slot_lanes(lane8, n % 8), moved, corner[n // 8])
        for v in range(4):
            dst[8 * v : 8 * v + 8, :] = corner[v]

    parity = sc[0] & 1

    @pl.when(parity == 0)
    def _():
        build(corner_a, True, False)
        build(corner_b, False, False)

    @pl.when(parity == 1)
    def _():
        build(corner_a, False, False)

    @pl.when((parity == 1) & (sc[0] < BLK - 1))
    def _():
        build(corner_b, True, False)

    @pl.when(sc[0] == BLK - 1)
    def _():
        build(corner_b, True, True)
        corner_low[...] = corner_b[...]
        corner_high[...] = corner_b[...]


GUARD = 8


def shifted_lanes(tiles, by, lane8):
    count = len(tiles)
    rolled = [pltpu.roll(t, (-by) % 128, axis=1) for t in tiles]
    if by > 0:
        return [jnp.where(lane8 >= 128 - by, rolled[(j + 1) % count], rolled[j]) for j in range(count)]
    return [jnp.where(lane8 < -by, rolled[(j - 1) % count], rolled[j]) for j in range(count)]


def place_ghost(load, corner, row_of, rows, old, q, v, u, taps, m, turned):
    lane8 = iota((8, 128), 1)
    edge_lanes = (lane8 < 6) | (lane8 >= 122)
    row8 = iota((8, 128), 0)
    for n in range(29):
        tiles = [load(j, n) for j in range(4)]
        fifth = pltpu.roll(corner(n // 8), (256 - 6 - 16 * (n % 8)) % 128, axis=1)
        tiles.append(jnp.where(edge_lanes, fifth, 0.0))
        if n == 28:
            for j in range(5):
                for i in range(6):
                    m[pl.ds(GUARD + j * rows + row_of(i), 1), :] = tiles[j][i : i + 1]
            continue
        i, rt = n // 5, n % 5
        for j in range(5):
            tile = tiles[j]
            if turned and rt in (2, 3):
                tile = -tile
            if turned and rt == 4:
                tile = jnp.where(row8 < 4, 8.0 - tile, tile)
            if rt < 2:
                ref, block = q, j * 16 + 8 * rt
                at = old + GUARD + block * rows + row_of(i)
            else:
                ref = (v, u, taps)[rt - 2]
                at = GUARD + j * 8 * rows + row_of(i)
            ref[pl.ds(at, 8, stride=rows), :] = tile


def own_rows(st, vn, ve, cd, wt, mk, sides, count, rows, at, side_row, q, v, u, taps, m):
    def put(ref, block, value):
        ref[pl.ds(GUARD + block * rows + at, count), :] = value

    def side(s):
        return sides[pl.ds(ROWS * s + side_row, count), :]

    for j in range(5):
        cols = slice(128 * j, 128 * j + 128)
        for t in range(2):
            for k in range(LEVELS):
                s = 8 * t + k
                put(q, j * 16 + s, st[t, k, :, cols] if j < 4 else side(s))
        for k in range(LEVELS):
            put(v, j * 8 + k, vn[k, :, cols] if j < 4 else side(16 + k))
            put(u, j * 8 + k, ve[k, :, cols] if j < 4 else side(24 + k))
        for k in range(4):
            put(taps, j * 8 + k, cd[k, :, cols].astype(F32) if j < 4 else side(32 + k))
            put(taps, j * 8 + 4 + k, wt[k, :, cols] if j < 4 else side(36 + k))
        put(m, j, mk[:, cols].astype(F32) if j < 4 else side(40))


def clear_rows(ref, blocks, rows, at, base=0):
    for b in range(blocks):
        ref[pl.ds(base + GUARD + b * rows + at, 8), :] = jnp.zeros((8, 128), F32)


def weights(is_fold, rows, first, low, count, doubled, v, u, taps, m, coef, force, ce, cw, cn, cs, cc):
    lane8 = iota((8, 128), 1)
    row8 = iota((8, 128), 0)

    def one(n):
        r = 8 * (low + n)
        ext_row = row8 + (first + r)

        def read(ref, block, shift=0):
            return ref[pl.ds(GUARD + block * rows + r + shift, 8), :]

        up_ok = jnp.where(is_fold & (ext_row >= 38) & (ext_row < 40), 0.0, 1.0)
        down_ok = jnp.where(is_fold & (ext_row >= 40) & (ext_row < 42), 0.0, 1.0)
        for j in range(5):
            w = [read(taps, 8 * j + 4 + t) for t in range(4)]
            c = [read(taps, 8 * j + t) for t in range(4)]
            wsum = w[0] + w[1] + w[2] + w[3]
            inv = 1.0 / jnp.where(wsum > 0.0, wsum, 1.0)
            w = [x * inv for x in w]
            for code in range(9):
                hit = [jnp.where(c[t] == float(code), w[t], 0.0) for t in range(4)]
                total = (hit[0] + hit[1]) + (hit[2] + hit[3])
                if code < 3 and n == 5:
                    total = total * down_ok
                if code >= 6 and n == 4:
                    total = total * up_ok
                coef[8 * (5 * code + j) : 8 * (5 * code + j) + 8, :] = total
        fields = []
        for f in range(5):
            total = None
            for dy in (-1, 0, 1):
                at = [GUARD + (5 * f + j) * 48 + first + r + 2 * dy for j in range(5)]
                grid = [doubled[pl.ds(a, 8), :] for a in at]
                for dx in (-1, 0, 1):
                    code = 3 * (dy + 1) + dx + 1
                    moved = grid if dx == 0 else shifted_lanes(grid, 2 * dx, lane8)
                    part = [
                        moved[j] * coef[8 * (5 * code + j) : 8 * (5 * code + j) + 8, :] for j in range(5)
                    ]
                    total = part if total is None else [a + b for a, b in zip(total, part)]
            fields.append(total)
        mc = [read(m, j) for j in range(5)]
        me, mw = shifted_lanes(mc, 1, lane8), shifted_lanes(mc, -1, lane8)
        oe = [mc[j] * me[j] for j in range(5)]
        ow = [mc[j] * mw[j] for j in range(5)]
        on = [mc[j] * read(m, j, 1) for j in range(5)]
        os = [mc[j] * read(m, j, -1) for j in range(5)]

        def put(ref, block, value):
            ref[pl.ds(GUARD + block * rows + r, 8), :] = value

        top, mid = [], []
        for j in range(5):
            sw, heat, fresh, tx, ty = (fields[f][j] for f in range(5))
            kv = 0.05 + 0.04 * jnp.sqrt(tx * tx + ty * ty + 0.01)
            top.append(mc[j] * kv)
            mid.append(0.05 * mc[j])
            put(force, j, 0.05 * mc[j] * sw)
            put(force, 5 + j, 0.05 * mc[j] * heat)
            put(force, 10 + j, -0.05 * mc[j] * fresh)
            put(force, 15 + j, top[j])
            put(force, 20 + j, mid[j])
        over = is_fold & (ext_row >= 40)
        for k in range(LEVELS):
            uc = [read(u, 8 * j + k) for j in range(5)]
            west = shifted_lanes(uc, -1, lane8)
            east = shifted_lanes(uc, 1, lane8) if n == 5 else None
            for j in range(5):
                vc = read(v, 8 * j + k)
                et, wt, vt, vb = uc[j], west[j], vc, read(v, 8 * j + k, -1)
                if n == 5:
                    et, wt = jnp.where(over, east[j], et), jnp.where(over, uc[j], wt)
                    vt, vb = jnp.where(over, read(v, 8 * j + k, 1), vt), jnp.where(over, vc, vb)
                put(ce, 8 * j + k, oe[j] * (0.08 - jnp.minimum(et, 0.0)))
                put(cw, 8 * j + k, ow[j] * (0.08 + jnp.maximum(wt, 0.0)))
                put(cn, 8 * j + k, on[j] * (0.08 - jnp.minimum(vt, 0.0)))
                put(cs, 8 * j + k, os[j] * (0.08 + jnp.maximum(vb, 0.0)))
                centre = 1.0 - oe[j] * (0.08 + jnp.maximum(et, 0.0)) - ow[j] * (0.08 - jnp.minimum(wt, 0.0))
                centre = centre - on[j] * (0.08 + jnp.maximum(vt, 0.0)) - os[j] * (0.08 - jnp.minimum(vb, 0.0))
                if k == 0:
                    centre = centre - top[j]
                elif k == 1:
                    centre = centre - top[j] - mid[j]
                elif k == LEVELS - 1:
                    centre = centre - mid[j]
                else:
                    centre = centre - 2.0 * mid[j]
                put(cc, 8 * j + k, centre)

    for n in range(count):
        one(n)


def steps(rows, qa, qb, force, ce, cw, cn, cs, cc):
    lane8 = iota((8, 128), 1)

    def one(q, p, r, width):
        def read(ref, block, shift=0):
            at = GUARD + block * rows + r + shift
            return ref[at : at + 8, :]

        def state(t, k, j, shift=0):
            return read(q, 16 * j + 8 * t + k, shift)

        mid = [read(force, 20 + j) for j in range(width)]
        here = [[state(t, 0, j) for j in range(5)] for t in range(2)]
        below = [None, None]
        for k in range(LEVELS):
            weight = [[read(ref, 8 * j + k) for j in range(width)] for ref in (cc, ce, cw, cn, cs)]
            for t in range(2):
                above = here[t]
                after = [state(t, k + 1, j) for j in range(5)] if k < LEVELS - 1 else None
                east, west = shifted_lanes(above, 1, lane8), shifted_lanes(above, -1, lane8)
                for j in range(width):
                    total = weight[0][j] * above[j] + weight[1][j] * east[j]
                    total = total + weight[2][j] * west[j]
                    total = total + weight[3][j] * state(t, k, j, 1)
                    total = total + weight[4][j] * state(t, k, j, -1)
                    if k == 0:
                        total = total + read(force, 15 + j) * after[j]
                    elif k == 1:
                        total = total + read(force, 15 + j) * below[t][j] + mid[j] * after[j]
                    elif k == LEVELS - 1:
                        total = total + mid[j] * below[t][j]
                    else:
                        total = total + mid[j] * (below[t][j] + after[j])
                    if t == 0:
                        total = total + (0.5 ** (k + 1)) * read(force, j)
                        if k == 0:
                            total = total + read(force, 5 + j)
                    elif k == 0:
                        total = total + read(force, 10 + j)
                    at = GUARD + (16 * j + 8 * t + k) * rows + r
                    p[at : at + 8, :] = total
                below[t], here[t] = above, after

    def step(q, p, last=False):
        for n in range(1, 5) if last else range(6):
            one(q, p, 8 * n, 4 if last else 5)

    def two(i, carry):
        step(qa, qb)
        step(qb, qa)
        return carry

    lax.fori_loop(0, STEPS // 2 - 1, two, 0)
    step(qa, qb)
    step(qb, qa, True)


def skin_rows(q, m, rows, at, count, pairs):
    sums = []
    table = (iota((COLS, COLS // 2), 0) // 2 == iota((COLS, COLS // 2), 1)).astype(F32)
    for with_heat in (True, False):
        parts = []
        for j in range(4):
            value = m[GUARD + j * rows + at : GUARD + j * rows + at + count, :]
            if with_heat:
                value = value * q[GUARD + 16 * j * rows + at : GUARD + 16 * j * rows + at + count, :]
            pairs[0:count, :] = value
            parts.append(
                pairs[pl.ds(0, count // 2, stride=2), :] + pairs[pl.ds(1, count // 2, stride=2), :]
            )
        narrow = jnp.concatenate(parts, axis=1)
        sums.append(jnp.dot(narrow, table, precision=lax.Precision.HIGHEST, preferred_element_type=F32))
    return sums[0] / jnp.maximum(sums[1], 1.0)


def clear_guards(refs):
    for ref in refs:
        ref[0:GUARD, :] = jnp.zeros((GUARD, 128), F32)
        ref[ref.shape[0] - GUARD :, :] = jnp.zeros((GUARD, 128), F32)


def interval(
    sc, st, vn, ve, cd, wt, mk, sides, got_a, got_b, major, minor, atm, atm_top, out, sst,
    qa, qb, v, u, taps, m, atm_rows, grids, coef, force, ce, cw, cn, cs, cc, pairs,
):
    rows = EXT_ROWS
    lane8 = iota((8, 128), 1)
    is_fold = sc[0] == BLK - 1
    odd = sc[0] & 1
    clear_guards((qa, qb, v, u, taps, m, grids))
    for at in (0, 40):
        clear_rows(qa, 80, rows, at)
        clear_rows(v, 40, rows, at)
        clear_rows(u, 40, rows, at)
        clear_rows(taps, 40, rows, at)
        clear_rows(m, 5, rows, at)
    own_rows(st, vn, ve, cd, wt, mk, sides, ROWS, rows, 8, 0, qa, v, u, taps, m)

    def to_north(i):
        return 40 + i

    def to_south(i):
        return 7 - i

    def plain(msg, row_of):
        place_ghost(
            lambda j, n: msg[HEAD + j * PART + 8 * n : HEAD + j * PART + 8 * n + 8, :],
            lambda g: msg[8 * g : 8 * g + 8, :],
            row_of, rows, 0, qa, v, u, taps, m, False,
        )

    @pl.when(odd == 0)
    def _():
        plain(got_a, to_north)
        plain(got_b, to_south)

    @pl.when(odd == 1)
    def _():
        plain(got_a, to_south)

    @pl.when((odd == 1) & jnp.logical_not(is_fold))
    def _():
        plain(got_b, to_north)

    def fold(first_is_major):
        seam = sc[3]

        def load(j, n):
            at = HEAD + j * PART + 8 * n
            value = major[at : at + 8, :]
            if first_is_major == (j >= 2):
                at = HEAD + (j % 2) * PART + 8 * n
                second = lane8 + 128 * j > seam
                value = jnp.where(second if first_is_major else ~second, minor[at : at + 8, :], value)
            return value

        def corner(g):
            at = slice(8 * g, 8 * g + 8)
            one, two = (major, minor) if first_is_major else (minor, major)
            return jnp.where((lane8 & 15) < 6, one[at, :], two[at, :])

        place_ghost(load, corner, to_north, rows, 0, qa, v, u, taps, m, True)

    @pl.when(is_fold & (sc[3] >= 256))
    def _():
        fold(True)

    @pl.when(is_fold & (sc[3] < 256))
    def _():
        fold(False)

    lane16 = iota((16, 128), 1)

    def piece(ref, slot, f, part):
        if part < 2:
            return ref[pl.ds(10 * slot + 2 * f + part, 16, stride=CHUNK), :]
        side = pltpu.roll(ref[pl.ds(30, 16, stride=CHUNK), :], 128 - 4 - 8 * (5 * slot + f), axis=1)
        return jnp.where((lane16 < 4) | (lane16 >= 124), side, 0.0)

    def each(put):
        for f in range(5):
            for part in range(3):
                put(24 * f, slice(128 * part, 128 * part + 128), f, part)

    @pl.when(jnp.logical_not(is_fold))
    def _():
        def put(at, cols, f, part):
            far = piece(atm, 1, f, part)
            atm_rows[at : at + 4, cols] = far[12:16]
            atm_rows[at + 4 : at + 20, cols] = piece(atm, 0, f, part)
            atm_rows[at + 20 : at + 24, cols] = far[0:4]

        each(put)

    @pl.when(sc[0] == RELAY)
    def _():
        def put(at, cols, f, part):
            atm_rows[at + 20 : at + 24, cols] = piece(atm, 2, f, part)[0:4]

        each(put)

    @pl.when(is_fold)
    def _():
        def put(at, cols, f, part):
            atm_rows[at : at + 4, cols] = piece(atm_top, 0, f, part)[12:16]
            atm_rows[at + 4 : at + 20, cols] = piece(atm_top, 2, f, part)
            atm_rows[at + 20 : at + 24, cols] = piece(atm_top, 1, f, part)[0:4]

        each(put)

    src = iota((384, EXT_COLS), 0)
    dst = iota((384, EXT_COLS), 1)
    table = (src == jnp.where(dst < 576, dst // 2, dst // 2 + 64)).astype(F32)
    wide = jnp.dot(atm_rows[...], table, precision=lax.Precision.HIGHEST, preferred_element_type=F32)
    for f in range(5):
        for j in range(5):
            tile = wide[24 * f : 24 * f + 24, 128 * j : 128 * j + 128]
            base = GUARD + (5 * f + j) * 48
            grids[pl.ds(base, 24, stride=2), :] = tile
            grids[pl.ds(base + 1, 24, stride=2), :] = tile
    weights(is_fold, rows, 0, 0, 6, grids, v, u, taps, m, coef, force, ce, cw, cn, cs, cc)
    steps(rows, qa, qb, force, ce, cw, cn, cs, cc)
    for t in range(2):
        for k in range(LEVELS):
            for j in range(4):
                base = GUARD + (16 * j + 8 * t + k) * rows + 8
                out[t, k, :, 128 * j : 128 * j + 128] = qa[base : base + ROWS, :]
    result = skin_rows(qa, m, rows, 8, ROWS, pairs)
    sst[:, 0, :] = result[:, 0:128]
    sst[:, 1, :] = result[:, 128:256]


def place(b, l):
    return b * LON + l % LON


def body(temp_salt, east_vel, north_vel, land_mask, fluxes, remap_code, remap_weight, fold_source):
    axes = ("blk", "lon")
    arrays = (temp_salt, north_vel, east_vel, remap_code, remap_weight, land_mask)

    sds = lambda *shape: jax.ShapeDtypeStruct(shape, F32)
    sc, band = pl.pallas_call(
        combine_bands,
        grid=(1,),
        in_specs=[SCALARS, full((10, 32, 128))],
        out_specs=[SCALARS, full((5, 32, 128))],
        out_shape=[jax.ShapeDtypeStruct((8,), jnp.int32), sds(5, 32, 128)],
        compiler_params=limit(56),
        name="combine_bands",
    )(fold_source, fluxes.reshape(10, 32, 128))
    band_pairs = []
    for n in range(4):
        for blk in range(RELAY):
            band_pairs.append((place(blk + 1, n), place(blk, n)))
            band_pairs.append((place(blk, 12 + n), place(blk + 1, 12 + n)))
        band_pairs.append((place(BLK - 1, 15 - n), place(RELAY, n)))
    other = lax.ppermute(band, axes, band_pairs)
    top = lax.ppermute(band, axes, [(place(BLK - 1, n), place(RELAY, n)) for n in range(LON)])

    first, _ = lax.optimization_barrier((land_mask, band))
    specs, operands = [], []
    for x in (*arrays[:-1], first):
        lead = x.shape[:-2]
        for j in (0, 3):
            specs.append(at_block(lead + (ROWS, 128), (0,) * len(lead) + (0, j)))
            operands.append(x)
    to_west, to_east = pl.pallas_call(
        pack_columns,
        grid=(1,),
        in_specs=specs,
        out_specs=[full((3, ROWS, 128))] * 2,
        out_shape=[sds(3, ROWS, 128)] * 2,
        compiler_params=limit(56),
        name="pack_columns",
    )(*operands)
    from_west = lax.ppermute(to_east, "lon", [(i, (i + 1) % LON) for i in range(LON)])
    from_east = lax.ppermute(to_west, "lon", [((i + 1) % LON, i) for i in range(LON)])

    first, _, other, top, case = lax.optimization_barrier((land_mask, to_west, other, top, sc[5]))
    specs, operands = [SCALARS], [sc]
    for x in (*arrays[:-1], first):
        lead = x.shape[:-2]
        for j in (0, 3):
            specs.append(at_block(lead + (8, COLS), (0,) * len(lead) + (j, 0)))
            operands.append(x)
    sizes = (WHOLE, WHOLE, HALF, HALF)
    *messages, window = pl.pallas_call(
        pack_rows,
        grid=(1,),
        in_specs=specs,
        out_specs=[full((n, 128)) for n in sizes] + [full((HEAD, 128))],
        out_shape=[sds(n, 128) for n in sizes] + [sds(HEAD, 128)],
        scratch_shapes=[VMEM((4 * SLABS * 8, 128), F32)] * 2,
        compiler_params=limit(56),
        name="pack_rows",
    )(*operands)
    sides, msg_a, msg_b, low, high = pl.pallas_call(
        pack_corners,
        grid=(1,),
        in_specs=[SCALARS, full((3, ROWS, 128)), full((3, ROWS, 128)), full((HEAD, 128))]
        + [pl.BlockSpec(memory_space=pl.ANY)] * 4,
        out_specs=[full((SLABS * ROWS, 128))] + [full((HEAD, 128))] * 4,
        out_shape=[sds(SLABS * ROWS, 128)] + [sds(n, 128) for n in sizes],
        input_output_aliases={4: 1, 5: 2, 6: 3, 7: 4},
        compiler_params=limit(56),
        name="pack_corners",
    )(sc, from_west, from_east, window, *messages)

    on_chip = [(place(i, n), place(i ^ 1, n)) for i in range(BLK) for n in range(LON)]
    across = []
    for i in range(1, BLK - 1, 2):
        for n in range(LON):
            across += [(place(i, n), place(i + 1, n)), (place(i + 1, n), place(i, n))]
    got_a = lax.ppermute(msg_a, axes, on_chip)
    got_b = lax.ppermute(msg_b, axes, across)

    def branch(shift, second_half):
        top = BLK - 1
        one = [(place(top, n), place(top, (shift - n) % LON)) for n in range(LON)]
        two = [(place(top, n), place(top, (shift - 1 - n) % LON)) for n in range(LON)]

        def send(whole, low, high):
            if second_half:
                return lax.ppermute(whole, axes, one), lax.ppermute(high, axes, two)
            return lax.ppermute(whole, axes, two), lax.ppermute(low, axes, one)

        return send

    got_f = lax.switch(
        case,
        [branch(shift, half) for shift in range(LON) for half in range(2)],
        msg_b,
        low,
        high,
    )

    def spread(band, other, top):
        chunks = pl.pallas_call(
            chunk_bands,
            grid=(1,),
            in_specs=[SCALARS] + [full((5, 32, 128))] * 3,
            out_specs=full((LON * CHUNK, 128)),
            out_shape=sds(LON * CHUNK, 128),
            scratch_shapes=[VMEM((160, 128), F32)] * 4,
            compiler_params=limit(8),
            name="chunk_bands",
        )(sc, band, other, top)
        return lax.all_to_all(chunks, "lon", split_axis=0, concat_axis=0, tiled=True)

    later, _ = lax.optimization_barrier((band, got_f[1]))
    atm = lax.cond(
        lax.axis_index("blk") == BLK - 1, lambda *x: jnp.zeros((LON * CHUNK, 128), F32), spread, later, other, top
    )
    atm_top = lax.ppermute(atm, axes, [(place(RELAY, n), place(BLK - 1, n)) for n in range(LON)])

    ext = lambda n: VMEM((GUARD * 2 + n * EXT_ROWS, 128), F32)
    state, skin = pl.pallas_call(
        interval,
        grid=(1,),
        in_specs=[SCALARS] + [full(x.shape) for x in (*arrays, sides, got_a, got_b, *got_f, atm, atm_top)],
        out_specs=[full((2, LEVELS, ROWS, COLS)), full((LON, 2, 128))],
        out_shape=[sds(2, LEVELS, ROWS, COLS), sds(LON, 2, 128)],
        scratch_shapes=[ext(80), ext(80), ext(40), ext(40), ext(40), ext(5), VMEM((120, 384), F32), ext(25)]
        + [VMEM((360, 128), F32), ext(25)]
        + [ext(40)] * 5
        + [VMEM((ROWS, 128), F32)],
        compiler_params=limit(36),
        name="interval",
    )(sc, *arrays, sides, got_a, got_b, *got_f, atm, atm_top)
    bands = lax.all_to_all(skin, "lon", split_axis=0, concat_axis=0, tiled=True)
    return state, bands.reshape(1, LON * 256)


def solution(mesh):
    placed = (
        P(None, None, "blk", "lon"),
        P(None, "blk", "lon"),
        P(None, "blk", "lon"),
        P("blk", "lon"),
        P(None, ("blk", "lon"), None),
        P(None, "blk", "lon"),
        P(None, "blk", "lon"),
        P("lon"),
    )
    return jax.shard_map(
        body,
        mesh=mesh,
        in_specs=placed,
        out_specs=(P(None, None, "blk", "lon"), P(("blk", "lon"), None)),
        check_vma=False,
    )
```

```python
import jax
import jax.numpy as jnp
from jax import lax
from jax.experimental import pallas as pl
from jax.experimental.pallas import tpu as pltpu
from jax.sharding import PartitionSpec as P

STEPS = 6
F32 = jnp.float32
LEVELS = 8
BLK, LON = 8, 16
ROWS, COLS = 32, 512
EXT_ROWS, EXT_COLS = 48, 640
NX = 8192
SLABS = 41
PART = 232
HEAD = 32
WHOLE = HEAD + 4 * PART
HALF = HEAD + 2 * PART
VMEM = pltpu.VMEM
SMEM = pltpu.SMEM


def limit(mib):
    return pltpu.CompilerParams(vmem_limit_bytes=mib * 1024 * 1024)


RELAY = BLK - 2
CHUNK = 32


def iota(shape, dim):
    return lax.broadcasted_iota(jnp.int32, shape, dim)


def full(shape):
    return pl.BlockSpec(shape, lambda i: (0,) * len(shape))


def at_block(shape, place):
    return pl.BlockSpec(shape, lambda i: place)


SCALARS = pl.BlockSpec(memory_space=SMEM)


def combine_bands(fold, flux, sc, band):
    l = lax.axis_index("lon")
    mirror = lax.rem(fold[0] + COLS * l, NX)
    sc[0] = lax.axis_index("blk")
    sc[1] = l
    sc[2] = mirror // COLS
    sc[3] = lax.rem(mirror, COLS)
    sc[4] = (mirror - 1) // 2
    sc[5] = mirror // 256
    sc[6] = 0
    sc[7] = 0
    band[0] = flux[0]
    band[1] = flux[1] + flux[2] + flux[3] - 0.33 * flux[5]
    band[2] = flux[4] + flux[5] + flux[6] + flux[7]
    band[3] = flux[8]
    band[4] = flux[9]


def pack_columns(st0, st3, vn0, vn3, ve0, ve3, cd0, cd3, wt0, wt3, mk0, mk3, to_west, to_east):
    lane = iota((ROWS, 128), 1)

    def pack(groups, shift, out):
        for g, tiles in enumerate(groups):
            acc = jnp.zeros((ROWS, 128), F32)
            for j, tile in enumerate(tiles):
                moved = pltpu.roll(tile().astype(F32), (8 * j + shift) % 128, axis=1)
                acc = jnp.where((lane >= 8 * j) & (lane < 8 * j + 8), moved, acc)
            out[g] = acc

    def groups(st, vn, ve, cd, wt, mk):
        first = [lambda t=t, k=k: st[t, k] for t in range(2) for k in range(LEVELS)]
        second = [lambda k=k: vn[k] for k in range(LEVELS)] + [lambda k=k: ve[k] for k in range(LEVELS)]
        third = [lambda k=k: cd[k] for k in range(4)] + [lambda k=k: wt[k] for k in range(4)] + [lambda: mk[...]]
        return [first, second, third]

    pack(groups(st0, vn0, ve0, cd0, wt0, mk0), 0, to_west)
    pack(groups(st3, vn3, ve3, cd3, wt3, mk3), 6, to_east)


def chunk_bands(sc, band, other, top, out, own, held, relayed, turned):
    own[...] = band[...].reshape(160, 128)
    held[...] = other[...].reshape(160, 128)
    relayed[...] = top[...].reshape(160, 128)
    is_relay = sc[0] == RELAY

    @pl.when(is_relay & (sc[1] < 4))
    def _():
        pole = sc[4]
        pq, pr = pole // 128, pole % 128
        lane8 = iota((8, 128), 1)
        index = (pr - lane8) & 127
        for n in range(20):
            turned[8 * n : 8 * n + 8, :] = jnp.take_along_axis(held[8 * n : 8 * n + 8, :], index, axis=1)
        lane1 = iota((1, 128), 1)

        def one(row, carry):
            near = (pq - row) & 31
            far = (pq - row - 1) & 31
            for f in range(5):
                a = turned[pl.ds(32 * f + near, 1), :]
                b = turned[pl.ds(32 * f + far, 1), :]
                held[pl.ds(32 * f + row, 1), :] = jnp.where(lane1 <= pr, a, b)
            return carry

        lax.fori_loop(0, 32, one, 0)

    lane = iota((16, 128), 1)
    sides = jnp.zeros((16, 128), F32)
    for slot, src in enumerate((own, held, relayed)):
        for f in range(5):
            even = src[pl.ds(32 * f, 16, stride=2), :]
            odd = src[pl.ds(32 * f + 1, 16, stride=2), :]
            out[pl.ds(10 * slot + 2 * f, 16, stride=CHUNK), :] = even
            out[pl.ds(10 * slot + 2 * f + 1, 16, stride=CHUNK), :] = odd
            side = jnp.where(lane < 64, pltpu.roll(even, 15, axis=0), pltpu.roll(odd, 1, axis=0))
            at = 8 * (5 * slot + f)
            sides = jnp.where((lane >= at) & (lane < at + 8), pltpu.roll(side, at + 4, axis=1), sides)
    out[pl.ds(30, 16, stride=CHUNK), :] = sides
    out[pl.ds(31, 16, stride=CHUNK), :] = jnp.zeros((16, 128), F32)


def slot_lanes(lane8, slot):
    return (lane8 >= 16 * slot) & (lane8 < 16 * slot + 12)


def fold_lanes(sc, lane8):
    rq, rr = sc[3] // 128, sc[3] % 128
    return rq, (rr - lane8) & 127, lane8 <= rr


def pack_rows(
    sc, st_s, st_n, vn_s, vn_n, ve_s, ve_n, cd_s, cd_n, wt_s, wt_n, mk_s, mk_n,
    msg_a, msg_b, low, high, window, south, north,
):
    lane8 = iota((8, 128), 1)

    def stage(dst, st, vn, ve, cd, wt):
        for j in range(4):
            cols = slice(128 * j, 128 * j + 128)

            def put(s, value):
                dst[(j * SLABS + s) * 8 : (j * SLABS + s) * 8 + 8, :] = value

            for k in range(LEVELS):
                put(k, st[0, k, :, cols])
                put(8 + k, st[1, k, :, cols])
                put(16 + k, vn[k, :, cols])
                put(24 + k, ve[k, :, cols])
            for k in range(4):
                put(32 + k, cd[k, :, cols].astype(F32))
                put(36 + k, wt[k, :, cols])

    stage(south, st_s, vn_s, ve_s, cd_s, wt_s)
    stage(north, st_n, vn_n, ve_n, cd_n, wt_n)
    for j in range(4):
        base = (j * SLABS + 40) * 8
        cols = slice(128 * j, 128 * j + 128)
        south[base : base + 8, :] = mk_s[:, cols].astype(F32)
        flipped = mk_n[:, cols].astype(F32)
        for i in range(8):
            north[base + i : base + i + 1, :] = flipped[7 - i : 8 - i]

    def loader(edge, is_north, n):
        if n == 28:
            return lambda j: edge[pl.ds((j * SLABS + 40) * 8, 8), :]
        i, rt = n // 5, n % 5
        row = 7 - i if is_north else i
        return lambda j: edge[pl.ds((j * SLABS + rt * 8) * 8 + row, 8, stride=8), :]

    def build(put, edge, is_north):
        for n in range(29):
            load = loader(edge, is_north, n)
            for j in range(4):
                put(j, n, load(j))

    def put_a(j, n, tile):
        at = HEAD + j * PART + 8 * n
        msg_a[at : at + 8, :] = tile

    def put_b(j, n, tile):
        at = HEAD + j * PART + 8 * n
        msg_b[at : at + 8, :] = tile

    parity = sc[0] & 1
    window[...] = jnp.zeros_like(window)

    @pl.when(parity == 0)
    def _():
        build(put_a, north, True)
        build(put_b, south, False)

    @pl.when(parity == 1)
    def _():
        build(put_a, south, False)

    @pl.when((parity == 1) & (sc[0] < BLK - 1))
    def _():
        build(put_b, north, True)

    @pl.when(sc[0] == BLK - 1)
    def _():
        rq, index, near = fold_lanes(sc, lane8)
        order = [rq, (rq - 1) & 3, (rq - 2) & 3, (rq - 3) & 3]
        corner = [jnp.zeros((8, 128), F32) for _ in range(4)]
        for n in range(29):
            load = loader(north, True, n)
            g = [jnp.take_along_axis(load(j), index, axis=1) for j in order]
            for j in range(4):
                tile = jnp.where(near, g[j], g[(j + 1) % 4])
                put_b(j, n, tile)
                at = HEAD + (j % 2) * PART + 8 * n
                (low, high)[j // 2][at : at + 8, :] = tile
            below = jnp.where(rq == 0, 0.0, g[1])
            above = jnp.where(rq == 3, 0.0, g[3])
            fifth = jnp.where(lane8 < 64, jnp.where(near, g[0], below), jnp.where(near, above, g[0]))
            moved = pltpu.roll(fifth, (6 + 16 * (n % 8)) % 128, axis=1)
            corner[n // 8] = jnp.where(slot_lanes(lane8, n % 8), moved, corner[n // 8])
        for v in range(4):
            window[8 * v : 8 * v + 8, :] = corner[v]


def pack_corners(
    sc, from_west, from_east, window, a_in, b_in, low_in, high_in, sides, corner_a, corner_b, corner_low, corner_high
):
    lane = iota((ROWS, 128), 1)
    for s in range(SLABS):
        g, j = s // 16, s % 16
        east = pltpu.roll(from_east[g], (128 - 8 * j) % 128, axis=1)
        west = pltpu.roll(from_west[g], (122 - 8 * j) % 128, axis=1)
        sides[ROWS * s : ROWS * s + ROWS, :] = jnp.where(lane < 6, east, jnp.where(lane >= 122, west, 0.0))
    lane8 = iota((8, 128), 1)

    def build(dst, is_north, turn):
        corner = [window[8 * v : 8 * v + 8, :] if turn else jnp.zeros((8, 128), F32) for v in range(4)]
        if turn:
            rq, index, near = fold_lanes(sc, lane8)
            low = (lane8 < 64) & (rq == 0) & ~near
            high = (lane8 >= 64) & (rq == 3) & near
        for n in range(29):
            if n < 28:
                i, rt = n // 5, n % 5
                row = 31 - i if is_north else i
                fifth = sides[pl.ds(rt * 8 * ROWS + row, 8, stride=ROWS), :]
            else:
                mask = sides[40 * ROWS + (24 if is_north else 0) : 40 * ROWS + (32 if is_north else 8), :]
                fifth = jnp.concatenate([mask[7 - i : 8 - i] for i in range(8)], axis=0) if is_north else mask
            if turn:
                fifth = jnp.where(low | high, jnp.take_along_axis(fifth, index, axis=1), 0.0)
            moved = pltpu.roll(fifth, (6 + 16 * (n % 8)) % 128, axis=1)
            if turn:
                corner[n // 8] = corner[n // 8] + jnp.where(slot_lanes(lane8, n % 8), moved, 0.0)
            else:
                corner[n // 8] = jnp.where(slot_lanes(lane8, n % 8), moved, corner[n // 8])
        for v in range(4):
            dst[8 * v : 8 * v + 8, :] = corner[v]

    parity = sc[0] & 1

    @pl.when(parity == 0)
    def _():
        build(corner_a, True, False)
        build(corner_b, False, False)

    @pl.when(parity == 1)
    def _():
        build(corner_a, False, False)

    @pl.when((parity == 1) & (sc[0] < BLK - 1))
    def _():
        build(corner_b, True, False)

    @pl.when(sc[0] == BLK - 1)
    def _():
        build(corner_b, True, True)
        corner_low[...] = corner_b[...]
        corner_high[...] = corner_b[...]


GUARD = 8


def shifted_lanes(tiles, by, lane8):
    count = len(tiles)
    rolled = [pltpu.roll(t, (-by) % 128, axis=1) for t in tiles]
    if by > 0:
        return [jnp.where(lane8 >= 128 - by, rolled[(j + 1) % count], rolled[j]) for j in range(count)]
    return [jnp.where(lane8 < -by, rolled[(j - 1) % count], rolled[j]) for j in range(count)]


def place_ghost(load, corner, row_of, rows, old, q, v, u, taps, m, turned):
    lane8 = iota((8, 128), 1)
    edge_lanes = (lane8 < 6) | (lane8 >= 122)
    row8 = iota((8, 128), 0)
    for n in range(29):
        tiles = [load(j, n) for j in range(4)]
        fifth = pltpu.roll(corner(n // 8), (256 - 6 - 16 * (n % 8)) % 128, axis=1)
        tiles.append(jnp.where(edge_lanes, fifth, 0.0))
        if n == 28:
            for j in range(5):
                for i in range(6):
                    m[pl.ds(GUARD + j * rows + row_of(i), 1), :] = tiles[j][i : i + 1]
            continue
        i, rt = n // 5, n % 5
        for j in range(5):
            tile = tiles[j]
            if turned and rt in (2, 3):
                tile = -tile
            if turned and rt == 4:
                tile = jnp.where(row8 < 4, 8.0 - tile, tile)
            if rt < 2:
                ref, block = q, j * 16 + 8 * rt
                at = old + GUARD + block * rows + row_of(i)
            else:
                ref = (v, u, taps)[rt - 2]
                at = GUARD + j * 8 * rows + row_of(i)
            ref[pl.ds(at, 8, stride=rows), :] = tile


def own_rows(st, vn, ve, cd, wt, mk, sides, count, rows, at, side_row, q, v, u, taps, m):
    def put(ref, block, value):
        ref[pl.ds(GUARD + block * rows + at, count), :] = value

    def side(s):
        return sides[pl.ds(ROWS * s + side_row, count), :]

    for j in range(5):
        cols = slice(128 * j, 128 * j + 128)
        for t in range(2):
            for k in range(LEVELS):
                s = 8 * t + k
                put(q, j * 16 + s, st[t, k, :, cols] if j < 4 else side(s))
        for k in range(LEVELS):
            put(v, j * 8 + k, vn[k, :, cols] if j < 4 else side(16 + k))
            put(u, j * 8 + k, ve[k, :, cols] if j < 4 else side(24 + k))
        for k in range(4):
            put(taps, j * 8 + k, cd[k, :, cols].astype(F32) if j < 4 else side(32 + k))
            put(taps, j * 8 + 4 + k, wt[k, :, cols] if j < 4 else side(36 + k))
        put(m, j, mk[:, cols].astype(F32) if j < 4 else side(40))


def clear_rows(ref, blocks, rows, at, base=0):
    for b in range(blocks):
        ref[pl.ds(base + GUARD + b * rows + at, 8), :] = jnp.zeros((8, 128), F32)


def weights(is_fold, rows, first, low, count, doubled, v, u, taps, m, coef, force, ce, cw, cn, cs, cc):
    lane8 = iota((8, 128), 1)
    row8 = iota((8, 128), 0)

    def one(n):
        r = 8 * (low + n)
        ext_row = row8 + (first + r)

        def read(ref, block, shift=0):
            return ref[pl.ds(GUARD + block * rows + r + shift, 8), :]

        up_ok = jnp.where(is_fold & (ext_row >= 38) & (ext_row < 40), 0.0, 1.0)
        down_ok = jnp.where(is_fold & (ext_row >= 40) & (ext_row < 42), 0.0, 1.0)
        for j in range(5):
            w = [read(taps, 8 * j + 4 + t) for t in range(4)]
            c = [read(taps, 8 * j + t) for t in range(4)]
            wsum = w[0] + w[1] + w[2] + w[3]
            inv = 1.0 / jnp.where(wsum > 0.0, wsum, 1.0)
            w = [x * inv for x in w]
            for code in range(9):
                hit = [jnp.where(c[t] == float(code), w[t], 0.0) for t in range(4)]
                total = (hit[0] + hit[1]) + (hit[2] + hit[3])
                if code < 3 and n == 5:
                    total = total * down_ok
                if code >= 6 and n == 4:
                    total = total * up_ok
                coef[8 * (5 * code + j) : 8 * (5 * code + j) + 8, :] = total
        fields = []
        for f in range(5):
            total = None
            for dy in (-1, 0, 1):
                at = [GUARD + (5 * f + j) * 48 + first + r + 2 * dy for j in range(5)]
                grid = [doubled[pl.ds(a, 8), :] for a in at]
                for dx in (-1, 0, 1):
                    code = 3 * (dy + 1) + dx + 1
                    moved = grid if dx == 0 else shifted_lanes(grid, 2 * dx, lane8)
                    part = [
                        moved[j] * coef[8 * (5 * code + j) : 8 * (5 * code + j) + 8, :] for j in range(5)
                    ]
                    total = part if total is None else [a + b for a, b in zip(total, part)]
            fields.append(total)
        mc = [read(m, j) for j in range(5)]
        me, mw = shifted_lanes(mc, 1, lane8), shifted_lanes(mc, -1, lane8)
        oe = [mc[j] * me[j] for j in range(5)]
        ow = [mc[j] * mw[j] for j in range(5)]
        on = [mc[j] * read(m, j, 1) for j in range(5)]
        os = [mc[j] * read(m, j, -1) for j in range(5)]

        def put(ref, block, value):
            ref[pl.ds(GUARD + block * rows + r, 8), :] = value

        top, mid = [], []
        for j in range(5):
            sw, heat, fresh, tx, ty = (fields[f][j] for f in range(5))
            kv = 0.05 + 0.04 * jnp.sqrt(tx * tx + ty * ty + 0.01)
            top.append(mc[j] * kv)
            mid.append(0.05 * mc[j])
            put(force, j, 0.05 * mc[j] * sw)
            put(force, 5 + j, 0.05 * mc[j] * heat)
            put(force, 10 + j, -0.05 * mc[j] * fresh)
            put(force, 15 + j, top[j])
            put(force, 20 + j, mid[j])
        over = is_fold & (ext_row >= 40)
        for k in range(LEVELS):
            uc = [read(u, 8 * j + k) for j in range(5)]
            west = shifted_lanes(uc, -1, lane8)
            east = shifted_lanes(uc, 1, lane8) if n == 5 else None
            for j in range(5):
                vc = read(v, 8 * j + k)
                et, wt, vt, vb = uc[j], west[j], vc, read(v, 8 * j + k, -1)
                if n == 5:
                    et, wt = jnp.where(over, east[j], et), jnp.where(over, uc[j], wt)
                    vt, vb = jnp.where(over, read(v, 8 * j + k, 1), vt), jnp.where(over, vc, vb)
                put(ce, 8 * j + k, oe[j] * (0.08 - jnp.minimum(et, 0.0)))
                put(cw, 8 * j + k, ow[j] * (0.08 + jnp.maximum(wt, 0.0)))
                put(cn, 8 * j + k, on[j] * (0.08 - jnp.minimum(vt, 0.0)))
                put(cs, 8 * j + k, os[j] * (0.08 + jnp.maximum(vb, 0.0)))
                centre = 1.0 - oe[j] * (0.08 + jnp.maximum(et, 0.0)) - ow[j] * (0.08 - jnp.minimum(wt, 0.0))
                centre = centre - on[j] * (0.08 + jnp.maximum(vt, 0.0)) - os[j] * (0.08 - jnp.minimum(vb, 0.0))
                if k == 0:
                    centre = centre - top[j]
                elif k == 1:
                    centre = centre - top[j] - mid[j]
                elif k == LEVELS - 1:
                    centre = centre - mid[j]
                else:
                    centre = centre - 2.0 * mid[j]
                put(cc, 8 * j + k, centre)

    for n in range(count):
        one(n)


def steps(rows, qa, qb, force, ce, cw, cn, cs, cc):
    lane8 = iota((8, 128), 1)

    def one(q, p, r, width):
        def read(ref, block, shift=0):
            at = GUARD + block * rows + r + shift
            return ref[at : at + 8, :]

        def state(t, k, j, shift=0):
            return read(q, 16 * j + 8 * t + k, shift)

        mid = [read(force, 20 + j) for j in range(width)]
        here = [[state(t, 0, j) for j in range(5)] for t in range(2)]
        below = [None, None]
        for k in range(LEVELS):
            weight = [[read(ref, 8 * j + k) for j in range(width)] for ref in (cc, ce, cw, cn, cs)]
            for t in range(2):
                above = here[t]
                after = [state(t, k + 1, j) for j in range(5)] if k < LEVELS - 1 else None
                east, west = shifted_lanes(above, 1, lane8), shifted_lanes(above, -1, lane8)
                for j in range(width):
                    total = weight[0][j] * above[j] + weight[1][j] * east[j]
                    total = total + weight[2][j] * west[j]
                    total = total + weight[3][j] * state(t, k, j, 1)
                    total = total + weight[4][j] * state(t, k, j, -1)
                    if k == 0:
                        total = total + read(force, 15 + j) * after[j]
                    elif k == 1:
                        total = total + read(force, 15 + j) * below[t][j] + mid[j] * after[j]
                    elif k == LEVELS - 1:
                        total = total + mid[j] * below[t][j]
                    else:
                        total = total + mid[j] * (below[t][j] + after[j])
                    if t == 0:
                        total = total + (0.5 ** (k + 1)) * read(force, j)
                        if k == 0:
                            total = total + read(force, 5 + j)
                    elif k == 0:
                        total = total + read(force, 10 + j)
                    at = GUARD + (16 * j + 8 * t + k) * rows + r
                    p[at : at + 8, :] = total
                below[t], here[t] = above, after

    def step(q, p, last=False):
        for n in range(1, 5) if last else range(6):
            one(q, p, 8 * n, 4 if last else 5)

    def two(i, carry):
        step(qa, qb)
        step(qb, qa)
        return carry

    lax.fori_loop(0, STEPS // 2 - 1, two, 0)
    step(qa, qb)
    step(qb, qa, True)


def skin_rows(q, m, rows, at, count, pairs):
    sums = []
    table = (iota((COLS, COLS // 2), 0) // 2 == iota((COLS, COLS // 2), 1)).astype(F32)
    for with_heat in (True, False):
        parts = []
        for j in range(4):
            value = m[GUARD + j * rows + at : GUARD + j * rows + at + count, :]
            if with_heat:
                value = value * q[GUARD + 16 * j * rows + at : GUARD + 16 * j * rows + at + count, :]
            pairs[0:count, :] = value
            parts.append(
                pairs[pl.ds(0, count // 2, stride=2), :] + pairs[pl.ds(1, count // 2, stride=2), :]
            )
        narrow = jnp.concatenate(parts, axis=1)
        sums.append(jnp.dot(narrow, table, precision=lax.Precision.HIGHEST, preferred_element_type=F32))
    return sums[0] / jnp.maximum(sums[1], 1.0)


def clear_guards(refs):
    for ref in refs:
        ref[0:GUARD, :] = jnp.zeros((GUARD, 128), F32)
        ref[ref.shape[0] - GUARD :, :] = jnp.zeros((GUARD, 128), F32)


def interval(
    sc, st, vn, ve, cd, wt, mk, sides, got_a, got_b, major, minor, atm, atm_top, out, sst,
    qa, qb, v, u, taps, m, atm_rows, grids, coef, force, ce, cw, cn, cs, cc, pairs,
):
    rows = EXT_ROWS
    lane8 = iota((8, 128), 1)
    is_fold = sc[0] == BLK - 1
    odd = sc[0] & 1
    clear_guards((qa, qb, v, u, taps, m, grids))
    for at in (0, 40):
        clear_rows(qa, 80, rows, at)
        clear_rows(v, 40, rows, at)
        clear_rows(u, 40, rows, at)
        clear_rows(taps, 40, rows, at)
        clear_rows(m, 5, rows, at)
    own_rows(st, vn, ve, cd, wt, mk, sides, ROWS, rows, 8, 0, qa, v, u, taps, m)

    def to_north(i):
        return 40 + i

    def to_south(i):
        return 7 - i

    def plain(msg, row_of):
        place_ghost(
            lambda j, n: msg[HEAD + j * PART + 8 * n : HEAD + j * PART + 8 * n + 8, :],
            lambda g: msg[8 * g : 8 * g + 8, :],
            row_of, rows, 0, qa, v, u, taps, m, False,
        )

    @pl.when(odd == 0)
    def _():
        plain(got_a, to_north)
        plain(got_b, to_south)

    @pl.when(odd == 1)
    def _():
        plain(got_a, to_south)

    @pl.when((odd == 1) & jnp.logical_not(is_fold))
    def _():
        plain(got_b, to_north)

    def fold(first_is_major):
        seam = sc[3]

        def load(j, n):
            at = HEAD + j * PART + 8 * n
            value = major[at : at + 8, :]
            if first_is_major == (j >= 2):
                at = HEAD + (j % 2) * PART + 8 * n
                second = lane8 + 128 * j > seam
                value = jnp.where(second if first_is_major else ~second, minor[at : at + 8, :], value)
            return value

        def corner(g):
            at = slice(8 * g, 8 * g + 8)
            one, two = (major, minor) if first_is_major else (minor, major)
            return jnp.where((lane8 & 15) < 6, one[at, :], two[at, :])

        place_ghost(load, corner, to_north, rows, 0, qa, v, u, taps, m, True)

    @pl.when(is_fold & (sc[3] >= 256))
    def _():
        fold(True)

    @pl.when(is_fold & (sc[3] < 256))
    def _():
        fold(False)

    lane16 = iota((16, 128), 1)

    def piece(ref, slot, f, part):
        if part < 2:
            return ref[pl.ds(10 * slot + 2 * f + part, 16, stride=CHUNK), :]
        side = pltpu.roll(ref[pl.ds(30, 16, stride=CHUNK), :], 128 - 4 - 8 * (5 * slot + f), axis=1)
        return jnp.where((lane16 < 4) | (lane16 >= 124), side, 0.0)

    def each(put):
        for f in range(5):
            for part in range(3):
                put(24 * f, slice(128 * part, 128 * part + 128), f, part)

    @pl.when(jnp.logical_not(is_fold))
    def _():
        def put(at, cols, f, part):
            far = piece(atm, 1, f, part)
            atm_rows[at : at + 4, cols] = far[12:16]
            atm_rows[at + 4 : at + 20, cols] = piece(atm, 0, f, part)
            atm_rows[at + 20 : at + 24, cols] = far[0:4]

        each(put)

    @pl.when(sc[0] == RELAY)
    def _():
        def put(at, cols, f, part):
            atm_rows[at + 20 : at + 24, cols] = piece(atm, 2, f, part)[0:4]

        each(put)

    @pl.when(is_fold)
    def _():
        def put(at, cols, f, part):
            atm_rows[at : at + 4, cols] = piece(atm_top, 0, f, part)[12:16]
            atm_rows[at + 4 : at + 20, cols] = piece(atm_top, 2, f, part)
            atm_rows[at + 20 : at + 24, cols] = piece(atm_top, 1, f, part)[0:4]

        each(put)

    src = iota((384, EXT_COLS), 0)
    dst = iota((384, EXT_COLS), 1)
    table = (src == jnp.where(dst < 576, dst // 2, dst // 2 + 64)).astype(F32)
    wide = jnp.dot(atm_rows[...], table, precision=lax.Precision.HIGHEST, preferred_element_type=F32)
    for f in range(5):
        for j in range(5):
            tile = wide[24 * f : 24 * f + 24, 128 * j : 128 * j + 128]
            base = GUARD + (5 * f + j) * 48
            grids[pl.ds(base, 24, stride=2), :] = tile
            grids[pl.ds(base + 1, 24, stride=2), :] = tile
    weights(is_fold, rows, 0, 0, 6, grids, v, u, taps, m, coef, force, ce, cw, cn, cs, cc)
    steps(rows, qa, qb, force, ce, cw, cn, cs, cc)
    for t in range(2):
        for k in range(LEVELS):
            for j in range(4):
                base = GUARD + (16 * j + 8 * t + k) * rows + 8
                out[t, k, :, 128 * j : 128 * j + 128] = qa[base : base + ROWS, :]
    result = skin_rows(qa, m, rows, 8, ROWS, pairs)
    sst[:, 0, :] = result[:, 0:128]
    sst[:, 1, :] = result[:, 128:256]


def place(b, l):
    return b * LON + l % LON


def body(temp_salt, east_vel, north_vel, land_mask, fluxes, remap_code, remap_weight, fold_source):
    axes = ("blk", "lon")
    arrays = (temp_salt, north_vel, east_vel, remap_code, remap_weight, land_mask)

    sds = lambda *shape: jax.ShapeDtypeStruct(shape, F32)
    specs, operands = [], []
    for x in arrays:
        lead = x.shape[:-2]
        for j in (0, 3):
            specs.append(at_block(lead + (ROWS, 128), (0,) * len(lead) + (0, j)))
            operands.append(x)
    to_west, to_east = pl.pallas_call(
        pack_columns,
        grid=(1,),
        in_specs=specs,
        out_specs=[full((3, ROWS, 128))] * 2,
        out_shape=[sds(3, ROWS, 128)] * 2,
        compiler_params=limit(56),
        name="pack_columns",
    )(*operands)
    from_west = lax.ppermute(to_east, "lon", [(i, (i + 1) % LON) for i in range(LON)])
    from_east = lax.ppermute(to_west, "lon", [((i + 1) % LON, i) for i in range(LON)])

    after_columns, _ = lax.optimization_barrier((fluxes, to_west))
    sc, band = pl.pallas_call(
        combine_bands,
        grid=(1,),
        in_specs=[SCALARS, full((10, 32, 128))],
        out_specs=[SCALARS, full((5, 32, 128))],
        out_shape=[jax.ShapeDtypeStruct((8,), jnp.int32), sds(5, 32, 128)],
        compiler_params=limit(56),
        name="combine_bands",
    )(fold_source, after_columns.reshape(10, 32, 128))
    band_pairs = []
    for n in range(4):
        for blk in range(RELAY):
            band_pairs.append((place(blk + 1, n), place(blk, n)))
            band_pairs.append((place(blk, 12 + n), place(blk + 1, 12 + n)))
        band_pairs.append((place(BLK - 1, 15 - n), place(RELAY, n)))
    other = lax.ppermute(band, axes, band_pairs)
    top = lax.ppermute(band, axes, [(place(BLK - 1, n), place(RELAY, n)) for n in range(LON)])


    first, _, case = lax.optimization_barrier((land_mask, band, sc[5]))
    specs, operands = [SCALARS], [sc]
    for x in (*arrays[:-1], first):
        lead = x.shape[:-2]
        for j in (0, 3):
            specs.append(at_block(lead + (8, COLS), (0,) * len(lead) + (j, 0)))
            operands.append(x)
    sizes = (WHOLE, WHOLE, HALF, HALF)
    *messages, window = pl.pallas_call(
        pack_rows,
        grid=(1,),
        in_specs=specs,
        out_specs=[full((n, 128)) for n in sizes] + [full((HEAD, 128))],
        out_shape=[sds(n, 128) for n in sizes] + [sds(HEAD, 128)],
        scratch_shapes=[VMEM((4 * SLABS * 8, 128), F32)] * 2,
        compiler_params=limit(56),
        name="pack_rows",
    )(*operands)
    window, other, top = lax.optimization_barrier((window, other, top))
    sides, msg_a, msg_b, low, high = pl.pallas_call(
        pack_corners,
        grid=(1,),
        in_specs=[SCALARS, full((3, ROWS, 128)), full((3, ROWS, 128)), full((HEAD, 128))]
        + [pl.BlockSpec(memory_space=pl.ANY)] * 4,
        out_specs=[full((SLABS * ROWS, 128))] + [full((HEAD, 128))] * 4,
        out_shape=[sds(SLABS * ROWS, 128)] + [sds(n, 128) for n in sizes],
        input_output_aliases={4: 1, 5: 2, 6: 3, 7: 4},
        compiler_params=limit(56),
        name="pack_corners",
    )(sc, from_west, from_east, window, *messages)

    on_chip = [(place(i, n), place(i ^ 1, n)) for i in range(BLK) for n in range(LON)]
    across = []
    for i in range(1, BLK - 1, 2):
        for n in range(LON):
            across += [(place(i, n), place(i + 1, n)), (place(i + 1, n), place(i, n))]
    got_a = lax.ppermute(msg_a, axes, on_chip)
    got_b = lax.ppermute(msg_b, axes, across)

    def branch(shift, second_half):
        top = BLK - 1
        one = [(place(top, n), place(top, (shift - n) % LON)) for n in range(LON)]
        two = [(place(top, n), place(top, (shift - 1 - n) % LON)) for n in range(LON)]

        def send(whole, low, high):
            if second_half:
                return lax.ppermute(whole, axes, one), lax.ppermute(high, axes, two)
            return lax.ppermute(whole, axes, two), lax.ppermute(low, axes, one)

        return send

    got_f = lax.switch(
        case,
        [branch(shift, half) for shift in range(LON) for half in range(2)],
        msg_b,
        low,
        high,
    )

    def spread(band, other, top):
        chunks = pl.pallas_call(
            chunk_bands,
            grid=(1,),
            in_specs=[SCALARS] + [full((5, 32, 128))] * 3,
            out_specs=full((LON * CHUNK, 128)),
            out_shape=sds(LON * CHUNK, 128),
            scratch_shapes=[VMEM((160, 128), F32)] * 4,
            compiler_params=limit(8),
            name="chunk_bands",
        )(sc, band, other, top)
        return lax.all_to_all(chunks, "lon", split_axis=0, concat_axis=0, tiled=True)

    later, _ = lax.optimization_barrier((band, got_f[1]))
    atm = lax.cond(
        lax.axis_index("blk") == BLK - 1, lambda *x: jnp.zeros((LON * CHUNK, 128), F32), spread, later, other, top
    )
    atm_top = lax.ppermute(atm, axes, [(place(RELAY, n), place(BLK - 1, n)) for n in range(LON)])

    ext = lambda n: VMEM((GUARD * 2 + n * EXT_ROWS, 128), F32)
    state, skin = pl.pallas_call(
        interval,
        grid=(1,),
        in_specs=[SCALARS] + [full(x.shape) for x in (*arrays, sides, got_a, got_b, *got_f, atm, atm_top)],
        out_specs=[full((2, LEVELS, ROWS, COLS)), full((LON, 2, 128))],
        out_shape=[sds(2, LEVELS, ROWS, COLS), sds(LON, 2, 128)],
        scratch_shapes=[ext(80), ext(80), ext(40), ext(40), ext(40), ext(5), VMEM((120, 384), F32), ext(25)]
        + [VMEM((360, 128), F32), ext(25)]
        + [ext(40)] * 5
        + [VMEM((ROWS, 128), F32)],
        compiler_params=limit(36),
        name="interval",
    )(sc, *arrays, sides, got_a, got_b, *got_f, atm, atm_top)
    bands = lax.all_to_all(skin, "lon", split_axis=0, concat_axis=0, tiled=True)
    return state, bands.reshape(1, LON * 256)


def solution(mesh):
    placed = (
        P(None, None, "blk", "lon"),
        P(None, "blk", "lon"),
        P(None, "blk", "lon"),
        P("blk", "lon"),
        P(None, ("blk", "lon"), None),
        P(None, "blk", "lon"),
        P(None, "blk", "lon"),
        P("lon"),
    )
    return jax.shard_map(
        body,
        mesh=mesh,
        in_specs=placed,
        out_specs=(P(None, None, "blk", "lon"), P(("blk", "lon"), None)),
        check_vma=False,
    )
```

```python
import jax
import jax.numpy as jnp
from jax import lax
from jax.experimental import pallas as pl
from jax.experimental.pallas import tpu as pltpu
from jax.sharding import PartitionSpec as P

STEPS = 6
F32 = jnp.float32
LEVELS = 8
BLK, LON = 8, 16
ROWS, COLS = 32, 512
EXT_ROWS, EXT_COLS = 48, 640
NX = 8192
SLABS = 41
PART = 232
HEAD = 32
WHOLE = HEAD + 4 * PART
HALF = HEAD + 2 * PART
VMEM = pltpu.VMEM
SMEM = pltpu.SMEM


def limit(mib):
    return pltpu.CompilerParams(vmem_limit_bytes=mib * 1024 * 1024)


RELAY = BLK - 2
CHUNK = 32


def iota(shape, dim):
    return lax.broadcasted_iota(jnp.int32, shape, dim)


def full(shape):
    return pl.BlockSpec(shape, lambda i: (0,) * len(shape))


def at_block(shape, place):
    return pl.BlockSpec(shape, lambda i: place)


SCALARS = pl.BlockSpec(memory_space=SMEM)


def combine_bands(fold, flux, sc, band):
    l = lax.axis_index("lon")
    mirror = lax.rem(fold[0] + COLS * l, NX)
    sc[0] = lax.axis_index("blk")
    sc[1] = l
    sc[2] = mirror // COLS
    sc[3] = lax.rem(mirror, COLS)
    sc[4] = (mirror - 1) // 2
    sc[5] = mirror // 256
    sc[6] = 0
    sc[7] = 0
    band[0] = flux[0]
    band[1] = flux[1] + flux[2] + flux[3] - 0.33 * flux[5]
    band[2] = flux[4] + flux[5] + flux[6] + flux[7]
    band[3] = flux[8]
    band[4] = flux[9]


def pack_columns(st0, st3, vn0, vn3, ve0, ve3, cd0, cd3, wt0, wt3, mk0, mk3, to_west, to_east):
    lane = iota((ROWS, 128), 1)

    def pack(groups, shift, out):
        for g, tiles in enumerate(groups):
            acc = jnp.zeros((ROWS, 128), F32)
            for j, tile in enumerate(tiles):
                moved = pltpu.roll(tile().astype(F32), (8 * j + shift) % 128, axis=1)
                acc = jnp.where((lane >= 8 * j) & (lane < 8 * j + 8), moved, acc)
            out[g] = acc

    def groups(st, vn, ve, cd, wt, mk):
        first = [lambda t=t, k=k: st[t, k] for t in range(2) for k in range(LEVELS)]
        second = [lambda k=k: vn[k] for k in range(LEVELS)] + [lambda k=k: ve[k] for k in range(LEVELS)]
        third = [lambda k=k: cd[k] for k in range(4)] + [lambda k=k: wt[k] for k in range(4)] + [lambda: mk[...]]
        return [first, second, third]

    pack(groups(st0, vn0, ve0, cd0, wt0, mk0), 0, to_west)
    pack(groups(st3, vn3, ve3, cd3, wt3, mk3), 6, to_east)


def chunk_bands(sc, band, other, top, out, own, held, relayed, turned):
    own[...] = band[...].reshape(160, 128)
    held[...] = other[...].reshape(160, 128)
    relayed[...] = top[...].reshape(160, 128)
    is_relay = sc[0] == RELAY

    @pl.when(is_relay & (sc[1] < 4))
    def _():
        pole = sc[4]
        pq, pr = pole // 128, pole % 128
        lane8 = iota((8, 128), 1)
        index = (pr - lane8) & 127
        for n in range(20):
            turned[8 * n : 8 * n + 8, :] = jnp.take_along_axis(held[8 * n : 8 * n + 8, :], index, axis=1)
        lane1 = iota((1, 128), 1)

        def one(row, carry):
            near = (pq - row) & 31
            far = (pq - row - 1) & 31
            for f in range(5):
                a = turned[pl.ds(32 * f + near, 1), :]
                b = turned[pl.ds(32 * f + far, 1), :]
                held[pl.ds(32 * f + row, 1), :] = jnp.where(lane1 <= pr, a, b)
            return carry

        lax.fori_loop(0, 32, one, 0)

    lane = iota((16, 128), 1)
    sides = jnp.zeros((16, 128), F32)
    for slot, src in enumerate((own, held, relayed)):
        for f in range(5):
            even = src[pl.ds(32 * f, 16, stride=2), :]
            odd = src[pl.ds(32 * f + 1, 16, stride=2), :]
            out[pl.ds(10 * slot + 2 * f, 16, stride=CHUNK), :] = even
            out[pl.ds(10 * slot + 2 * f + 1, 16, stride=CHUNK), :] = odd
            side = jnp.where(lane < 64, pltpu.roll(even, 15, axis=0), pltpu.roll(odd, 1, axis=0))
            at = 8 * (5 * slot + f)
            sides = jnp.where((lane >= at) & (lane < at + 8), pltpu.roll(side, at + 4, axis=1), sides)
    out[pl.ds(30, 16, stride=CHUNK), :] = sides
    out[pl.ds(31, 16, stride=CHUNK), :] = jnp.zeros((16, 128), F32)


def slot_lanes(lane8, slot):
    return (lane8 >= 16 * slot) & (lane8 < 16 * slot + 12)


def fold_lanes(sc, lane8):
    rq, rr = sc[3] // 128, sc[3] % 128
    return rq, (rr - lane8) & 127, lane8 <= rr


def pack_rows(
    sc, st_s, st_n, vn_s, vn_n, ve_s, ve_n, cd_s, cd_n, wt_s, wt_n, mk_s, mk_n,
    msg_a, msg_b, low, high, window, south, north,
):
    lane8 = iota((8, 128), 1)

    def stage(dst, st, vn, ve, cd, wt):
        for j in range(4):
            cols = slice(128 * j, 128 * j + 128)

            def put(s, value):
                dst[(j * SLABS + s) * 8 : (j * SLABS + s) * 8 + 8, :] = value

            for k in range(LEVELS):
                put(k, st[0, k, :, cols])
                put(8 + k, st[1, k, :, cols])
                put(16 + k, vn[k, :, cols])
                put(24 + k, ve[k, :, cols])
            for k in range(4):
                put(32 + k, cd[k, :, cols].astype(F32))
                put(36 + k, wt[k, :, cols])

    stage(south, st_s, vn_s, ve_s, cd_s, wt_s)
    stage(north, st_n, vn_n, ve_n, cd_n, wt_n)
    for j in range(4):
        base = (j * SLABS + 40) * 8
        cols = slice(128 * j, 128 * j + 128)
        south[base : base + 8, :] = mk_s[:, cols].astype(F32)
        flipped = mk_n[:, cols].astype(F32)
        for i in range(8):
            north[base + i : base + i + 1, :] = flipped[7 - i : 8 - i]

    def loader(edge, is_north, n):
        if n == 28:
            return lambda j: edge[pl.ds((j * SLABS + 40) * 8, 8), :]
        i, rt = n // 5, n % 5
        row = 7 - i if is_north else i
        return lambda j: edge[pl.ds((j * SLABS + rt * 8) * 8 + row, 8, stride=8), :]

    def build(put, edge, is_north):
        for n in range(29):
            load = loader(edge, is_north, n)
            for j in range(4):
                put(j, n, load(j))

    def put_a(j, n, tile):
        at = HEAD + j * PART + 8 * n
        msg_a[at : at + 8, :] = tile

    def put_b(j, n, tile):
        at = HEAD + j * PART + 8 * n
        msg_b[at : at + 8, :] = tile

    parity = sc[0] & 1
    window[...] = jnp.zeros_like(window)

    @pl.when(parity == 0)
    def _():
        build(put_a, north, True)
        build(put_b, south, False)

    @pl.when(parity == 1)
    def _():
        build(put_a, south, False)

    @pl.when((parity == 1) & (sc[0] < BLK - 1))
    def _():
        build(put_b, north, True)

    @pl.when(sc[0] == BLK - 1)
    def _():
        rq, index, near = fold_lanes(sc, lane8)
        order = [rq, (rq - 1) & 3, (rq - 2) & 3, (rq - 3) & 3]
        corner = [jnp.zeros((8, 128), F32) for _ in range(4)]
        for n in range(29):
            load = loader(north, True, n)
            g = [jnp.take_along_axis(load(j), index, axis=1) for j in order]
            for j in range(4):
                tile = jnp.where(near, g[j], g[(j + 1) % 4])
                put_b(j, n, tile)
                at = HEAD + (j % 2) * PART + 8 * n
                (low, high)[j // 2][at : at + 8, :] = tile
            below = jnp.where(rq == 0, 0.0, g[1])
            above = jnp.where(rq == 3, 0.0, g[3])
            fifth = jnp.where(lane8 < 64, jnp.where(near, g[0], below), jnp.where(near, above, g[0]))
            moved = pltpu.roll(fifth, (6 + 16 * (n % 8)) % 128, axis=1)
            corner[n // 8] = jnp.where(slot_lanes(lane8, n % 8), moved, corner[n // 8])
        for v in range(4):
            window[8 * v : 8 * v + 8, :] = corner[v]


def pack_corners(
    sc, from_west, from_east, window, a_in, b_in, low_in, high_in, sides, corner_a, corner_b, corner_low, corner_high
):
    lane = iota((ROWS, 128), 1)
    for s in range(SLABS):
        g, j = s // 16, s % 16
        east = pltpu.roll(from_east[g], (128 - 8 * j) % 128, axis=1)
        west = pltpu.roll(from_west[g], (122 - 8 * j) % 128, axis=1)
        sides[ROWS * s : ROWS * s + ROWS, :] = jnp.where(lane < 6, east, jnp.where(lane >= 122, west, 0.0))
    lane8 = iota((8, 128), 1)

    def build(dst, is_north, turn):
        corner = [window[8 * v : 8 * v + 8, :] if turn else jnp.zeros((8, 128), F32) for v in range(4)]
        if turn:
            rq, index, near = fold_lanes(sc, lane8)
            low = (lane8 < 64) & (rq == 0) & ~near
            high = (lane8 >= 64) & (rq == 3) & near
        for n in range(29):
            if n < 28:
                i, rt = n // 5, n % 5
                row = 31 - i if is_north else i
                fifth = sides[pl.ds(rt * 8 * ROWS + row, 8, stride=ROWS), :]
            else:
                mask = sides[40 * ROWS + (24 if is_north else 0) : 40 * ROWS + (32 if is_north else 8), :]
                fifth = jnp.concatenate([mask[7 - i : 8 - i] for i in range(8)], axis=0) if is_north else mask
            if turn:
                fifth = jnp.where(low | high, jnp.take_along_axis(fifth, index, axis=1), 0.0)
            moved = pltpu.roll(fifth, (6 + 16 * (n % 8)) % 128, axis=1)
            if turn:
                corner[n // 8] = corner[n // 8] + jnp.where(slot_lanes(lane8, n % 8), moved, 0.0)
            else:
                corner[n // 8] = jnp.where(slot_lanes(lane8, n % 8), moved, corner[n // 8])
        for v in range(4):
            dst[8 * v : 8 * v + 8, :] = corner[v]

    parity = sc[0] & 1

    @pl.when(parity == 0)
    def _():
        build(corner_a, True, False)
        build(corner_b, False, False)

    @pl.when(parity == 1)
    def _():
        build(corner_a, False, False)

    @pl.when((parity == 1) & (sc[0] < BLK - 1))
    def _():
        build(corner_b, True, False)

    @pl.when(sc[0] == BLK - 1)
    def _():
        build(corner_b, True, True)
        corner_low[...] = corner_b[...]
        corner_high[...] = corner_b[...]


GUARD = 8


def shifted_lanes(tiles, by, lane8):
    count = len(tiles)
    rolled = [pltpu.roll(t, (-by) % 128, axis=1) for t in tiles]
    if by > 0:
        return [jnp.where(lane8 >= 128 - by, rolled[(j + 1) % count], rolled[j]) for j in range(count)]
    return [jnp.where(lane8 < -by, rolled[(j - 1) % count], rolled[j]) for j in range(count)]


def place_ghost(load, corner, row_of, rows, old, q, v, u, taps, m, turned):
    lane8 = iota((8, 128), 1)
    edge_lanes = (lane8 < 6) | (lane8 >= 122)
    row8 = iota((8, 128), 0)
    for n in range(29):
        tiles = [load(j, n) for j in range(4)]
        fifth = pltpu.roll(corner(n // 8), (256 - 6 - 16 * (n % 8)) % 128, axis=1)
        tiles.append(jnp.where(edge_lanes, fifth, 0.0))
        if n == 28:
            for j in range(5):
                for i in range(6):
                    m[pl.ds(GUARD + j * rows + row_of(i), 1), :] = tiles[j][i : i + 1]
            continue
        i, rt = n // 5, n % 5
        for j in range(5):
            tile = tiles[j]
            if turned and rt in (2, 3):
                tile = -tile
            if turned and rt == 4:
                tile = jnp.where(row8 < 4, 8.0 - tile, tile)
            if rt < 2:
                ref, block = q, j * 16 + 8 * rt
                at = old + GUARD + block * rows + row_of(i)
            else:
                ref = (v, u, taps)[rt - 2]
                at = GUARD + j * 8 * rows + row_of(i)
            ref[pl.ds(at, 8, stride=rows), :] = tile


def own_rows(st, vn, ve, cd, wt, mk, sides, count, rows, at, side_row, q, v, u, taps, m):
    def put(ref, block, value):
        ref[pl.ds(GUARD + block * rows + at, count), :] = value

    def side(s):
        return sides[pl.ds(ROWS * s + side_row, count), :]

    for j in range(5):
        cols = slice(128 * j, 128 * j + 128)
        for t in range(2):
            for k in range(LEVELS):
                s = 8 * t + k
                put(q, j * 16 + s, st[t, k, :, cols] if j < 4 else side(s))
        for k in range(LEVELS):
            put(v, j * 8 + k, vn[k, :, cols] if j < 4 else side(16 + k))
            put(u, j * 8 + k, ve[k, :, cols] if j < 4 else side(24 + k))
        for k in range(4):
            put(taps, j * 8 + k, cd[k, :, cols].astype(F32) if j < 4 else side(32 + k))
            put(taps, j * 8 + 4 + k, wt[k, :, cols] if j < 4 else side(36 + k))
        put(m, j, mk[:, cols].astype(F32) if j < 4 else side(40))


def clear_rows(ref, blocks, rows, at, base=0):
    for b in range(blocks):
        ref[pl.ds(base + GUARD + b * rows + at, 8), :] = jnp.zeros((8, 128), F32)


def weights(is_fold, rows, first, low, count, doubled, v, u, taps, m, coef, force, ce, cw, cn, cs, cc):
    lane8 = iota((8, 128), 1)
    row8 = iota((8, 128), 0)

    def one(n):
        r = 8 * (low + n)
        ext_row = row8 + (first + r)

        def read(ref, block, shift=0):
            return ref[pl.ds(GUARD + block * rows + r + shift, 8), :]

        up_ok = jnp.where(is_fold & (ext_row >= 38) & (ext_row < 40), 0.0, 1.0)
        down_ok = jnp.where(is_fold & (ext_row >= 40) & (ext_row < 42), 0.0, 1.0)
        for j in range(5):
            w = [read(taps, 8 * j + 4 + t) for t in range(4)]
            c = [read(taps, 8 * j + t) for t in range(4)]
            wsum = w[0] + w[1] + w[2] + w[3]
            inv = 1.0 / jnp.where(wsum > 0.0, wsum, 1.0)
            w = [x * inv for x in w]
            for code in range(9):
                hit = [jnp.where(c[t] == float(code), w[t], 0.0) for t in range(4)]
                total = (hit[0] + hit[1]) + (hit[2] + hit[3])
                if code < 3 and n == 5:
                    total = total * down_ok
                if code >= 6 and n == 4:
                    total = total * up_ok
                coef[8 * (5 * code + j) : 8 * (5 * code + j) + 8, :] = total
        fields = []
        for f in range(5):
            total = None
            for dy in (-1, 0, 1):
                at = [GUARD + (5 * f + j) * 48 + first + r + 2 * dy for j in range(5)]
                grid = [doubled[pl.ds(a, 8), :] for a in at]
                for dx in (-1, 0, 1):
                    code = 3 * (dy + 1) + dx + 1
                    moved = grid if dx == 0 else shifted_lanes(grid, 2 * dx, lane8)
                    part = [
                        moved[j] * coef[8 * (5 * code + j) : 8 * (5 * code + j) + 8, :] for j in range(5)
                    ]
                    total = part if total is None else [a + b for a, b in zip(total, part)]
            fields.append(total)
        mc = [read(m, j) for j in range(5)]
        me, mw = shifted_lanes(mc, 1, lane8), shifted_lanes(mc, -1, lane8)
        oe = [mc[j] * me[j] for j in range(5)]
        ow = [mc[j] * mw[j] for j in range(5)]
        on = [mc[j] * read(m, j, 1) for j in range(5)]
        os = [mc[j] * read(m, j, -1) for j in range(5)]

        def put(ref, block, value):
            ref[pl.ds(GUARD + block * rows + r, 8), :] = value

        top, mid = [], []
        for j in range(5):
            sw, heat, fresh, tx, ty = (fields[f][j] for f in range(5))
            kv = 0.05 + 0.04 * jnp.sqrt(tx * tx + ty * ty + 0.01)
            top.append(mc[j] * kv)
            mid.append(0.05 * mc[j])
            put(force, j, 0.05 * mc[j] * sw)
            put(force, 5 + j, 0.05 * mc[j] * heat)
            put(force, 10 + j, -0.05 * mc[j] * fresh)
            put(force, 15 + j, top[j])
            put(force, 20 + j, mid[j])
        over = is_fold & (ext_row >= 40)
        for k in range(LEVELS):
            uc = [read(u, 8 * j + k) for j in range(5)]
            west = shifted_lanes(uc, -1, lane8)
            east = shifted_lanes(uc, 1, lane8) if n == 5 else None
            for j in range(5):
                vc = read(v, 8 * j + k)
                et, wt, vt, vb = uc[j], west[j], vc, read(v, 8 * j + k, -1)
                if n == 5:
                    et, wt = jnp.where(over, east[j], et), jnp.where(over, uc[j], wt)
                    vt, vb = jnp.where(over, read(v, 8 * j + k, 1), vt), jnp.where(over, vc, vb)
                put(ce, 8 * j + k, oe[j] * (0.08 - jnp.minimum(et, 0.0)))
                put(cw, 8 * j + k, ow[j] * (0.08 + jnp.maximum(wt, 0.0)))
                put(cn, 8 * j + k, on[j] * (0.08 - jnp.minimum(vt, 0.0)))
                put(cs, 8 * j + k, os[j] * (0.08 + jnp.maximum(vb, 0.0)))
                centre = 1.0 - oe[j] * (0.08 + jnp.maximum(et, 0.0)) - ow[j] * (0.08 - jnp.minimum(wt, 0.0))
                centre = centre - on[j] * (0.08 + jnp.maximum(vt, 0.0)) - os[j] * (0.08 - jnp.minimum(vb, 0.0))
                if k == 0:
                    centre = centre - top[j]
                elif k == 1:
                    centre = centre - top[j] - mid[j]
                elif k == LEVELS - 1:
                    centre = centre - mid[j]
                else:
                    centre = centre - 2.0 * mid[j]
                put(cc, 8 * j + k, centre)

    for n in range(count):
        one(n)


def steps(rows, qa, qb, force, ce, cw, cn, cs, cc):
    lane8 = iota((8, 128), 1)

    def one(q, p, r, width):
        def read(ref, block, shift=0):
            at = GUARD + block * rows + r + shift
            return ref[at : at + 8, :]

        def state(t, k, j, shift=0):
            return read(q, 16 * j + 8 * t + k, shift)

        mid = [read(force, 20 + j) for j in range(width)]
        here = [[state(t, 0, j) for j in range(5)] for t in range(2)]
        below = [None, None]
        for k in range(LEVELS):
            weight = [[read(ref, 8 * j + k) for j in range(width)] for ref in (cc, ce, cw, cn, cs)]
            for t in range(2):
                above = here[t]
                after = [state(t, k + 1, j) for j in range(5)] if k < LEVELS - 1 else None
                east, west = shifted_lanes(above, 1, lane8), shifted_lanes(above, -1, lane8)
                for j in range(width):
                    total = weight[0][j] * above[j] + weight[1][j] * east[j]
                    total = total + weight[2][j] * west[j]
                    total = total + weight[3][j] * state(t, k, j, 1)
                    total = total + weight[4][j] * state(t, k, j, -1)
                    if k == 0:
                        total = total + read(force, 15 + j) * after[j]
                    elif k == 1:
                        total = total + read(force, 15 + j) * below[t][j] + mid[j] * after[j]
                    elif k == LEVELS - 1:
                        total = total + mid[j] * below[t][j]
                    else:
                        total = total + mid[j] * (below[t][j] + after[j])
                    if t == 0:
                        total = total + (0.5 ** (k + 1)) * read(force, j)
                        if k == 0:
                            total = total + read(force, 5 + j)
                    elif k == 0:
                        total = total + read(force, 10 + j)
                    at = GUARD + (16 * j + 8 * t + k) * rows + r
                    p[at : at + 8, :] = total
                below[t], here[t] = above, after

    def step(q, p, last=False):
        for n in range(1, 5) if last else range(6):
            one(q, p, 8 * n, 4 if last else 5)

    def two(i, carry):
        step(qa, qb)
        step(qb, qa)
        return carry

    lax.fori_loop(0, STEPS // 2 - 1, two, 0)
    step(qa, qb)
    step(qb, qa, True)


def skin_rows(q, m, rows, at, count, pairs):
    sums = []
    table = (iota((COLS, COLS // 2), 0) // 2 == iota((COLS, COLS // 2), 1)).astype(F32)
    for with_heat in (True, False):
        parts = []
        for j in range(4):
            value = m[GUARD + j * rows + at : GUARD + j * rows + at + count, :]
            if with_heat:
                value = value * q[GUARD + 16 * j * rows + at : GUARD + 16 * j * rows + at + count, :]
            pairs[0:count, :] = value
            parts.append(
                pairs[pl.ds(0, count // 2, stride=2), :] + pairs[pl.ds(1, count // 2, stride=2), :]
            )
        narrow = jnp.concatenate(parts, axis=1)
        sums.append(jnp.dot(narrow, table, precision=lax.Precision.HIGHEST, preferred_element_type=F32))
    return sums[0] / jnp.maximum(sums[1], 1.0)


def clear_guards(refs):
    for ref in refs:
        ref[0:GUARD, :] = jnp.zeros((GUARD, 128), F32)
        ref[ref.shape[0] - GUARD :, :] = jnp.zeros((GUARD, 128), F32)


def interval(
    sc, st, vn, ve, cd, wt, mk, sides, got_a, got_b, major, minor, atm, atm_top, out, sst,
    qa, qb, v, u, taps, m, atm_rows, grids, coef, force, ce, cw, cn, cs, cc, pairs,
):
    rows = EXT_ROWS
    lane8 = iota((8, 128), 1)
    is_fold = sc[0] == BLK - 1
    odd = sc[0] & 1
    clear_guards((qa, qb, v, u, taps, m, grids))
    for at in (0, 40):
        clear_rows(qa, 80, rows, at)
        clear_rows(v, 40, rows, at)
        clear_rows(u, 40, rows, at)
        clear_rows(taps, 40, rows, at)
        clear_rows(m, 5, rows, at)
    own_rows(st, vn, ve, cd, wt, mk, sides, ROWS, rows, 8, 0, qa, v, u, taps, m)

    def to_north(i):
        return 40 + i

    def to_south(i):
        return 7 - i

    def plain(msg, row_of):
        place_ghost(
            lambda j, n: msg[HEAD + j * PART + 8 * n : HEAD + j * PART + 8 * n + 8, :],
            lambda g: msg[8 * g : 8 * g + 8, :],
            row_of, rows, 0, qa, v, u, taps, m, False,
        )

    @pl.when(odd == 0)
    def _():
        plain(got_a, to_north)
        plain(got_b, to_south)

    @pl.when(odd == 1)
    def _():
        plain(got_a, to_south)

    @pl.when((odd == 1) & jnp.logical_not(is_fold))
    def _():
        plain(got_b, to_north)

    def fold(first_is_major):
        seam = sc[3]

        def load(j, n):
            at = HEAD + j * PART + 8 * n
            value = major[at : at + 8, :]
            if first_is_major == (j >= 2):
                at = HEAD + (j % 2) * PART + 8 * n
                second = lane8 + 128 * j > seam
                value = jnp.where(second if first_is_major else ~second, minor[at : at + 8, :], value)
            return value

        def corner(g):
            at = slice(8 * g, 8 * g + 8)
            one, two = (major, minor) if first_is_major else (minor, major)
            return jnp.where((lane8 & 15) < 6, one[at, :], two[at, :])

        place_ghost(load, corner, to_north, rows, 0, qa, v, u, taps, m, True)

    @pl.when(is_fold & (sc[3] >= 256))
    def _():
        fold(True)

    @pl.when(is_fold & (sc[3] < 256))
    def _():
        fold(False)

    lane16 = iota((16, 128), 1)

    def piece(ref, slot, f, part):
        if part < 2:
            return ref[pl.ds(10 * slot + 2 * f + part, 16, stride=CHUNK), :]
        side = pltpu.roll(ref[pl.ds(30, 16, stride=CHUNK), :], 128 - 4 - 8 * (5 * slot + f), axis=1)
        return jnp.where((lane16 < 4) | (lane16 >= 124), side, 0.0)

    def each(put):
        for f in range(5):
            for part in range(3):
                put(24 * f, slice(128 * part, 128 * part + 128), f, part)

    @pl.when(jnp.logical_not(is_fold))
    def _():
        def put(at, cols, f, part):
            far = piece(atm, 1, f, part)
            atm_rows[at : at + 4, cols] = far[12:16]
            atm_rows[at + 4 : at + 20, cols] = piece(atm, 0, f, part)
            atm_rows[at + 20 : at + 24, cols] = far[0:4]

        each(put)

    @pl.when(sc[0] == RELAY)
    def _():
        def put(at, cols, f, part):
            atm_rows[at + 20 : at + 24, cols] = piece(atm, 2, f, part)[0:4]

        each(put)

    @pl.when(is_fold)
    def _():
        def put(at, cols, f, part):
            atm_rows[at : at + 4, cols] = piece(atm_top, 0, f, part)[12:16]
            atm_rows[at + 4 : at + 20, cols] = piece(atm_top, 2, f, part)
            atm_rows[at + 20 : at + 24, cols] = piece(atm_top, 1, f, part)[0:4]

        each(put)

    src = iota((384, EXT_COLS), 0)
    dst = iota((384, EXT_COLS), 1)
    table = (src == jnp.where(dst < 576, dst // 2, dst // 2 + 64)).astype(F32)
    wide = jnp.dot(atm_rows[...], table, precision=lax.Precision.HIGHEST, preferred_element_type=F32)
    for f in range(5):
        for j in range(5):
            tile = wide[24 * f : 24 * f + 24, 128 * j : 128 * j + 128]
            base = GUARD + (5 * f + j) * 48
            grids[pl.ds(base, 24, stride=2), :] = tile
            grids[pl.ds(base + 1, 24, stride=2), :] = tile
    weights(is_fold, rows, 0, 0, 6, grids, v, u, taps, m, coef, force, ce, cw, cn, cs, cc)
    steps(rows, qa, qb, force, ce, cw, cn, cs, cc)
    for t in range(2):
        for k in range(LEVELS):
            for j in range(4):
                base = GUARD + (16 * j + 8 * t + k) * rows + 8
                out[t, k, :, 128 * j : 128 * j + 128] = qa[base : base + ROWS, :]
    result = skin_rows(qa, m, rows, 8, ROWS, pairs)
    sst[:, 0, :] = result[:, 0:128]
    sst[:, 1, :] = result[:, 128:256]


def place(b, l):
    return b * LON + l % LON


def body(temp_salt, east_vel, north_vel, land_mask, fluxes, remap_code, remap_weight, fold_source):
    axes = ("blk", "lon")
    arrays = (temp_salt, north_vel, east_vel, remap_code, remap_weight, land_mask)

    sds = lambda *shape: jax.ShapeDtypeStruct(shape, F32)
    sc, band = pl.pallas_call(
        combine_bands,
        grid=(1,),
        in_specs=[SCALARS, full((10, 32, 128))],
        out_specs=[SCALARS, full((5, 32, 128))],
        out_shape=[jax.ShapeDtypeStruct((8,), jnp.int32), sds(5, 32, 128)],
        compiler_params=limit(56),
        name="combine_bands",
    )(fold_source, fluxes.reshape(10, 32, 128))
    band_pairs = []
    for n in range(4):
        for blk in range(RELAY):
            band_pairs.append((place(blk + 1, n), place(blk, n)))
            band_pairs.append((place(blk, 12 + n), place(blk + 1, 12 + n)))
        band_pairs.append((place(BLK - 1, 15 - n), place(RELAY, n)))
    first, _ = lax.optimization_barrier((land_mask, band))
    specs, operands = [], []
    for x in (*arrays[:-1], first):
        lead = x.shape[:-2]
        for j in (0, 3):
            specs.append(at_block(lead + (ROWS, 128), (0,) * len(lead) + (0, j)))
            operands.append(x)
    to_west, to_east = pl.pallas_call(
        pack_columns,
        grid=(1,),
        in_specs=specs,
        out_specs=[full((3, ROWS, 128))] * 2,
        out_shape=[sds(3, ROWS, 128)] * 2,
        compiler_params=limit(56),
        name="pack_columns",
    )(*operands)
    from_west = lax.ppermute(to_east, "lon", [(i, (i + 1) % LON) for i in range(LON)])
    from_east = lax.ppermute(to_west, "lon", [((i + 1) % LON, i) for i in range(LON)])
    moving, from_west = lax.optimization_barrier((band, from_west))
    other = lax.ppermute(moving, axes, band_pairs)
    top = lax.ppermute(moving, axes, [(place(BLK - 1, n), place(RELAY, n)) for n in range(LON)])

    first, _, case = lax.optimization_barrier((land_mask, to_west, sc[5]))
    specs, operands = [SCALARS], [sc]
    for x in (*arrays[:-1], first):
        lead = x.shape[:-2]
        for j in (0, 3):
            specs.append(at_block(lead + (8, COLS), (0,) * len(lead) + (j, 0)))
            operands.append(x)
    sizes = (WHOLE, WHOLE, HALF, HALF)
    *messages, window = pl.pallas_call(
        pack_rows,
        grid=(1,),
        in_specs=specs,
        out_specs=[full((n, 128)) for n in sizes] + [full((HEAD, 128))],
        out_shape=[sds(n, 128) for n in sizes] + [sds(HEAD, 128)],
        scratch_shapes=[VMEM((4 * SLABS * 8, 128), F32)] * 2,
        compiler_params=limit(56),
        name="pack_rows",
    )(*operands)
    window, other, top = lax.optimization_barrier((window, other, top))
    sides, msg_a, msg_b, low, high = pl.pallas_call(
        pack_corners,
        grid=(1,),
        in_specs=[SCALARS, full((3, ROWS, 128)), full((3, ROWS, 128)), full((HEAD, 128))]
        + [pl.BlockSpec(memory_space=pl.ANY)] * 4,
        out_specs=[full((SLABS * ROWS, 128))] + [full((HEAD, 128))] * 4,
        out_shape=[sds(SLABS * ROWS, 128)] + [sds(n, 128) for n in sizes],
        input_output_aliases={4: 1, 5: 2, 6: 3, 7: 4},
        compiler_params=limit(56),
        name="pack_corners",
    )(sc, from_west, from_east, window, *messages)

    on_chip = [(place(i, n), place(i ^ 1, n)) for i in range(BLK) for n in range(LON)]
    across = []
    for i in range(1, BLK - 1, 2):
        for n in range(LON):
            across += [(place(i, n), place(i + 1, n)), (place(i + 1, n), place(i, n))]
    got_a = lax.ppermute(msg_a, axes, on_chip)
    got_b = lax.ppermute(msg_b, axes, across)

    def branch(shift, second_half):
        top = BLK - 1
        one = [(place(top, n), place(top, (shift - n) % LON)) for n in range(LON)]
        two = [(place(top, n), place(top, (shift - 1 - n) % LON)) for n in range(LON)]

        def send(whole, low, high):
            if second_half:
                return lax.ppermute(whole, axes, one), lax.ppermute(high, axes, two)
            return lax.ppermute(whole, axes, two), lax.ppermute(low, axes, one)

        return send

    got_f = lax.switch(
        case,
        [branch(shift, half) for shift in range(LON) for half in range(2)],
        msg_b,
        low,
        high,
    )

    def spread(band, other, top):
        chunks = pl.pallas_call(
            chunk_bands,
            grid=(1,),
            in_specs=[SCALARS] + [full((5, 32, 128))] * 3,
            out_specs=full((LON * CHUNK, 128)),
            out_shape=sds(LON * CHUNK, 128),
            scratch_shapes=[VMEM((160, 128), F32)] * 4,
            compiler_params=limit(8),
            name="chunk_bands",
        )(sc, band, other, top)
        return lax.all_to_all(chunks, "lon", split_axis=0, concat_axis=0, tiled=True)

    later, _ = lax.optimization_barrier((band, got_f[1]))
    atm = lax.cond(
        lax.axis_index("blk") == BLK - 1, lambda *x: jnp.zeros((LON * CHUNK, 128), F32), spread, later, other, top
    )
    atm_top = lax.ppermute(atm, axes, [(place(RELAY, n), place(BLK - 1, n)) for n in range(LON)])

    ext = lambda n: VMEM((GUARD * 2 + n * EXT_ROWS, 128), F32)
    state, skin = pl.pallas_call(
        interval,
        grid=(1,),
        in_specs=[SCALARS] + [full(x.shape) for x in (*arrays, sides, got_a, got_b, *got_f, atm, atm_top)],
        out_specs=[full((2, LEVELS, ROWS, COLS)), full((LON, 2, 128))],
        out_shape=[sds(2, LEVELS, ROWS, COLS), sds(LON, 2, 128)],
        scratch_shapes=[ext(80), ext(80), ext(40), ext(40), ext(40), ext(5), VMEM((120, 384), F32), ext(25)]
        + [VMEM((360, 128), F32), ext(25)]
        + [ext(40)] * 5
        + [VMEM((ROWS, 128), F32)],
        compiler_params=limit(36),
        name="interval",
    )(sc, *arrays, sides, got_a, got_b, *got_f, atm, atm_top)
    bands = lax.all_to_all(skin, "lon", split_axis=0, concat_axis=0, tiled=True)
    return state, bands.reshape(1, LON * 256)


def solution(mesh):
    placed = (
        P(None, None, "blk", "lon"),
        P(None, "blk", "lon"),
        P(None, "blk", "lon"),
        P("blk", "lon"),
        P(None, ("blk", "lon"), None),
        P(None, "blk", "lon"),
        P(None, "blk", "lon"),
        P("lon"),
    )
    return jax.shard_map(
        body,
        mesh=mesh,
        in_specs=placed,
        out_specs=(P(None, None, "blk", "lon"), P(("blk", "lon"), None)),
        check_vma=False,
    )
```
